32 devices in a mesh: dp: 8 (over y, x, core), mp: 4 (over z).
Axes of the slice: x: 2, y: 2, z: 4, core: 2. Of those that a mesh axis runs over, the one named last changes fastest.
Arguments:
- queries: bfloat16 [16, 128, 8192], P('dp', None, 'mp'), may hold values from -6 to 6
- out_grad: bfloat16 [16, 128, 8192], P('dp', None, 'mp'), may hold values from -12 to 12
- images: bfloat16 [16, 128, 7680], P('dp', 'mp'), may hold values from -6 to 6
- key_weight: bfloat16 [7680, 1024], P('dp', 'mp'), may hold values from -0.0625 to 0.0625
- value_weight: bfloat16 [7680, 1024], P('dp', 'mp'), may hold values from -0.0625 to 0.0625
- query_gain: float32 [128], replicated, may hold values from 0.1 to 1.9
- key_gain: float32 [128], replicated, may hold values from 0.1 to 1.9
- assignment: int32 [16], P('dp'), may hold values from 0 to 1
- tile_counts: int32 [16], P('dp'), may hold values from 1 to 4
- lengths: int32 [16], P('dp'), may hold values from 1 to 128
Outputs:
- query_grad: bfloat16 [16, 128, 8192], P('dp', None, 'mp')
- image_grad: bfloat16 [16, 128, 7680], P('dp', 'mp')
- key_weight_grad: float32 [7680, 1024], P('dp', 'mp')
- value_weight_grad: float32 [7680, 1024], P('dp', 'mp')
The draws below stay inside these ranges and needn't reach their ends.
Inputs may be any that keep to these rules, and one draw needn't show every extreme that they name: assignment[s] picks one of the 2 images of the same block: sequence s attends to image (s // 2) * 2 + assignment[s]. Image i has tile_counts[i] * 32 rows in use, the first ones; the others are padding. Sequence s has its first lengths[s] tokens in use.
All inputs are finite; a program needn't handle non-finite values.
Results may differ from the reference program's by a relative error of at most 0.012.
Values may be sent and summed in bfloat16 or wider, within the bound.
No kernel may reach another device: no remote copies, remote signals or barrier semaphores. Data moves between devices by JAX's collectives and lax.ppermute only.
A program may use at most 128 MiB of HBM per device.

```python
import math
import jax
import jax.numpy as jnp
from jax import lax

DV = 7680
H = 64
KVH = 8
HD = 128
TXT = 128
SEQ_DEV = 2
IMG_DEV = 2
TILE_ROWS = 32
TILES = 4
GROUP = 8
IMG_ROWS = 128
SEQS = 16
IMAGES = 16
N_DP = 8
N_MP = 4


def with_ends(array, own_key, low, high):
    place = [jax.random.randint(jax.random.fold_in(own_key, axis), (), 0, length) for axis, length in enumerate(array.shape)]
    main_axis = array.shape.index(max(array.shape))
    neighbour = place[:main_axis] + [(place[main_axis] + 1) % array.shape[main_axis]] + place[main_axis + 1:]
    return array.at[tuple(place)].set(low).at[tuple(neighbour)].set(high)


def spiked(values, rng, source, target, blocks, factor):
    owner, partner = [(jnp.arange(values.shape[position]) // (values.shape[position] // blocks)).reshape([-1 if axis == position else 1 for axis in range(values.ndim)]) for position in (source, target)]
    chosen = jax.random.permutation(rng, blocks)[partner]
    strong = (owner == chosen) | (owner == (partner + blocks // 2) % blocks)
    return jnp.where(strong, factor * values, values)


def level_of(rng, extent, pieces, smallest, largest):
    gain = 1.0
    for dim, parts in pieces:
        steps = jax.random.uniform(jax.random.fold_in(jax.random.fold_in(rng, 6), dim), (parts,), jnp.float32, smallest / len(pieces), largest / len(pieces))
        gain = gain * jnp.repeat(jnp.exp(steps), extent[dim] // parts).reshape((-1,) + (1,) * (len(extent) - 1 - dim))
    return gain


def normal_values(rng, shape, width, most, cuts=(), kind=jnp.bfloat16):
    result = jax.random.normal(rng, shape, jnp.float32) * width
    if len(cuts) > 0:
        result = level_of(rng, shape, cuts, -0.22, 0.18) * result
    return jnp.clip(result, min=-most, max=most).astype(kind)


def noise_with(own_key, shape, deviation, most, cuts, heavy, kind=jnp.bfloat16):
    entries = deviation * jax.random.normal(own_key, shape, jnp.float32)
    if cuts:
        entries = entries * level_of(own_key, shape, cuts, -0.22, 0.18)
    return jnp.clip(spiked(entries, jax.random.fold_in(own_key, 3), *heavy), -most, most).astype(kind)


def setup_inputs(seed: int = 0) -> dict:
    seeds = jax.random.split(jax.random.key(seed), 11)
    queries = normal_values(seeds[0], (SEQS, TXT, H * HD), 1.0, 6.0, ((0, 8), (2, 4)))
    out_grad = normal_values(seeds[1], (SEQS, TXT, H * HD), 2.0, 12.0, ((0, 8), (2, 4)))
    images = noise_with(seeds[2], (IMAGES, IMG_ROWS, DV), 1.0, 6.0, ((0, 8), (1, 4)), (0, 2, 8, 2.0))
    key_weight = normal_values(seeds[3], (DV, KVH * HD), DV ** -0.5, 0.0625, ((0, 8), (1, 4)))
    value_weight = normal_values(seeds[4], (DV, KVH * HD), DV ** -0.5, 0.0625, ((0, 8), (1, 4)))
    query_gain = jnp.clip(1.0 + 0.18 * jax.random.normal(seeds[5], (HD,), jnp.float32), 0.1, 1.9)
    key_gain = jnp.clip(1.0 + 0.18 * jax.random.normal(seeds[6], (HD,), jnp.float32), 0.1, 1.9)
    assignment = with_ends(jax.random.randint(seeds[7], (SEQS,), 0, IMG_DEV), jax.random.fold_in(seeds[7], 1), 0, IMG_DEV - 1).astype(jnp.int32)
    tile_counts = with_ends(jax.random.randint(seeds[8], (IMAGES,), 1, TILES + 1), jax.random.fold_in(seeds[8], 1), 1, TILES).astype(jnp.int32)
    lengths = with_ends(jax.random.randint(seeds[9], (SEQS,), 1, TXT + 1), jax.random.fold_in(seeds[9], 1), 1, TXT).astype(jnp.int32)
    return {"queries": queries, "out_grad": out_grad, "images": images, "key_weight": key_weight, "value_weight": value_weight, "query_gain": query_gain, "key_gain": key_gain, "assignment": assignment, "tile_counts": tile_counts, "lengths": lengths}


EPSILON = 1e-05

def rms_scale(source):
    return lax.rsqrt(lax.optimization_barrier(jnp.mean(source * source, axis=-1, keepdims=True)) + EPSILON)

def rms_back(source, factor, gain_vector, upstream):
    weighted = gain_vector * upstream
    return factor * weighted - source * (factor * factor * factor) * lax.optimization_barrier(jnp.mean(source * weighted, axis=-1, keepdims=True))

def attend(query_normed, masked_grad, key_normed, value_heads, key_live):
    inv_root = 1.0 / math.sqrt(query_normed.shape[-1])
    query_wide = query_normed.astype(jnp.float32)
    grad_wide = masked_grad.astype(jnp.float32)
    key_wide = key_normed.astype(jnp.float32)
    value_wide = value_heads.astype(jnp.float32)
    scores = jnp.einsum('btgjd,brgd->bgjtr', query_wide, key_wide) * inv_root
    raised = jnp.exp(scores) * key_live[:, None, None, None, :]
    prob_full = raised / lax.optimization_barrier(jnp.sum(raised, axis=-1, keepdims=True))
    prob_half = prob_full.astype(jnp.bfloat16)
    value_part = jnp.einsum('bgjtr,btgjd->brgd', prob_half.astype(jnp.float32), grad_wide)
    prob_grad = jnp.einsum('btgjd,brgd->bgjtr', grad_wide, value_wide)
    score_grad = (prob_full * (prob_grad - lax.optimization_barrier(jnp.sum(prob_full * prob_grad, axis=-1, keepdims=True)))).astype(jnp.bfloat16)
    score_wide = score_grad.astype(jnp.float32)
    query_part = jnp.einsum('bgjtr,brgd->btgjd', score_wide, key_wide) * inv_root
    key_part = jnp.einsum('bgjtr,btgjd->brgd', score_wide, query_wide) * inv_root
    return (query_part, key_part, value_part)

def reference(queries, out_grad, images, key_weight, value_weight, query_gain, key_gain, assignment, tile_counts, lengths):
    image_flat = images.reshape(IMAGES * IMG_ROWS, DV)
    key_pre = jnp.dot(image_flat, key_weight, preferred_element_type=jnp.float32).reshape(IMAGES, IMG_ROWS, KVH, HD)
    value_heads = jnp.dot(image_flat, value_weight, preferred_element_type=jnp.float32).astype(jnp.bfloat16)
    value_heads = value_heads.reshape(IMAGES, IMG_ROWS, KVH, HD)
    key_scale = rms_scale(key_pre)
    key_normed = (key_pre * key_scale * key_gain).astype(jnp.bfloat16)
    owner_index = jnp.arange(SEQS, dtype=jnp.int32) // SEQ_DEV * IMG_DEV + assignment.astype(jnp.int32)
    key_live = (jnp.arange(IMG_ROWS, dtype=jnp.int32)[None, :] < (tile_counts[owner_index] * TILE_ROWS)[:, None]).astype(jnp.float32)
    row_live = (jnp.arange(TXT, dtype=jnp.int32)[None, :] < lengths[:, None]).astype(jnp.bfloat16)
    query_float = queries.astype(jnp.float32).reshape(SEQS, TXT, KVH, GROUP, HD)
    query_scale = rms_scale(query_float)
    query_normed = (query_float * query_scale * query_gain).astype(jnp.bfloat16)
    masked_grad = (out_grad * row_live[:, :, None]).reshape(SEQS, TXT, KVH, GROUP, HD)

    def block_step(block_args):
        query_block, grad_block, owner_block, live_block = block_args
        return attend(query_block, grad_block, key_normed[owner_block], value_heads[owner_block], live_block)
    query_part, key_part, value_part = lax.map(block_step, (query_normed.reshape(N_DP, SEQ_DEV, TXT, KVH, GROUP, HD), masked_grad.reshape(N_DP, SEQ_DEV, TXT, KVH, GROUP, HD), owner_index.reshape(N_DP, SEQ_DEV), key_live.reshape(N_DP, SEQ_DEV, IMG_ROWS)))
    query_part = query_part.reshape(SEQS, TXT, KVH, GROUP, HD)
    key_part = key_part.reshape(SEQS, IMG_ROWS, KVH, HD)
    value_part = value_part.reshape(SEQS, IMG_ROWS, KVH, HD)
    image_key = jax.ops.segment_sum(key_part, owner_index, num_segments=IMAGES)
    image_value = jax.ops.segment_sum(value_part, owner_index, num_segments=IMAGES)
    value_rows = image_value.astype(jnp.bfloat16).reshape(IMAGES * IMG_ROWS, KVH * HD)
    key_rows = rms_back(key_pre, key_scale, key_gain, image_key).astype(jnp.bfloat16).reshape(IMAGES * IMG_ROWS, KVH * HD)
    query_grad = rms_back(query_float, query_scale, query_gain, query_part).astype(jnp.bfloat16).reshape(SEQS, TXT, H * HD)
    row_dims = (((0,), (0,)), ((), ()))
    key_weight_grad = lax.dot_general(image_flat, key_rows, row_dims, preferred_element_type=jnp.float32)
    value_weight_grad = lax.dot_general(image_flat, value_rows, row_dims, preferred_element_type=jnp.float32)
    col_dims = (((1,), (1,)), ((), ()))
    col_span = KVH * HD // N_MP
    total_sum = jnp.zeros((IMAGES * IMG_ROWS, DV), jnp.float32)
    for group_index in range(N_MP):
        low = group_index * col_span
        group_term = lax.dot_general(key_rows[:, low:low + col_span], key_weight[:, low:low + col_span], col_dims, preferred_element_type=jnp.float32)
        group_term = group_term + lax.dot_general(value_rows[:, low:low + col_span], value_weight[:, low:low + col_span], col_dims, preferred_element_type=jnp.float32)
        total_sum = total_sum + lax.optimization_barrier(group_term.astype(jnp.bfloat16)).astype(jnp.float32)
    image_grad = total_sum.astype(jnp.bfloat16).reshape(IMAGES, IMG_ROWS, DV)
    return (query_grad, image_grad, key_weight_grad, value_weight_grad)
```

```python
import math

import jax
import jax.numpy as jnp
from jax import lax
from jax.sharding import PartitionSpec as P

TILE_ROWS = 32


EPSILON = 1e-05


def rms_scale(source):
    return lax.rsqrt(jnp.mean(source * source, axis=-1, keepdims=True) + EPSILON)


def rms_back(source, factor, gain_vector, upstream):
    weighted = gain_vector * upstream
    return factor * weighted - source * (factor * factor * factor) * jnp.mean(
        source * weighted, axis=-1, keepdims=True
    )


def attend(query_normed, masked_grad, key_normed, value_heads, key_live):
    inv_root = 1.0 / math.sqrt(query_normed.shape[-1])
    scores = (
        jnp.einsum(
            "btgjd,brgd->bgjtr", query_normed, key_normed, preferred_element_type=jnp.float32
        )
        * inv_root
    )
    raised = jnp.exp(scores) * key_live[:, None, None, None, :]
    prob_full = raised / jnp.sum(raised, axis=-1, keepdims=True)
    prob_half = prob_full.astype(jnp.bfloat16)
    value_part = jnp.einsum(
        "bgjtr,btgjd->brgd", prob_half, masked_grad, preferred_element_type=jnp.float32
    )
    prob_grad = jnp.einsum(
        "btgjd,brgd->bgjtr", masked_grad, value_heads, preferred_element_type=jnp.float32
    )
    score_grad = (
        prob_full * (prob_grad - jnp.sum(prob_full * prob_grad, axis=-1, keepdims=True))
    ).astype(jnp.bfloat16)
    query_part = (
        jnp.einsum("bgjtr,brgd->btgjd", score_grad, key_normed, preferred_element_type=jnp.float32)
        * inv_root
    )
    key_part = (
        jnp.einsum(
            "bgjtr,btgjd->brgd", score_grad, query_normed, preferred_element_type=jnp.float32
        )
        * inv_root
    )
    return (query_part, key_part, value_part)


def per_device(
    dp_size,
    queries,
    out_grad,
    images,
    key_weight,
    value_weight,
    query_gain,
    key_gain,
    assignment,
    tile_counts,
    lengths,
):
    seq_count, text_len, query_cols = queries.shape
    img_count, own_rows, vis_width = images.shape
    head_dim = query_gain.shape[0]
    own_width, key_cols = key_weight.shape
    key_heads = key_cols // head_dim
    group_size = query_cols // head_dim // key_heads
    pairs = dp_size // 2
    width = 2 * own_width
    place = lax.axis_index("dp")
    pair, core = place // 2, place % 2

    def swap(value, mask):
        return lax.ppermute(value, "dp", [(i, i ^ mask) for i in range(dp_size)])

    own_weight = jnp.concatenate((key_weight, value_weight), axis=1)
    mate_weight = swap(own_weight, 1)
    weight = jnp.where(
        core == 0,
        jnp.concatenate((own_weight, mate_weight), axis=0),
        jnp.concatenate((mate_weight, own_weight), axis=0),
    )

    chunks = []
    for r in range(pairs):
        piece = lax.dynamic_slice_in_dim(images, (pair ^ r) * width, width, axis=2)
        chunks.append(swap(piece, 2 * r) if r else piece)
    mine = jnp.stack(chunks)
    features = lax.all_gather(mine, "mp", axis=0)
    mp_size = features.shape[0]
    img_rows = mp_size * own_rows
    flat = features.reshape(-1, width)
    partial = jnp.dot(flat, weight, preferred_element_type=jnp.float32).astype(jnp.bfloat16)
    partial = partial.reshape(mp_size, pairs, img_count, own_rows, 2 * key_cols)
    total = 0.0
    for r in range(pairs):
        piece = partial[:, r]
        total = total + (swap(piece, 2 * r) if r else piece).astype(jnp.float32)
    total = total.transpose(1, 0, 2, 3).reshape(img_count, img_rows, 2 * key_cols)
    key_pre = total[..., :key_cols].reshape(img_count, img_rows, key_heads, head_dim)
    value_heads = (
        total[..., key_cols:]
        .astype(jnp.bfloat16)
        .reshape(img_count, img_rows, key_heads, head_dim)
    )
    key_scale = rms_scale(key_pre)
    key_normed = (key_pre * key_scale * key_gain).astype(jnp.bfloat16)
    picker = assignment[:, None] == jnp.arange(img_count, dtype=jnp.int32)[None, :]
    pick_half = picker.astype(jnp.bfloat16)
    seq_keys = jnp.einsum(
        "bi,irgd->brgd", pick_half, key_normed, preferred_element_type=jnp.float32
    ).astype(jnp.bfloat16)
    seq_values = jnp.einsum(
        "bi,irgd->brgd", pick_half, value_heads, preferred_element_type=jnp.float32
    ).astype(jnp.bfloat16)
    seq_tiles = jnp.sum(picker.astype(jnp.int32) * tile_counts[None, :], axis=1)
    key_live = (
        jnp.arange(img_rows, dtype=jnp.int32)[None, :] < (seq_tiles * TILE_ROWS)[:, None]
    ).astype(jnp.float32)
    row_live = (jnp.arange(text_len, dtype=jnp.int32)[None, :] < lengths[:, None]).astype(
        jnp.bfloat16
    )
    query_float = queries.astype(jnp.float32).reshape(
        seq_count, text_len, key_heads, group_size, head_dim
    )
    query_scale = rms_scale(query_float)
    query_normed = (query_float * query_scale * query_gain).astype(jnp.bfloat16)
    masked_grad = (out_grad * row_live[:, :, None]).reshape(
        seq_count, text_len, key_heads, group_size, head_dim
    )
    query_part, key_part, value_part = attend(
        query_normed, masked_grad, seq_keys, seq_values, key_live
    )
    pick_float = picker.astype(jnp.float32)[:, :, None, None, None]
    image_value = jnp.sum(pick_float * value_part[:, None], axis=0)
    value_rows = image_value.astype(jnp.bfloat16).reshape(img_count, img_rows, key_cols)
    image_key = jnp.sum(pick_float * key_part[:, None], axis=0)
    key_rows = (
        rms_back(key_pre, key_scale, key_gain, image_key)
        .astype(jnp.bfloat16)
        .reshape(img_count, img_rows, key_cols)
    )
    query_grad = (
        rms_back(query_float, query_scale, query_gain, query_part)
        .astype(jnp.bfloat16)
        .reshape(seq_count, text_len, query_cols)
    )
    rows = jnp.concatenate((key_rows, value_rows), axis=2)
    rows = rows.reshape(img_count, mp_size, own_rows, 2 * key_cols).transpose(1, 0, 2, 3)
    all_rows = jnp.stack([swap(rows, 2 * r) if r else rows for r in range(pairs)], axis=1)
    all_rows = all_rows.reshape(-1, 2 * key_cols)
    image_part = lax.dot_general(
        all_rows, weight, (((1,), (1,)), ((), ())), preferred_element_type=jnp.float32
    ).astype(jnp.bfloat16)
    image_part = image_part.reshape(mp_size, pairs * img_count * own_rows, width)
    image_sum = lax.psum_scatter(image_part, "mp", scatter_dimension=0, tiled=False)
    weight_part = lax.dot_general(
        flat, all_rows, (((0,), (0,)), ((), ())), preferred_element_type=jnp.float32
    )
    weight_grad = lax.dynamic_slice_in_dim(weight_part, core * own_width, own_width, axis=0)
    weight_grad = weight_grad + swap(
        lax.dynamic_slice_in_dim(weight_part, (1 - core) * own_width, own_width, axis=0), 1
    )
    image_sum = image_sum.reshape(pairs, img_count, own_rows, width)
    image_grad = jnp.zeros((img_count, own_rows, vis_width), jnp.bfloat16)
    for r in range(pairs):
        piece = swap(image_sum[r], 2 * r) if r else image_sum[r]
        image_grad = lax.dynamic_update_slice_in_dim(
            image_grad, piece, (pair ^ r) * width, axis=2
        )
    return (query_grad, image_grad, weight_grad[:, :key_cols], weight_grad[:, key_cols:])


def solution(mesh):
    placed = (
        P("dp", None, "mp"),
        P("dp", None, "mp"),
        P("dp", "mp", None),
        P("dp", "mp"),
        P("dp", "mp"),
        P(),
        P(),
        P("dp"),
        P("dp"),
        P("dp"),
    )

    def body(*args):
        return per_device(mesh.shape["dp"], *args)

    return jax.shard_map(
        body,
        mesh=mesh,
        in_specs=placed,
        out_specs=(P("dp", None, "mp"), P("dp", "mp", None), P("dp", "mp"), P("dp", "mp")),
        check_vma=False,
    )
```

```python
import math

import jax
import jax.numpy as jnp
from jax import lax
from jax.sharding import PartitionSpec as P

TILE_ROWS = 32


EPSILON = 1e-05


def rms_scale(source):
    return lax.rsqrt(jnp.mean(source * source, axis=-1, keepdims=True) + EPSILON)


def rms_back(source, factor, gain_vector, upstream):
    weighted = gain_vector * upstream
    return factor * weighted - source * (factor * factor * factor) * jnp.mean(
        source * weighted, axis=-1, keepdims=True
    )


def attend(query_normed, masked_grad, key_normed, value_heads, key_live):
    inv_root = 1.0 / math.sqrt(query_normed.shape[-1])
    scores = (
        jnp.einsum(
            "btgjd,brgd->bgjtr", query_normed, key_normed, preferred_element_type=jnp.float32
        )
        * inv_root
    )
    raised = jnp.exp(scores) * key_live[:, None, None, None, :]
    prob_full = raised / jnp.sum(raised, axis=-1, keepdims=True)
    prob_half = prob_full.astype(jnp.bfloat16)
    value_part = jnp.einsum(
        "bgjtr,btgjd->brgd", prob_half, masked_grad, preferred_element_type=jnp.float32
    )
    prob_grad = jnp.einsum(
        "btgjd,brgd->bgjtr", masked_grad, value_heads, preferred_element_type=jnp.float32
    )
    score_grad = (
        prob_full * (prob_grad - jnp.sum(prob_full * prob_grad, axis=-1, keepdims=True))
    ).astype(jnp.bfloat16)
    query_part = (
        jnp.einsum("bgjtr,brgd->btgjd", score_grad, key_normed, preferred_element_type=jnp.float32)
        * inv_root
    )
    key_part = (
        jnp.einsum(
            "bgjtr,btgjd->brgd", score_grad, query_normed, preferred_element_type=jnp.float32
        )
        * inv_root
    )
    return (query_part, key_part, value_part)


def per_device(
    dp_size,
    mp_size,
    queries,
    out_grad,
    images,
    key_weight,
    value_weight,
    query_gain,
    key_gain,
    assignment,
    tile_counts,
    lengths,
):
    seq_count, text_len, query_cols = queries.shape
    img_count, own_rows, vis_width = images.shape
    head_dim = query_gain.shape[0]
    own_width, key_cols = key_weight.shape
    key_heads = key_cols // head_dim
    group_size = query_cols // head_dim // key_heads
    pairs = dp_size // 2
    width = 2 * own_width
    place = lax.axis_index("dp")
    pair, core = place // 2, place % 2

    def swap(value, mask):
        return lax.ppermute(value, "dp", [(i, i ^ mask) for i in range(dp_size)])

    own_weight = jnp.concatenate((key_weight, value_weight), axis=1)
    mate_weight = swap(own_weight, 1)
    weight = jnp.where(
        core == 0,
        jnp.concatenate((own_weight, mate_weight), axis=0),
        jnp.concatenate((mate_weight, own_weight), axis=0),
    )

    def ring(value, step):
        return lax.ppermute(value, "mp", [(i, (i + step) % mp_size) for i in range(mp_size)])

    half = mp_size // 2
    blocks = []
    for r in range(pairs):
        piece = lax.dynamic_slice_in_dim(images, (pair ^ r) * width, width, axis=2)
        piece = swap(piece, 2 * r) if r else piece
        parts = [piece] + [None] * (mp_size - 1)
        right = left = piece
        for k in range(1, half + 1):
            if k < half or r < pairs // 2:
                parts[k] = right = ring(right, 1)
            if k < half or r >= pairs // 2:
                parts[mp_size - k] = left = ring(left, -1)
        blocks.append(jnp.stack(parts))
    img_rows = mp_size * own_rows
    total = 0.0
    for r in range(pairs):
        piece = jnp.dot(
            blocks[r].reshape(-1, width), weight, preferred_element_type=jnp.float32
        ).astype(jnp.bfloat16)
        total = total + (swap(piece, 2 * r) if r else piece).astype(jnp.float32)
    total = total.reshape(mp_size, img_count, own_rows, 2 * key_cols)
    total = total.transpose(1, 0, 2, 3).reshape(img_count, img_rows, 2 * key_cols)
    key_pre = total[..., :key_cols].reshape(img_count, img_rows, key_heads, head_dim)
    value_heads = (
        total[..., key_cols:]
        .astype(jnp.bfloat16)
        .reshape(img_count, img_rows, key_heads, head_dim)
    )
    key_scale = rms_scale(key_pre)
    key_normed = (key_pre * key_scale * key_gain).astype(jnp.bfloat16)
    picker = assignment[:, None] == jnp.arange(img_count, dtype=jnp.int32)[None, :]
    pick_half = picker.astype(jnp.bfloat16)
    seq_keys = jnp.einsum(
        "bi,irgd->brgd", pick_half, key_normed, preferred_element_type=jnp.float32
    ).astype(jnp.bfloat16)
    seq_values = jnp.einsum(
        "bi,irgd->brgd", pick_half, value_heads, preferred_element_type=jnp.float32
    ).astype(jnp.bfloat16)
    seq_tiles = jnp.sum(picker.astype(jnp.int32) * tile_counts[None, :], axis=1)
    owners = (lax.axis_index("mp") - jnp.arange(mp_size, dtype=jnp.int32)) % mp_size
    row_place = (
        owners[:, None] * own_rows + jnp.arange(own_rows, dtype=jnp.int32)[None, :]
    ).reshape(1, img_rows)
    key_live = (row_place < (seq_tiles * TILE_ROWS)[:, None]).astype(jnp.float32)
    row_live = (jnp.arange(text_len, dtype=jnp.int32)[None, :] < lengths[:, None]).astype(
        jnp.bfloat16
    )
    query_float = queries.astype(jnp.float32).reshape(
        seq_count, text_len, key_heads, group_size, head_dim
    )
    query_scale = rms_scale(query_float)
    query_normed = (query_float * query_scale * query_gain).astype(jnp.bfloat16)
    masked_grad = (out_grad * row_live[:, :, None]).reshape(
        seq_count, text_len, key_heads, group_size, head_dim
    )
    query_part, key_part, value_part = attend(
        query_normed, masked_grad, seq_keys, seq_values, key_live
    )
    pick_float = picker.astype(jnp.float32)[:, :, None, None, None]
    image_value = jnp.sum(pick_float * value_part[:, None], axis=0)
    value_rows = image_value.astype(jnp.bfloat16).reshape(img_count, img_rows, key_cols)
    image_key = jnp.sum(pick_float * key_part[:, None], axis=0)
    key_rows = (
        rms_back(key_pre, key_scale, key_gain, image_key)
        .astype(jnp.bfloat16)
        .reshape(img_count, img_rows, key_cols)
    )
    query_grad = (
        rms_back(query_float, query_scale, query_gain, query_part)
        .astype(jnp.bfloat16)
        .reshape(seq_count, text_len, query_cols)
    )
    rows = jnp.concatenate((key_rows, value_rows), axis=2)
    rows = rows.reshape(img_count, mp_size, own_rows, 2 * key_cols).transpose(1, 0, 2, 3)
    all_rows = []
    image_grad = jnp.zeros((img_count, own_rows, vis_width), jnp.bfloat16)
    for r in range(pairs):
        block_rows = (swap(rows, 2 * r) if r else rows).reshape(-1, 2 * key_cols)
        all_rows.append(block_rows)
        term = lax.dot_general(
            block_rows, weight, (((1,), (1,)), ((), ())), preferred_element_type=jnp.float32
        ).astype(jnp.bfloat16)
        term = term.reshape(mp_size, img_count, own_rows, width)
        total = term[0].astype(jnp.float32)
        leftward = rightward = None
        for k in range(half, 0, -1):
            if k < half or r < pairs // 2:
                own = term[k]
                if leftward is not None:
                    own = (own.astype(jnp.float32) + leftward.astype(jnp.float32)).astype(
                        jnp.bfloat16
                    )
                leftward = ring(own, -1)
            if k < half or r >= pairs // 2:
                own = term[mp_size - k]
                if rightward is not None:
                    own = (own.astype(jnp.float32) + rightward.astype(jnp.float32)).astype(
                        jnp.bfloat16
                    )
                rightward = ring(own, 1)
        for arrived in (leftward, rightward):
            if arrived is not None:
                total = total + arrived.astype(jnp.float32)
        piece = total.astype(jnp.bfloat16)
        image_grad = lax.dynamic_update_slice_in_dim(
            image_grad, swap(piece, 2 * r) if r else piece, (pair ^ r) * width, axis=2
        )
    weight_part = lax.dot_general(
        jnp.stack(blocks).reshape(-1, width),
        jnp.stack(all_rows).reshape(-1, 2 * key_cols),
        (((0,), (0,)), ((), ())),
        preferred_element_type=jnp.float32,
    )
    weight_grad = lax.dynamic_slice_in_dim(weight_part, core * own_width, own_width, axis=0)
    weight_grad = weight_grad + swap(
        lax.dynamic_slice_in_dim(weight_part, (1 - core) * own_width, own_width, axis=0), 1
    )
    return (query_grad, image_grad, weight_grad[:, :key_cols], weight_grad[:, key_cols:])


def solution(mesh):
    placed = (
        P("dp", None, "mp"),
        P("dp", None, "mp"),
        P("dp", "mp", None),
        P("dp", "mp"),
        P("dp", "mp"),
        P(),
        P(),
        P("dp"),
        P("dp"),
        P("dp"),
    )

    def body(*args):
        return per_device(mesh.shape["dp"], mesh.shape["mp"], *args)

    return jax.shard_map(
        body,
        mesh=mesh,
        in_specs=placed,
        out_specs=(P("dp", None, "mp"), P("dp", "mp", None), P("dp", "mp"), P("dp", "mp")),
        check_vma=False,
    )
```

```python
import functools
import math

import jax
import jax.numpy as jnp
from jax import lax
from jax.experimental import pallas as pl
from jax.experimental.pallas import tpu as pltpu
from jax.sharding import PartitionSpec as P

TILE_ROWS = 32


EPSILON = 1e-05


def rms_scale(source):
    return lax.rsqrt(jnp.mean(source * source, axis=-1, keepdims=True) + EPSILON)


def rms_back(source, factor, gain_vector, upstream):
    weighted = gain_vector * upstream
    return factor * weighted - source * (factor * factor * factor) * jnp.mean(
        source * weighted, axis=-1, keepdims=True
    )


def dot(left, right, left_dim, right_dim):
    return lax.dot_general(
        left,
        right,
        (((left_dim,), (right_dim,)), ((), ())),
        preferred_element_type=jnp.float32,
    )


def before_kernel(lengths, query, grad, gain, normed, masked):
    text_len, columns = query.shape[1:]
    head_dim = gain.shape[1]
    live = lax.broadcasted_iota(jnp.int32, (text_len, head_dim), 0) < lengths[pl.program_id(0)]
    for j in range(columns // head_dim):
        head = pl.ds(j * head_dim, head_dim)
        rows = pl.ds(j * text_len, text_len)
        source = query[0, :, head].astype(jnp.float32)
        normed[0, 0, rows, :] = (source * rms_scale(source) * gain[...]).astype(jnp.bfloat16)
        upstream = grad[0, :, head]
        masked[0, 0, rows, :] = jnp.where(live, upstream, jnp.zeros_like(upstream))


def before(queries, out_grad, gain, lengths, groups):
    seq_count, text_len, columns = queries.shape
    head_dim = gain.shape[1]
    span = columns // groups
    stacked = span // head_dim * text_len
    source = pl.BlockSpec((1, text_len, span), lambda b, g, *_: (b, 0, g))
    target = pl.BlockSpec((1, 1, stacked, head_dim), lambda b, g, *_: (b, g, 0, 0))
    shape = jax.ShapeDtypeStruct((seq_count, groups, stacked, head_dim), jnp.bfloat16)
    return pl.pallas_call(
        before_kernel,
        out_shape=(shape, shape),
        grid_spec=pltpu.PrefetchScalarGridSpec(
            num_scalar_prefetch=1,
            grid=(seq_count, groups),
            in_specs=[source, source, pl.BlockSpec((1, head_dim), lambda *_: (0, 0))],
            out_specs=(target, target),
        ),
        name="before",
    )(lengths, queries, out_grad, gain)


def attend_kernel(count, assignment, tiles, owners, *refs):
    key_parts, value_parts = refs[:count], refs[count : 2 * count]
    normed, masked, gain = refs[2 * count : 2 * count + 3]
    key_out, value_out, score_out, picked = refs[2 * count + 3 : 2 * count + 7]
    key_pre, key_normed, values, key_sum, value_sum = refs[2 * count + 7 :]
    parts, img_count, own_rows, head_dim = key_parts[0].shape
    img_rows = parts * own_rows
    step = pl.program_id(1)
    inv_root = 1.0 / math.sqrt(head_dim)

    @pl.when(step == 0)
    def _():
        for i in range(img_count):
            for target, sources in ((0, key_parts), (1, value_parts)):
                total = sources[0][:, i].astype(jnp.float32)
                for source in sources[1:]:
                    total = total + source[:, i].astype(jnp.float32)
                total = total.reshape(img_rows, head_dim)
                if target == 0:
                    key_pre[i] = total
                    key_normed[i] = (total * rms_scale(total) * gain[...]).astype(jnp.bfloat16)
                else:
                    values[i] = total.astype(jnp.bfloat16)
        key_sum[...] = jnp.zeros_like(key_sum)
        value_sum[...] = jnp.zeros_like(value_sum)

    image = assignment[step]
    keys = key_normed[image]
    picked[0, 0] = keys
    column = lax.broadcasted_iota(jnp.int32, (1, img_rows), 1)
    place = jnp.zeros_like(column)
    for k in range(parts):
        inside = (column >= k * own_rows) & (column < (k + 1) * own_rows)
        place = jnp.where(inside, column + (owners[k] - k) * own_rows, place)
    live = (place < tiles[image] * TILE_ROWS).astype(jnp.float32)
    queries = normed[0, 0]
    upstream = masked[0, 0]
    raised = jnp.exp(dot(queries, keys, 1, 1) * inv_root) * live
    prob = raised * (1.0 / jnp.sum(raised, axis=-1, keepdims=True))
    prob_grad = dot(upstream, values[image], 1, 1)
    inner = jnp.sum(prob * prob_grad, axis=-1, keepdims=True)
    score_grad = (prob * (prob_grad - inner)).astype(jnp.bfloat16)
    score_out[0, 0] = score_grad
    value_sum[image] += dot(prob.astype(jnp.bfloat16), upstream, 0, 0)
    key_sum[image] += dot(score_grad, queries, 0, 0) * inv_root

    @pl.when(step == pl.num_programs(1) - 1)
    def _():
        for i in range(img_count):
            source = key_pre[i]
            key_rows = rms_back(source, rms_scale(source), gain[...], key_sum[i])
            shape = (parts, own_rows, head_dim)
            key_out[:, i] = key_rows.astype(jnp.bfloat16).reshape(shape)
            value_out[:, i] = value_sum[i].astype(jnp.bfloat16).reshape(shape)


def attend(pieces, normed, masked, gain, assignment, tiles, owners):
    seq_count, groups, stacked, head_dim = normed.shape
    parts, img_count, own_rows, columns = pieces[0].shape
    img_rows = parts * own_rows
    count = len(pieces)
    part = (parts, img_count, own_rows, head_dim)
    keys = pl.BlockSpec(part, lambda g, b, *_: (0, 0, 0, g))
    values = pl.BlockSpec(part, lambda g, b, *_: (0, 0, 0, groups + g))
    stack = pl.BlockSpec((1, 1, stacked, head_dim), lambda g, b, *_: (b, g, 0, 0))
    rows = jax.ShapeDtypeStruct((parts, img_count, own_rows, columns // 2), jnp.bfloat16)
    return pl.pallas_call(
        functools.partial(attend_kernel, count),
        out_shape=(
            rows,
            rows,
            jax.ShapeDtypeStruct((seq_count, groups, stacked, img_rows), jnp.bfloat16),
            jax.ShapeDtypeStruct((seq_count, groups, img_rows, head_dim), jnp.bfloat16),
        ),
        grid_spec=pltpu.PrefetchScalarGridSpec(
            num_scalar_prefetch=3,
            grid=(groups, seq_count),
            in_specs=[keys] * count
            + [values] * count
            + [stack, stack, pl.BlockSpec((1, head_dim), lambda *_: (0, 0))],
            out_specs=(
                keys,
                keys,
                pl.BlockSpec((1, 1, stacked, img_rows), lambda g, b, *_: (b, g, 0, 0)),
                pl.BlockSpec((1, 1, img_rows, head_dim), lambda g, b, *_: (b, g, 0, 0)),
            ),
            scratch_shapes=[
                pltpu.VMEM((img_count, img_rows, head_dim), jnp.float32),
                pltpu.VMEM((img_count, img_rows, head_dim), jnp.bfloat16),
                pltpu.VMEM((img_count, img_rows, head_dim), jnp.bfloat16),
                pltpu.VMEM((img_count, img_rows, head_dim), jnp.float32),
                pltpu.VMEM((img_count, img_rows, head_dim), jnp.float32),
            ],
        ),
        compiler_params=pltpu.CompilerParams(vmem_limit_bytes=32 * 1024 * 1024),
        name="attend",
    )(assignment, tiles, owners, *pieces, *pieces, normed, masked, gain)


def after_kernel(query, score_grad, keys, gain, target):
    text_len, columns = query.shape[1:]
    head_dim = gain.shape[1]
    inv_root = 1.0 / math.sqrt(head_dim)
    for j in range(columns // head_dim):
        head = pl.ds(j * head_dim, head_dim)
        source = query[0, :, head].astype(jnp.float32)
        part = dot(score_grad[0, 0, pl.ds(j * text_len, text_len), :], keys[0, 0], 1, 0)
        grad = rms_back(source, rms_scale(source), gain[...], part * inv_root)
        target[0, :, head] = grad.astype(jnp.bfloat16)


def after(queries, score_grad, keys, gain):
    seq_count, text_len, columns = queries.shape
    groups, stacked, img_rows = score_grad.shape[1:]
    head_dim = gain.shape[1]
    source = pl.BlockSpec((1, text_len, columns // groups), lambda b, g: (b, 0, g))
    return pl.pallas_call(
        after_kernel,
        out_shape=jax.ShapeDtypeStruct(queries.shape, jnp.bfloat16),
        grid=(seq_count, groups),
        in_specs=[
            source,
            pl.BlockSpec((1, 1, stacked, img_rows), lambda b, g: (b, g, 0, 0)),
            pl.BlockSpec((1, 1, img_rows, head_dim), lambda b, g: (b, g, 0, 0)),
            pl.BlockSpec((1, head_dim), lambda *_: (0, 0)),
        ],
        out_specs=source,
        name="after",
    )(queries, score_grad, keys, gain)


def per_device(
    dp_size,
    mp_size,
    queries,
    out_grad,
    images,
    key_weight,
    value_weight,
    query_gain,
    key_gain,
    assignment,
    tile_counts,
    lengths,
):
    img_count, own_rows, vis_width = images.shape
    head_dim = query_gain.shape[0]
    own_width, key_cols = key_weight.shape
    key_heads = key_cols // head_dim
    pairs = dp_size // 2
    width = 2 * own_width
    place = lax.axis_index("dp")
    pair, core = place // 2, place % 2

    def swap(value, mask):
        return lax.ppermute(value, "dp", [(i, i ^ mask) for i in range(dp_size)])

    own_weight = jnp.concatenate((key_weight, value_weight), axis=1)
    mate_weight = swap(own_weight, 1)
    weight = jnp.where(
        core == 0,
        jnp.concatenate((own_weight, mate_weight), axis=0),
        jnp.concatenate((mate_weight, own_weight), axis=0),
    )

    def ring(value, step):
        return lax.ppermute(value, "mp", [(i, (i + step) % mp_size) for i in range(mp_size)])

    half = mp_size // 2
    blocks = []
    for r in range(pairs):
        piece = lax.dynamic_slice_in_dim(images, (pair ^ r) * width, width, axis=2)
        piece = swap(piece, 2 * r) if r else piece
        parts = [piece] + [None] * (mp_size - 1)
        right = left = piece
        for k in range(1, half + 1):
            if k < half or r < pairs // 2:
                parts[k] = right = ring(right, 1)
            if k < half or r >= pairs // 2:
                parts[mp_size - k] = left = ring(left, -1)
        blocks.append(jnp.stack(parts))
    img_rows = mp_size * own_rows
    pieces = []
    for r in range(pairs):
        piece = jnp.dot(
            blocks[r].reshape(-1, width), weight, preferred_element_type=jnp.float32
        ).astype(jnp.bfloat16)
        piece = swap(piece, 2 * r) if r else piece
        pieces.append(piece.reshape(mp_size, img_count, own_rows, 2 * key_cols))
    if pairs > 4:
        pieces = [sum(piece.astype(jnp.float32) for piece in pieces)]
    query_gain, key_gain = query_gain[None, :], key_gain[None, :]
    normed, masked = before(queries, out_grad, query_gain, lengths, key_heads)
    owners = (lax.axis_index("mp") - jnp.arange(mp_size, dtype=jnp.int32)) % mp_size
    key_rows, value_rows, score_grad, seq_keys = attend(
        pieces, normed, masked, key_gain, assignment, tile_counts, owners
    )
    query_grad = after(queries, score_grad, seq_keys, query_gain)
    rows = jnp.concatenate((key_rows, value_rows), axis=3)
    all_rows = []
    image_grad = jnp.zeros((img_count, own_rows, vis_width), jnp.bfloat16)
    for r in range(pairs):
        block_rows = (swap(rows, 2 * r) if r else rows).reshape(-1, 2 * key_cols)
        all_rows.append(block_rows)
        term = lax.dot_general(
            block_rows, weight, (((1,), (1,)), ((), ())), preferred_element_type=jnp.float32
        ).astype(jnp.bfloat16)
        term = term.reshape(mp_size, img_count, own_rows, width)
        total = term[0].astype(jnp.float32)
        leftward = rightward = None
        for k in range(half, 0, -1):
            if k < half or r < pairs // 2:
                own = term[k]
                if leftward is not None:
                    own = (own.astype(jnp.float32) + leftward.astype(jnp.float32)).astype(
                        jnp.bfloat16
                    )
                leftward = ring(own, -1)
            if k < half or r >= pairs // 2:
                own = term[mp_size - k]
                if rightward is not None:
                    own = (own.astype(jnp.float32) + rightward.astype(jnp.float32)).astype(
                        jnp.bfloat16
                    )
                rightward = ring(own, 1)
        for arrived in (leftward, rightward):
            if arrived is not None:
                total = total + arrived.astype(jnp.float32)
        piece = total.astype(jnp.bfloat16)
        image_grad = lax.dynamic_update_slice_in_dim(
            image_grad, swap(piece, 2 * r) if r else piece, (pair ^ r) * width, axis=2
        )
    weight_part = lax.dot_general(
        jnp.stack(blocks).reshape(-1, width),
        jnp.stack(all_rows).reshape(-1, 2 * key_cols),
        (((0,), (0,)), ((), ())),
        preferred_element_type=jnp.float32,
    )
    weight_grad = lax.dynamic_slice_in_dim(weight_part, core * own_width, own_width, axis=0)
    weight_grad = weight_grad + swap(
        lax.dynamic_slice_in_dim(weight_part, (1 - core) * own_width, own_width, axis=0), 1
    )
    return (query_grad, image_grad, weight_grad[:, :key_cols], weight_grad[:, key_cols:])


def solution(mesh):
    placed = (
        P("dp", None, "mp"),
        P("dp", None, "mp"),
        P("dp", "mp", None),
        P("dp", "mp"),
        P("dp", "mp"),
        P(),
        P(),
        P("dp"),
        P("dp"),
        P("dp"),
    )

    def body(*args):
        return per_device(mesh.shape["dp"], mesh.shape["mp"], *args)

    return jax.shard_map(
        body,
        mesh=mesh,
        in_specs=placed,
        out_specs=(P("dp", None, "mp"), P("dp", "mp", None), P("dp", "mp"), P("dp", "mp")),
        check_vma=False,
    )
```

```python
import functools
import math

import jax
import jax.numpy as jnp
from jax import lax
from jax.experimental import pallas as pl
from jax.experimental.pallas import tpu as pltpu
from jax.sharding import PartitionSpec as P

TILE_ROWS = 32


EPSILON = 1e-05


def rms_scale(source):
    return lax.rsqrt(jnp.mean(source * source, axis=-1, keepdims=True) + EPSILON)


def rms_back(source, factor, gain_vector, upstream):
    weighted = gain_vector * upstream
    return factor * weighted - source * (factor * factor * factor) * jnp.mean(
        source * weighted, axis=-1, keepdims=True
    )


def dot(left, right, left_dim, right_dim):
    return lax.dot_general(
        left,
        right,
        (((left_dim,), (right_dim,)), ((), ())),
        preferred_element_type=jnp.float32,
    )


def before_kernel(lengths, query, grad, gain, normed, masked):
    text_len, columns = query.shape[1:]
    head_dim = gain.shape[1]
    live = lax.broadcasted_iota(jnp.int32, (text_len, head_dim), 0) < lengths[pl.program_id(0)]
    for j in range(columns // head_dim):
        head = pl.ds(j * head_dim, head_dim)
        rows = pl.ds(j * text_len, text_len)
        source = query[0, :, head].astype(jnp.float32)
        normed[0, 0, rows, :] = (source * rms_scale(source) * gain[...]).astype(jnp.bfloat16)
        upstream = grad[0, :, head]
        masked[0, 0, rows, :] = jnp.where(live, upstream, jnp.zeros_like(upstream))


def before(queries, out_grad, gain, lengths, groups):
    seq_count, text_len, columns = queries.shape
    head_dim = gain.shape[1]
    span = columns // groups
    stacked = span // head_dim * text_len
    source = pl.BlockSpec((1, text_len, span), lambda b, g, *_: (b, 0, g))
    target = pl.BlockSpec((1, 1, stacked, head_dim), lambda b, g, *_: (b, g, 0, 0))
    shape = jax.ShapeDtypeStruct((seq_count, groups, stacked, head_dim), jnp.bfloat16)
    return pl.pallas_call(
        before_kernel,
        out_shape=(shape, shape),
        grid_spec=pltpu.PrefetchScalarGridSpec(
            num_scalar_prefetch=1,
            grid=(seq_count, groups),
            in_specs=[source, source, pl.BlockSpec((1, head_dim), lambda *_: (0, 0))],
            out_specs=(target, target),
        ),
        name="before",
    )(lengths, queries, out_grad, gain)


def attend_kernel(count, assignment, tiles, owners, *refs):
    key_parts, value_parts = refs[:count], refs[count : 2 * count]
    normed, masked, gain = refs[2 * count : 2 * count + 3]
    key_out, value_out, score_out, picked = refs[2 * count + 3 : 2 * count + 7]
    key_pre, key_normed, values, key_sum, value_sum = refs[2 * count + 7 :]
    parts, img_count, own_rows, head_dim = key_parts[0].shape
    img_rows = parts * own_rows
    step = pl.program_id(1)
    inv_root = 1.0 / math.sqrt(head_dim)

    @pl.when(step == 0)
    def _():
        for i in range(img_count):
            for target, sources in ((0, key_parts), (1, value_parts)):
                total = sources[0][:, i].astype(jnp.float32)
                for source in sources[1:]:
                    total = total + source[:, i].astype(jnp.float32)
                total = total.reshape(img_rows, head_dim)
                if target == 0:
                    key_pre[i] = total
                    key_normed[i] = (total * rms_scale(total) * gain[...]).astype(jnp.bfloat16)
                else:
                    values[i] = total.astype(jnp.bfloat16)
        key_sum[...] = jnp.zeros_like(key_sum)
        value_sum[...] = jnp.zeros_like(value_sum)

    image = assignment[step]
    keys = key_normed[image]
    picked[0, 0] = keys
    column = lax.broadcasted_iota(jnp.int32, (1, img_rows), 1)
    place = jnp.zeros_like(column)
    for k in range(parts):
        inside = (column >= k * own_rows) & (column < (k + 1) * own_rows)
        place = jnp.where(inside, column + (owners[k] - k) * own_rows, place)
    live = (place < tiles[image] * TILE_ROWS).astype(jnp.float32)
    queries = normed[0, 0]
    upstream = masked[0, 0]
    raised = jnp.exp(dot(queries, keys, 1, 1) * inv_root) * live
    prob = raised * (1.0 / jnp.sum(raised, axis=-1, keepdims=True))
    prob_grad = dot(upstream, values[image], 1, 1)
    inner = jnp.sum(prob * prob_grad, axis=-1, keepdims=True)
    score_grad = (prob * (prob_grad - inner)).astype(jnp.bfloat16)
    score_out[0, 0] = score_grad
    value_sum[image] += dot(prob.astype(jnp.bfloat16), upstream, 0, 0)
    key_sum[image] += dot(score_grad, queries, 0, 0) * inv_root

    @pl.when(step == pl.num_programs(1) - 1)
    def _():
        for i in range(img_count):
            source = key_pre[i]
            key_rows = rms_back(source, rms_scale(source), gain[...], key_sum[i])
            shape = (parts, own_rows, head_dim)
            key_out[:, i] = key_rows.astype(jnp.bfloat16).reshape(shape)
            value_out[:, i] = value_sum[i].astype(jnp.bfloat16).reshape(shape)


def attend(pieces, normed, masked, gain, assignment, tiles, owners):
    seq_count, groups, stacked, head_dim = normed.shape
    parts, img_count, own_rows, columns = pieces[0].shape
    img_rows = parts * own_rows
    count = len(pieces)
    part = (parts, img_count, own_rows, head_dim)
    keys = pl.BlockSpec(part, lambda g, b, *_: (0, 0, 0, g))
    values = pl.BlockSpec(part, lambda g, b, *_: (0, 0, 0, groups + g))
    stack = pl.BlockSpec((1, 1, stacked, head_dim), lambda g, b, *_: (b, g, 0, 0))
    rows = jax.ShapeDtypeStruct((parts, img_count, own_rows, columns // 2), jnp.bfloat16)
    return pl.pallas_call(
        functools.partial(attend_kernel, count),
        out_shape=(
            rows,
            rows,
            jax.ShapeDtypeStruct((seq_count, groups, stacked, img_rows), jnp.bfloat16),
            jax.ShapeDtypeStruct((seq_count, groups, img_rows, head_dim), jnp.bfloat16),
        ),
        grid_spec=pltpu.PrefetchScalarGridSpec(
            num_scalar_prefetch=3,
            grid=(groups, seq_count),
            in_specs=[keys] * count
            + [values] * count
            + [stack, stack, pl.BlockSpec((1, head_dim), lambda *_: (0, 0))],
            out_specs=(
                keys,
                keys,
                pl.BlockSpec((1, 1, stacked, img_rows), lambda g, b, *_: (b, g, 0, 0)),
                pl.BlockSpec((1, 1, img_rows, head_dim), lambda g, b, *_: (b, g, 0, 0)),
            ),
            scratch_shapes=[
                pltpu.VMEM((img_count, img_rows, head_dim), jnp.float32),
                pltpu.VMEM((img_count, img_rows, head_dim), jnp.bfloat16),
                pltpu.VMEM((img_count, img_rows, head_dim), jnp.bfloat16),
                pltpu.VMEM((img_count, img_rows, head_dim), jnp.float32),
                pltpu.VMEM((img_count, img_rows, head_dim), jnp.float32),
            ],
        ),
        compiler_params=pltpu.CompilerParams(vmem_limit_bytes=32 * 1024 * 1024),
        name="attend",
    )(assignment, tiles, owners, *pieces, *pieces, normed, masked, gain)


def after_kernel(query, score_grad, keys, gain, target):
    text_len, columns = query.shape[1:]
    head_dim = gain.shape[1]
    inv_root = 1.0 / math.sqrt(head_dim)
    for j in range(columns // head_dim):
        head = pl.ds(j * head_dim, head_dim)
        source = query[0, :, head].astype(jnp.float32)
        part = dot(score_grad[0, 0, pl.ds(j * text_len, text_len), :], keys[0, 0], 1, 0)
        grad = rms_back(source, rms_scale(source), gain[...], part * inv_root)
        target[0, :, head] = grad.astype(jnp.bfloat16)


def after(queries, score_grad, keys, gain):
    seq_count, text_len, columns = queries.shape
    groups, stacked, img_rows = score_grad.shape[1:]
    head_dim = gain.shape[1]
    source = pl.BlockSpec((1, text_len, columns // groups), lambda b, g: (b, 0, g))
    return pl.pallas_call(
        after_kernel,
        out_shape=jax.ShapeDtypeStruct(queries.shape, jnp.bfloat16),
        grid=(seq_count, groups),
        in_specs=[
            source,
            pl.BlockSpec((1, 1, stacked, img_rows), lambda b, g: (b, g, 0, 0)),
            pl.BlockSpec((1, 1, img_rows, head_dim), lambda b, g: (b, g, 0, 0)),
            pl.BlockSpec((1, head_dim), lambda *_: (0, 0)),
        ],
        out_specs=source,
        name="after",
    )(queries, score_grad, keys, gain)


def per_device(
    dp_size,
    mp_size,
    queries,
    out_grad,
    images,
    key_weight,
    value_weight,
    query_gain,
    key_gain,
    assignment,
    tile_counts,
    lengths,
):
    img_count, own_rows, vis_width = images.shape
    head_dim = query_gain.shape[0]
    own_width, key_cols = key_weight.shape
    key_heads = key_cols // head_dim
    cols = 2 * key_cols
    pairs = dp_size // 2
    width = 2 * own_width
    place = lax.axis_index("dp")
    pair, core = place // 2, place % 2
    line = lax.axis_index("mp")
    is_inner = (line == 1) | (line == 2)

    def swap(value, mask):
        return lax.ppermute(value, "dp", [(i, i ^ mask) for i in range(dp_size)])

    def inward(value):
        return lax.ppermute(value, "mp", [(0, 1), (3, 2)])

    def outward(value):
        return lax.ppermute(value, "mp", [(1, 0), (2, 3)])

    def across(value):
        return lax.ppermute(value, "mp", [(1, 2), (2, 1)])

    own_weight = jnp.concatenate((key_weight, value_weight), axis=1)
    both_weight = jnp.concatenate((own_weight, inward(own_weight)), axis=1)
    mate_weight = swap(both_weight, 1)
    weight = jnp.where(
        core == 0,
        jnp.concatenate((both_weight, mate_weight), axis=0),
        jnp.concatenate((mate_weight, both_weight), axis=0),
    )

    blocks = []
    own_pieces = []
    outer_total = 0.0
    for r in range(pairs):
        piece = lax.dynamic_slice_in_dim(images, (pair ^ r) * width, width, axis=2)
        piece = swap(piece, 2 * r) if r else piece
        outer = inward(piece)
        block = jnp.stack((piece, outer, across(piece), across(outer)))
        blocks.append(block)
        part = jnp.dot(block.reshape(-1, width), weight, preferred_element_type=jnp.float32)
        part = part.astype(jnp.bfloat16)
        part = swap(part, 2 * r) if r else part
        own_pieces.append(part[:, :cols])
        outer_total = outer_total + part[:, cols:].astype(jnp.float32)
    given = outward(outer_total.astype(jnp.bfloat16))
    own_total = sum(piece.astype(jnp.float32) for piece in own_pieces)
    total = jnp.where(is_inner, own_total, given.astype(jnp.float32))
    total = total.reshape(mp_size, img_count, own_rows, cols)
    query_gain, key_gain = query_gain[None, :], key_gain[None, :]
    normed, masked = before(queries, out_grad, query_gain, lengths, key_heads)
    owners = jnp.where(
        line < 2, jnp.array((1, 0, 2, 3), jnp.int32), jnp.array((2, 3, 1, 0), jnp.int32)
    )
    key_rows, value_rows, score_grad, seq_keys = attend(
        [total], normed, masked, key_gain, assignment, tile_counts, owners
    )
    query_grad = after(queries, score_grad, seq_keys, query_gain)

    rows = jnp.concatenate((key_rows, value_rows), axis=3).reshape(-1, cols)
    both_rows = jnp.concatenate((rows, inward(rows)), axis=1)
    all_rows = []
    image_grad = jnp.zeros((img_count, own_rows, vis_width), jnp.bfloat16)
    for r in range(pairs):
        block_rows = swap(both_rows, 2 * r) if r else both_rows
        all_rows.append(block_rows)
        term = dot(block_rows, weight, 1, 1).reshape(mp_size, img_count, own_rows, width)
        far = across(term[3].astype(jnp.bfloat16)).astype(jnp.float32)
        near = across(term[2].astype(jnp.bfloat16)).astype(jnp.float32)
        given = outward((term[1] + far).astype(jnp.bfloat16))
        piece = jnp.where(is_inner, (term[0] + near).astype(jnp.bfloat16), given)
        image_grad = lax.dynamic_update_slice_in_dim(
            image_grad, swap(piece, 2 * r) if r else piece, (pair ^ r) * width, axis=2
        )
    weight_part = dot(
        jnp.stack(blocks).reshape(-1, width), jnp.stack(all_rows).reshape(-1, 2 * cols), 0, 0
    )
    weight_grad = lax.dynamic_slice_in_dim(weight_part, core * own_width, own_width, axis=0)
    weight_grad = weight_grad + swap(
        lax.dynamic_slice_in_dim(weight_part, (1 - core) * own_width, own_width, axis=0), 1
    )
    given = outward(weight_grad[:, cols:].astype(jnp.bfloat16)).astype(jnp.float32)
    weight_grad = jnp.where(is_inner, weight_grad[:, :cols], given)
    return (query_grad, image_grad, weight_grad[:, :key_cols], weight_grad[:, key_cols:])


def solution(mesh):
    placed = (
        P("dp", None, "mp"),
        P("dp", None, "mp"),
        P("dp", "mp", None),
        P("dp", "mp"),
        P("dp", "mp"),
        P(),
        P(),
        P("dp"),
        P("dp"),
        P("dp"),
    )

    def body(*args):
        return per_device(mesh.shape["dp"], mesh.shape["mp"], *args)

    return jax.shard_map(
        body,
        mesh=mesh,
        in_specs=placed,
        out_specs=(P("dp", None, "mp"), P("dp", "mp", None), P("dp", "mp"), P("dp", "mp")),
        check_vma=False,
    )
```

```python
import functools
import math

import jax
import jax.numpy as jnp
from jax import lax
from jax.experimental import pallas as pl
from jax.experimental.pallas import tpu as pltpu
from jax.sharding import PartitionSpec as P

TILE_ROWS = 32
CHUNKS = 4


EPSILON = 1e-05


def rms_scale(source):
    return lax.rsqrt(jnp.mean(source * source, axis=-1, keepdims=True) + EPSILON)


def rms_back(source, factor, gain_vector, upstream):
    weighted = gain_vector * upstream
    return factor * weighted - source * (factor * factor * factor) * jnp.mean(
        source * weighted, axis=-1, keepdims=True
    )


def dot(left, right, left_dim, right_dim):
    return lax.dot_general(
        left,
        right,
        (((left_dim,), (right_dim,)), ((), ())),
        preferred_element_type=jnp.float32,
    )


def before_kernel(lengths, query, grad, gain, normed, masked):
    text_len, columns = query.shape[1:]
    head_dim = gain.shape[1]
    live = lax.broadcasted_iota(jnp.int32, (text_len, head_dim), 0) < lengths[pl.program_id(0)]
    for j in range(columns // head_dim):
        head = pl.ds(j * head_dim, head_dim)
        rows = pl.ds(j * text_len, text_len)
        source = query[0, :, head].astype(jnp.float32)
        normed[0, 0, rows, :] = (source * rms_scale(source) * gain[...]).astype(jnp.bfloat16)
        upstream = grad[0, :, head]
        masked[0, 0, rows, :] = jnp.where(live, upstream, jnp.zeros_like(upstream))


def before(queries, out_grad, gain, lengths, groups):
    seq_count, text_len, columns = queries.shape
    head_dim = gain.shape[1]
    span = columns // groups
    stacked = span // head_dim * text_len
    source = pl.BlockSpec((1, text_len, span), lambda b, g, *_: (b, 0, g))
    target = pl.BlockSpec((1, 1, stacked, head_dim), lambda b, g, *_: (b, g, 0, 0))
    shape = jax.ShapeDtypeStruct((seq_count, groups, stacked, head_dim), jnp.bfloat16)
    return pl.pallas_call(
        before_kernel,
        out_shape=(shape, shape),
        grid_spec=pltpu.PrefetchScalarGridSpec(
            num_scalar_prefetch=1,
            grid=(seq_count, groups),
            in_specs=[source, source, pl.BlockSpec((1, head_dim), lambda *_: (0, 0))],
            out_specs=(target, target),
        ),
        name="before",
    )(lengths, queries, out_grad, gain)


def attend_kernel(count, assignment, tiles, owners, *refs):
    key_parts, value_parts = refs[:count], refs[count : 2 * count]
    normed, masked, gain = refs[2 * count : 2 * count + 3]
    key_out, value_out, score_out, picked = refs[2 * count + 3 : 2 * count + 7]
    key_pre, key_normed, values, key_sum, value_sum = refs[2 * count + 7 :]
    parts, img_count, own_rows, head_dim = key_parts[0].shape
    img_rows = parts * own_rows
    step = pl.program_id(1)
    inv_root = 1.0 / math.sqrt(head_dim)

    @pl.when(step == 0)
    def _():
        for i in range(img_count):
            for target, sources in ((0, key_parts), (1, value_parts)):
                total = sources[0][:, i].astype(jnp.float32)
                for source in sources[1:]:
                    total = total + source[:, i].astype(jnp.float32)
                total = total.reshape(img_rows, head_dim)
                if target == 0:
                    key_pre[i] = total
                    key_normed[i] = (total * rms_scale(total) * gain[...]).astype(jnp.bfloat16)
                else:
                    values[i] = total.astype(jnp.bfloat16)
        key_sum[...] = jnp.zeros_like(key_sum)
        value_sum[...] = jnp.zeros_like(value_sum)

    image = assignment[step]
    keys = key_normed[image]
    picked[0, 0] = keys
    column = lax.broadcasted_iota(jnp.int32, (1, img_rows), 1)
    place = jnp.zeros_like(column)
    for k in range(parts):
        inside = (column >= k * own_rows) & (column < (k + 1) * own_rows)
        place = jnp.where(inside, column + (owners[k] - k) * own_rows, place)
    live = (place < tiles[image] * TILE_ROWS).astype(jnp.float32)
    queries = normed[0, 0]
    upstream = masked[0, 0]
    raised = jnp.exp(dot(queries, keys, 1, 1) * inv_root) * live
    prob = raised * (1.0 / jnp.sum(raised, axis=-1, keepdims=True))
    prob_grad = dot(upstream, values[image], 1, 1)
    inner = jnp.sum(prob * prob_grad, axis=-1, keepdims=True)
    score_grad = (prob * (prob_grad - inner)).astype(jnp.bfloat16)
    score_out[0, 0] = score_grad
    value_sum[image] += dot(prob.astype(jnp.bfloat16), upstream, 0, 0)
    key_sum[image] += dot(score_grad, queries, 0, 0) * inv_root

    @pl.when(step == pl.num_programs(1) - 1)
    def _():
        for i in range(img_count):
            source = key_pre[i]
            key_rows = rms_back(source, rms_scale(source), gain[...], key_sum[i])
            shape = (parts, own_rows, head_dim)
            key_out[:, i] = key_rows.astype(jnp.bfloat16).reshape(shape)
            value_out[:, i] = value_sum[i].astype(jnp.bfloat16).reshape(shape)


def attend(pieces, normed, masked, gain, assignment, tiles, owners):
    seq_count, groups, stacked, head_dim = normed.shape
    parts, img_count, own_rows, columns = pieces[0].shape
    img_rows = parts * own_rows
    count = len(pieces)
    part = (parts, img_count, own_rows, head_dim)
    keys = pl.BlockSpec(part, lambda g, b, *_: (0, 0, 0, g))
    values = pl.BlockSpec(part, lambda g, b, *_: (0, 0, 0, groups + g))
    stack = pl.BlockSpec((1, 1, stacked, head_dim), lambda g, b, *_: (b, g, 0, 0))
    rows = jax.ShapeDtypeStruct((parts, img_count, own_rows, columns // 2), jnp.bfloat16)
    return pl.pallas_call(
        functools.partial(attend_kernel, count),
        out_shape=(
            rows,
            rows,
            jax.ShapeDtypeStruct((seq_count, groups, stacked, img_rows), jnp.bfloat16),
            jax.ShapeDtypeStruct((seq_count, groups, img_rows, head_dim), jnp.bfloat16),
        ),
        grid_spec=pltpu.PrefetchScalarGridSpec(
            num_scalar_prefetch=3,
            grid=(groups, seq_count),
            in_specs=[keys] * count
            + [values] * count
            + [stack, stack, pl.BlockSpec((1, head_dim), lambda *_: (0, 0))],
            out_specs=(
                keys,
                keys,
                pl.BlockSpec((1, 1, stacked, img_rows), lambda g, b, *_: (b, g, 0, 0)),
                pl.BlockSpec((1, 1, img_rows, head_dim), lambda g, b, *_: (b, g, 0, 0)),
            ),
            scratch_shapes=[
                pltpu.VMEM((img_count, img_rows, head_dim), jnp.float32),
                pltpu.VMEM((img_count, img_rows, head_dim), jnp.bfloat16),
                pltpu.VMEM((img_count, img_rows, head_dim), jnp.bfloat16),
                pltpu.VMEM((img_count, img_rows, head_dim), jnp.float32),
                pltpu.VMEM((img_count, img_rows, head_dim), jnp.float32),
            ],
        ),
        compiler_params=pltpu.CompilerParams(vmem_limit_bytes=32 * 1024 * 1024),
        name="attend",
    )(assignment, tiles, owners, *pieces, *pieces, normed, masked, gain)


def after_kernel(query, score_grad, keys, gain, target):
    text_len, columns = query.shape[1:]
    head_dim = gain.shape[1]
    inv_root = 1.0 / math.sqrt(head_dim)
    for j in range(columns // head_dim):
        head = pl.ds(j * head_dim, head_dim)
        source = query[0, :, head].astype(jnp.float32)
        part = dot(score_grad[0, 0, pl.ds(j * text_len, text_len), :], keys[0, 0], 1, 0)
        grad = rms_back(source, rms_scale(source), gain[...], part * inv_root)
        target[0, :, head] = grad.astype(jnp.bfloat16)


def after(queries, score_grad, keys, gain):
    seq_count, text_len, columns = queries.shape
    groups, stacked, img_rows = score_grad.shape[1:]
    head_dim = gain.shape[1]
    source = pl.BlockSpec((1, text_len, columns // groups), lambda b, g: (b, 0, g))
    return pl.pallas_call(
        after_kernel,
        out_shape=jax.ShapeDtypeStruct(queries.shape, jnp.bfloat16),
        grid=(seq_count, groups),
        in_specs=[
            source,
            pl.BlockSpec((1, 1, stacked, img_rows), lambda b, g: (b, g, 0, 0)),
            pl.BlockSpec((1, 1, img_rows, head_dim), lambda b, g: (b, g, 0, 0)),
            pl.BlockSpec((1, head_dim), lambda *_: (0, 0)),
        ],
        out_specs=source,
        name="after",
    )(queries, score_grad, keys, gain)


def per_device(
    mp_size,
    queries,
    out_grad,
    images,
    key_weight,
    value_weight,
    query_gain,
    key_gain,
    assignment,
    tile_counts,
    lengths,
):
    img_count, own_rows, vis_width = images.shape
    head_dim = query_gain.shape[0]
    key_cols = key_weight.shape[1]
    key_heads = key_cols // head_dim
    cols = 2 * key_cols
    half = mp_size // 2
    width = vis_width // CHUNKS

    def ring(value, step):
        return lax.ppermute(value, "mp", [(i, (i + step) % mp_size) for i in range(mp_size)])

    own_weight = jnp.concatenate((key_weight, value_weight), axis=1)
    weight = lax.all_gather(own_weight, "dp", axis=0, tiled=True)

    blocks = []
    total = 0.0
    for c in range(CHUNKS):
        piece = images[:, :, c * width : (c + 1) * width]
        parts = [piece] + [None] * (mp_size - 1)
        right = left = piece
        for k in range(1, half + 1):
            if k < half or c < CHUNKS // 2:
                parts[k] = right = ring(right, 1)
            if k < half or c >= CHUNKS // 2:
                parts[mp_size - k] = left = ring(left, -1)
        blocks.append(jnp.stack(parts).reshape(-1, width))
        total = total + dot(blocks[c], weight[c * width : (c + 1) * width], 1, 0)
    total = total.reshape(mp_size, img_count, own_rows, cols)
    query_gain, key_gain = query_gain[None, :], key_gain[None, :]
    normed, masked = before(queries, out_grad, query_gain, lengths, key_heads)
    owners = (lax.axis_index("mp") - jnp.arange(mp_size, dtype=jnp.int32)) % mp_size
    key_rows, value_rows, score_grad, seq_keys = attend(
        [total], normed, masked, key_gain, assignment, tile_counts, owners
    )
    query_grad = after(queries, score_grad, seq_keys, query_gain)
    rows = jnp.concatenate((key_rows, value_rows), axis=3).reshape(-1, cols)
    image_grad = []
    for c in range(CHUNKS):
        term = dot(rows, weight[c * width : (c + 1) * width], 1, 1)
        term = term.astype(jnp.bfloat16).reshape(mp_size, img_count, own_rows, width)
        total = term[0].astype(jnp.float32)
        leftward = rightward = None
        for k in range(half, 0, -1):
            if k < half or c < CHUNKS // 2:
                own = term[k]
                if leftward is not None:
                    own = (own.astype(jnp.float32) + leftward.astype(jnp.float32)).astype(
                        jnp.bfloat16
                    )
                leftward = ring(own, -1)
            if k < half or c >= CHUNKS // 2:
                own = term[mp_size - k]
                if rightward is not None:
                    own = (own.astype(jnp.float32) + rightward.astype(jnp.float32)).astype(
                        jnp.bfloat16
                    )
                rightward = ring(own, 1)
        for arrived in (leftward, rightward):
            if arrived is not None:
                total = total + arrived.astype(jnp.float32)
        image_grad.append(total.astype(jnp.bfloat16))
    image_grad = jnp.concatenate(image_grad, axis=2)
    weight_part = jnp.concatenate(
        [dot(block, rows, 0, 0).astype(jnp.bfloat16) for block in blocks], axis=0
    )
    weight_grad = lax.psum_scatter(weight_part, "dp", scatter_dimension=0, tiled=True)
    weight_grad = weight_grad.astype(jnp.float32)
    return (query_grad, image_grad, weight_grad[:, :key_cols], weight_grad[:, key_cols:])


def solution(mesh):
    placed = (
        P("dp", None, "mp"),
        P("dp", None, "mp"),
        P("dp", "mp", None),
        P("dp", "mp"),
        P("dp", "mp"),
        P(),
        P(),
        P("dp"),
        P("dp"),
        P("dp"),
    )

    def body(*args):
        return per_device(mesh.shape["mp"], *args)

    return jax.shard_map(
        body,
        mesh=mesh,
        in_specs=placed,
        out_specs=(P("dp", None, "mp"), P("dp", "mp", None), P("dp", "mp"), P("dp", "mp")),
        check_vma=False,
    )
```

```python
import functools
import math

import jax
import jax.numpy as jnp
from jax import lax
from jax.experimental import pallas as pl
from jax.experimental.pallas import tpu as pltpu
from jax.sharding import PartitionSpec as P

TILE_ROWS = 32


EPSILON = 1e-05


def rms_scale(source):
    return lax.rsqrt(jnp.mean(source * source, axis=-1, keepdims=True) + EPSILON)


def rms_back(source, factor, gain_vector, upstream):
    weighted = gain_vector * upstream
    return factor * weighted - source * (factor * factor * factor) * jnp.mean(
        source * weighted, axis=-1, keepdims=True
    )


def dot(left, right, left_dim, right_dim):
    return lax.dot_general(
        left,
        right,
        (((left_dim,), (right_dim,)), ((), ())),
        preferred_element_type=jnp.float32,
    )


def before_kernel(lengths, query, grad, gain, normed, masked):
    text_len, columns = query.shape[1:]
    head_dim = gain.shape[1]
    live = lax.broadcasted_iota(jnp.int32, (text_len, head_dim), 0) < lengths[pl.program_id(0)]
    for j in range(columns // head_dim):
        head = pl.ds(j * head_dim, head_dim)
        rows = pl.ds(j * text_len, text_len)
        source = query[0, :, head].astype(jnp.float32)
        normed[0, 0, rows, :] = (source * rms_scale(source) * gain[...]).astype(jnp.bfloat16)
        upstream = grad[0, :, head]
        masked[0, 0, rows, :] = jnp.where(live, upstream, jnp.zeros_like(upstream))


def before(queries, out_grad, gain, lengths, groups):
    seq_count, text_len, columns = queries.shape
    head_dim = gain.shape[1]
    span = columns // groups
    stacked = span // head_dim * text_len
    source = pl.BlockSpec((1, text_len, span), lambda b, g, *_: (b, 0, g))
    target = pl.BlockSpec((1, 1, stacked, head_dim), lambda b, g, *_: (b, g, 0, 0))
    shape = jax.ShapeDtypeStruct((seq_count, groups, stacked, head_dim), jnp.bfloat16)
    return pl.pallas_call(
        before_kernel,
        out_shape=(shape, shape),
        grid_spec=pltpu.PrefetchScalarGridSpec(
            num_scalar_prefetch=1,
            grid=(seq_count, groups),
            in_specs=[source, source, pl.BlockSpec((1, head_dim), lambda *_: (0, 0))],
            out_specs=(target, target),
        ),
        name="before",
    )(lengths, queries, out_grad, gain)


def attend_kernel(count, assignment, tiles, owners, *refs):
    key_parts, value_parts = refs[:count], refs[count : 2 * count]
    normed, masked, gain = refs[2 * count : 2 * count + 3]
    rows_out, score_out, picked = refs[2 * count + 3 : 2 * count + 6]
    key_pre, key_normed, values, key_sum, value_sum = refs[2 * count + 6 :]
    img_count, own_rows, head_dim = key_parts[0].shape[1:]
    parts = rows_out.shape[0]
    img_rows = parts * own_rows
    group, step = pl.program_id(0), pl.program_id(1)
    inv_root = 1.0 / math.sqrt(head_dim)

    @pl.when(step == 0)
    def _():
        for i in range(img_count):
            keys, upper = [
                jnp.concatenate(
                    [source[:, i].reshape(-1, head_dim) for source in sources], axis=0
                )
                for sources in (key_parts, value_parts)
            ]
            key_pre[i] = keys
            key_normed[i] = (keys * rms_scale(keys) * gain[...]).astype(jnp.bfloat16)
            values[i] = upper.astype(jnp.bfloat16)
        key_sum[...] = jnp.zeros_like(key_sum)
        value_sum[...] = jnp.zeros_like(value_sum)

    image = assignment[step]
    keys = key_normed[image]
    picked[0, 0] = keys
    column = lax.broadcasted_iota(jnp.int32, (1, img_rows), 1)
    place = jnp.zeros_like(column)
    for k in range(parts):
        inside = (column >= k * own_rows) & (column < (k + 1) * own_rows)
        place = jnp.where(inside, column + (owners[k] - k) * own_rows, place)
    live = (place < tiles[image] * TILE_ROWS).astype(jnp.float32)
    queries = normed[0, 0]
    upstream = masked[0, 0]
    raised = jnp.exp(dot(queries, keys, 1, 1) * inv_root) * live
    prob = raised * (1.0 / jnp.sum(raised, axis=-1, keepdims=True))
    prob_grad = dot(upstream, values[image], 1, 1)
    inner = jnp.sum(prob * prob_grad, axis=-1, keepdims=True)
    score_grad = (prob * (prob_grad - inner)).astype(jnp.bfloat16)
    score_out[0, 0] = score_grad
    value_sum[image] += dot(prob.astype(jnp.bfloat16), upstream, 0, 0)
    key_sum[image] += dot(score_grad, queries, 0, 0) * inv_root

    @pl.when(step == pl.num_programs(1) - 1)
    def _():
        shape = (parts, own_rows, head_dim)
        key_cols = pl.ds(pl.multiple_of(group * head_dim, head_dim), head_dim)
        value_cols = pl.ds(
            pl.multiple_of((pl.num_programs(0) + group) * head_dim, head_dim), head_dim
        )
        for i in range(img_count):
            source = key_pre[i]
            key_rows = rms_back(source, rms_scale(source), gain[...], key_sum[i])
            rows_out[:, i, :, key_cols] = key_rows.astype(jnp.bfloat16).reshape(shape)
            rows_out[:, i, :, value_cols] = value_sum[i].astype(jnp.bfloat16).reshape(shape)


def attend(pieces, normed, masked, gain, assignment, tiles, owners):
    seq_count, groups, stacked, head_dim = normed.shape
    img_count, own_rows, columns = pieces[0].shape[1:]
    parts = sum(piece.shape[0] for piece in pieces)
    img_rows = parts * own_rows
    shapes = [(piece.shape[0], img_count, own_rows, head_dim) for piece in pieces]
    keys = [pl.BlockSpec(shape, lambda g, b, *_: (0, 0, 0, g)) for shape in shapes]
    values = [pl.BlockSpec(shape, lambda g, b, *_: (0, 0, 0, groups + g)) for shape in shapes]
    stack = pl.BlockSpec((1, 1, stacked, head_dim), lambda g, b, *_: (b, g, 0, 0))
    rows = (parts, img_count, own_rows, columns)
    return pl.pallas_call(
        functools.partial(attend_kernel, len(pieces)),
        out_shape=(
            jax.ShapeDtypeStruct(rows, jnp.bfloat16),
            jax.ShapeDtypeStruct((seq_count, groups, stacked, img_rows), jnp.bfloat16),
            jax.ShapeDtypeStruct((seq_count, groups, img_rows, head_dim), jnp.bfloat16),
        ),
        grid_spec=pltpu.PrefetchScalarGridSpec(
            num_scalar_prefetch=3,
            grid=(groups, seq_count),
            in_specs=keys
            + values
            + [stack, stack, pl.BlockSpec((1, head_dim), lambda *_: (0, 0))],
            out_specs=(
                pl.BlockSpec(rows, lambda *_: (0, 0, 0, 0)),
                pl.BlockSpec((1, 1, stacked, img_rows), lambda g, b, *_: (b, g, 0, 0)),
                pl.BlockSpec((1, 1, img_rows, head_dim), lambda g, b, *_: (b, g, 0, 0)),
            ),
            scratch_shapes=[
                pltpu.VMEM((img_count, img_rows, head_dim), jnp.float32),
                pltpu.VMEM((img_count, img_rows, head_dim), jnp.bfloat16),
                pltpu.VMEM((img_count, img_rows, head_dim), jnp.bfloat16),
                pltpu.VMEM((img_count, img_rows, head_dim), jnp.float32),
                pltpu.VMEM((img_count, img_rows, head_dim), jnp.float32),
            ],
        ),
        compiler_params=pltpu.CompilerParams(vmem_limit_bytes=32 * 1024 * 1024),
        name="attend",
    )(assignment, tiles, owners, *pieces, *pieces, normed, masked, gain)


def after_kernel(query, score_grad, keys, gain, target):
    text_len, columns = query.shape[1:]
    head_dim = gain.shape[1]
    inv_root = 1.0 / math.sqrt(head_dim)
    for j in range(columns // head_dim):
        head = pl.ds(j * head_dim, head_dim)
        source = query[0, :, head].astype(jnp.float32)
        part = dot(score_grad[0, 0, pl.ds(j * text_len, text_len), :], keys[0, 0], 1, 0)
        grad = rms_back(source, rms_scale(source), gain[...], part * inv_root)
        target[0, :, head] = grad.astype(jnp.bfloat16)


def after(queries, score_grad, keys, gain):
    seq_count, text_len, columns = queries.shape
    groups, stacked, img_rows = score_grad.shape[1:]
    head_dim = gain.shape[1]
    source = pl.BlockSpec((1, text_len, columns // groups), lambda b, g: (b, 0, g))
    return pl.pallas_call(
        after_kernel,
        out_shape=jax.ShapeDtypeStruct(queries.shape, jnp.bfloat16),
        grid=(seq_count, groups),
        in_specs=[
            source,
            pl.BlockSpec((1, 1, stacked, img_rows), lambda b, g: (b, g, 0, 0)),
            pl.BlockSpec((1, 1, img_rows, head_dim), lambda b, g: (b, g, 0, 0)),
            pl.BlockSpec((1, head_dim), lambda *_: (0, 0)),
        ],
        out_specs=source,
        name="after",
    )(queries, score_grad, keys, gain)


def terms_kernel(rows, weight, own, left, right, leaving_right, leaving_left):
    parts, img_count, own_rows, cols = rows.shape
    first = leaving_right.shape[0]
    term = dot(rows[...].reshape(-1, cols), weight[...], 1, 1).astype(jnp.bfloat16)
    term = term.reshape(parts, img_count, own_rows, -1)
    own[...] = term[0]
    left[...] = term[1]
    right[...] = term[2]
    leaving_right[...] = term[3, :first]
    leaving_left[...] = term[3, first:]


def terms(rows, weight, chunks):
    parts, img_count, own_rows, cols = rows.shape
    vis_width = weight.shape[0]
    width = vis_width // chunks
    first = img_count // 2
    counts = (img_count, img_count, img_count, first, img_count - first)
    return pl.pallas_call(
        terms_kernel,
        out_shape=[
            jax.ShapeDtypeStruct((count, own_rows, vis_width), jnp.bfloat16) for count in counts
        ],
        grid=(chunks,),
        in_specs=[
            pl.BlockSpec(rows.shape, lambda c: (0, 0, 0, 0)),
            pl.BlockSpec((width, cols), lambda c: (c, 0)),
        ],
        out_specs=[
            pl.BlockSpec((count, own_rows, width), lambda c: (0, 0, c)) for count in counts
        ],
        compiler_params=pltpu.CompilerParams(vmem_limit_bytes=32 * 1024 * 1024),
        name="terms",
    )(rows, weight)


def per_device(
    dp_size,
    mp_size,
    queries,
    out_grad,
    images,
    key_weight,
    value_weight,
    query_gain,
    key_gain,
    assignment,
    tile_counts,
    lengths,
):
    img_count, own_rows, vis_width = images.shape
    head_dim = query_gain.shape[0]
    own_width, key_cols = key_weight.shape
    key_heads = key_cols // head_dim
    cols = 2 * key_cols
    pairs = dp_size // 2
    place = lax.axis_index("dp")
    pair, core = place // 2, place % 2
    line = lax.axis_index("mp")
    first = img_count // 2

    def ring(value, step):
        return lax.ppermute(value, "mp", [(i, (i + step) % mp_size) for i in range(mp_size)])

    def swap(value, mask):
        return lax.ppermute(value, "dp", [(i, i ^ mask) for i in range(dp_size)])

    from_left, from_right = ring(images, 1), ring(images, -1)
    query_gain, key_gain = query_gain[None, :], key_gain[None, :]
    normed, masked = before(queries, out_grad, query_gain, lengths, key_heads)

    own_weight = jnp.concatenate((key_weight, value_weight), axis=1)
    if pairs > 4:
        weight = lax.all_gather(own_weight, "dp", axis=0, tiled=True)
    else:
        sent = [swap(own_weight, 2 * r) for r in range(1, pairs)]
        weight = jnp.zeros((2 * pairs, own_width, cols), jnp.bfloat16)
        from_left, from_right, sent, weight, normed, masked = lax.optimization_barrier(
            (from_left, from_right, sent, weight, normed, masked)
        )
        mine = jnp.stack([own_weight, *sent])
        mates = swap(mine, 1)
        for r in range(pairs):
            for source, side in ((mine, core), (mates, 1 - core)):
                weight = lax.dynamic_update_slice_in_dim(
                    weight, source[r : r + 1], 2 * (pair ^ r) + side, axis=0
                )
        weight = weight.reshape(vis_width, cols)
    opposite = (ring(from_left[:first], 1), ring(from_right[first:], -1))

    near = jnp.stack((images, from_left, from_right)).reshape(-1, vis_width)
    near_total = dot(near, weight, 1, 0)
    near_total, opposite = lax.optimization_barrier((near_total, opposite))
    near_total = near_total.reshape(3, img_count, own_rows, cols)
    far = jnp.concatenate(opposite).reshape(-1, vis_width)
    far_total = dot(far, weight, 1, 0).reshape(1, img_count, own_rows, cols)
    owners = (line + jnp.array((0, -1, 1, 2), jnp.int32)) % mp_size
    rows, score_grad, seq_keys = attend(
        [near_total, far_total], normed, masked, key_gain, assignment, tile_counts, owners
    )
    query_grad = after(queries, score_grad, seq_keys, query_gain)

    own, to_left, to_right, leaving_right, leaving_left = terms(rows, weight, 4)
    right_half = ring(leaving_right, 1).astype(jnp.float32)
    left_half = ring(leaving_left, -1).astype(jnp.float32)
    to_right = jnp.concatenate(
        ((to_right[:first].astype(jnp.float32) + right_half).astype(jnp.bfloat16), to_right[first:])
    )
    to_left = jnp.concatenate(
        (to_left[:first], (to_left[first:].astype(jnp.float32) + left_half).astype(jnp.bfloat16))
    )
    from_left = ring(to_right, 1).astype(jnp.float32)
    from_right = ring(to_left, -1).astype(jnp.float32)
    image_grad = (own.astype(jnp.float32) + from_left + from_right).astype(jnp.bfloat16)

    all_rows = rows.reshape(-1, cols)
    weight_part = dot(jnp.concatenate((near, far)), all_rows, 0, 0)
    if pairs > 4:
        weight_grad = lax.psum_scatter(weight_part, "dp", scatter_dimension=0, tiled=True)
    else:
        weight_part = weight_part.astype(jnp.bfloat16).reshape(pairs, 2, own_width, cols)
        both = lax.dynamic_index_in_dim(weight_part, core, 1, keepdims=False).astype(jnp.float32)
        both = both + swap(
            lax.dynamic_index_in_dim(weight_part, 1 - core, 1, keepdims=False), 1
        ).astype(jnp.float32)
        weight_grad = lax.dynamic_index_in_dim(both, pair, 0, keepdims=False)
        for r in range(1, pairs):
            sent = lax.dynamic_index_in_dim(both, pair ^ r, 0, keepdims=False)
            weight_grad = weight_grad + swap(sent.astype(jnp.bfloat16), 2 * r).astype(jnp.float32)
    return (query_grad, image_grad, weight_grad[:, :key_cols], weight_grad[:, key_cols:])


def solution(mesh):
    placed = (
        P("dp", None, "mp"),
        P("dp", None, "mp"),
        P("dp", "mp", None),
        P("dp", "mp"),
        P("dp", "mp"),
        P(),
        P(),
        P("dp"),
        P("dp"),
        P("dp"),
    )

    def body(*args):
        return per_device(mesh.shape["dp"], mesh.shape["mp"], *args)

    return jax.shard_map(
        body,
        mesh=mesh,
        in_specs=placed,
        out_specs=(P("dp", None, "mp"), P("dp", "mp", None), P("dp", "mp"), P("dp", "mp")),
        check_vma=False,
    )
```

```python
import functools
import math

import jax
import jax.numpy as jnp
from jax import lax
from jax.experimental import pallas as pl
from jax.experimental.pallas import tpu as pltpu
from jax.sharding import PartitionSpec as P

TILE_ROWS = 32


EPSILON = 1e-05


def rms_scale(source):
    return lax.rsqrt(jnp.mean(source * source, axis=-1, keepdims=True) + EPSILON)


def rms_back(source, factor, gain_vector, upstream):
    weighted = gain_vector * upstream
    return factor * weighted - source * (factor * factor * factor) * jnp.mean(
        source * weighted, axis=-1, keepdims=True
    )


def dot(left, right, left_dim, right_dim):
    return lax.dot_general(
        left,
        right,
        (((left_dim,), (right_dim,)), ((), ())),
        preferred_element_type=jnp.float32,
    )


def before_kernel(lengths, query, grad, gain, normed, masked):
    text_len, columns = query.shape[1:]
    head_dim = gain.shape[1]
    live = lax.broadcasted_iota(jnp.int32, (text_len, head_dim), 0) < lengths[pl.program_id(0)]
    for j in range(columns // head_dim):
        head = pl.ds(j * head_dim, head_dim)
        rows = pl.ds(j * text_len, text_len)
        source = query[0, :, head].astype(jnp.float32)
        normed[0, 0, rows, :] = (source * rms_scale(source) * gain[...]).astype(jnp.bfloat16)
        upstream = grad[0, :, head]
        masked[0, 0, rows, :] = jnp.where(live, upstream, jnp.zeros_like(upstream))


def before(queries, out_grad, gain, lengths, groups):
    seq_count, text_len, columns = queries.shape
    head_dim = gain.shape[1]
    span = columns // groups
    stacked = span // head_dim * text_len
    source = pl.BlockSpec((1, text_len, span), lambda b, g, *_: (b, 0, g))
    target = pl.BlockSpec((1, 1, stacked, head_dim), lambda b, g, *_: (b, g, 0, 0))
    shape = jax.ShapeDtypeStruct((seq_count, groups, stacked, head_dim), jnp.bfloat16)
    return pl.pallas_call(
        before_kernel,
        out_shape=(shape, shape),
        grid_spec=pltpu.PrefetchScalarGridSpec(
            num_scalar_prefetch=1,
            grid=(seq_count, groups),
            in_specs=[source, source, pl.BlockSpec((1, head_dim), lambda *_: (0, 0))],
            out_specs=(target, target),
        ),
        name="before",
    )(lengths, queries, out_grad, gain)


def attend_kernel(count, assignment, tiles, owners, *refs):
    key_parts, value_parts = refs[:count], refs[count : 2 * count]
    normed, masked, gain = refs[2 * count : 2 * count + 3]
    rows_out, score_out, picked = refs[2 * count + 3 : 2 * count + 6]
    key_pre, key_normed, values, key_sum, value_sum = refs[2 * count + 6 :]
    img_count, own_rows, head_dim = key_parts[0].shape[1:]
    parts = rows_out.shape[0]
    img_rows = parts * own_rows
    group, step = pl.program_id(0), pl.program_id(1)
    inv_root = 1.0 / math.sqrt(head_dim)

    @pl.when(step == 0)
    def _():
        for i in range(img_count):
            keys, upper = [
                jnp.concatenate(
                    [source[:, i].reshape(-1, head_dim) for source in sources], axis=0
                )
                for sources in (key_parts, value_parts)
            ]
            key_pre[i] = keys
            key_normed[i] = (keys * rms_scale(keys) * gain[...]).astype(jnp.bfloat16)
            values[i] = upper.astype(jnp.bfloat16)
        key_sum[...] = jnp.zeros_like(key_sum)
        value_sum[...] = jnp.zeros_like(value_sum)

    image = assignment[step]
    keys = key_normed[image]
    picked[0, 0] = keys
    column = lax.broadcasted_iota(jnp.int32, (1, img_rows), 1)
    place = jnp.zeros_like(column)
    for k in range(parts):
        inside = (column >= k * own_rows) & (column < (k + 1) * own_rows)
        place = jnp.where(inside, column + (owners[k] - k) * own_rows, place)
    live = (place < tiles[image] * TILE_ROWS).astype(jnp.float32)
    queries = normed[0, 0]
    upstream = masked[0, 0]
    raised = jnp.exp(dot(queries, keys, 1, 1) * inv_root) * live
    prob = raised * (1.0 / jnp.sum(raised, axis=-1, keepdims=True))
    prob_grad = dot(upstream, values[image], 1, 1)
    inner = jnp.sum(prob * prob_grad, axis=-1, keepdims=True)
    score_grad = (prob * (prob_grad - inner)).astype(jnp.bfloat16)
    score_out[0, 0] = score_grad
    value_sum[image] += dot(prob.astype(jnp.bfloat16), upstream, 0, 0)
    key_sum[image] += dot(score_grad, queries, 0, 0) * inv_root

    @pl.when(step == pl.num_programs(1) - 1)
    def _():
        shape = (parts, own_rows, head_dim)
        key_cols = pl.ds(pl.multiple_of(group * head_dim, head_dim), head_dim)
        value_cols = pl.ds(
            pl.multiple_of((pl.num_programs(0) + group) * head_dim, head_dim), head_dim
        )
        for i in range(img_count):
            source = key_pre[i]
            key_rows = rms_back(source, rms_scale(source), gain[...], key_sum[i])
            rows_out[:, i, :, key_cols] = key_rows.astype(jnp.bfloat16).reshape(shape)
            rows_out[:, i, :, value_cols] = value_sum[i].astype(jnp.bfloat16).reshape(shape)


def attend(pieces, normed, masked, gain, assignment, tiles, owners):
    seq_count, groups, stacked, head_dim = normed.shape
    img_count, own_rows, columns = pieces[0].shape[1:]
    parts = sum(piece.shape[0] for piece in pieces)
    img_rows = parts * own_rows
    shapes = [(piece.shape[0], img_count, own_rows, head_dim) for piece in pieces]
    keys = [pl.BlockSpec(shape, lambda g, b, *_: (0, 0, 0, g)) for shape in shapes]
    values = [pl.BlockSpec(shape, lambda g, b, *_: (0, 0, 0, groups + g)) for shape in shapes]
    stack = pl.BlockSpec((1, 1, stacked, head_dim), lambda g, b, *_: (b, g, 0, 0))
    rows = (parts, img_count, own_rows, columns)
    return pl.pallas_call(
        functools.partial(attend_kernel, len(pieces)),
        out_shape=(
            jax.ShapeDtypeStruct(rows, jnp.bfloat16),
            jax.ShapeDtypeStruct((seq_count, groups, stacked, img_rows), jnp.bfloat16),
            jax.ShapeDtypeStruct((seq_count, groups, img_rows, head_dim), jnp.bfloat16),
        ),
        grid_spec=pltpu.PrefetchScalarGridSpec(
            num_scalar_prefetch=3,
            grid=(groups, seq_count),
            in_specs=keys
            + values
            + [stack, stack, pl.BlockSpec((1, head_dim), lambda *_: (0, 0))],
            out_specs=(
                pl.BlockSpec(rows, lambda *_: (0, 0, 0, 0)),
                pl.BlockSpec((1, 1, stacked, img_rows), lambda g, b, *_: (b, g, 0, 0)),
                pl.BlockSpec((1, 1, img_rows, head_dim), lambda g, b, *_: (b, g, 0, 0)),
            ),
            scratch_shapes=[
                pltpu.VMEM((img_count, img_rows, head_dim), jnp.float32),
                pltpu.VMEM((img_count, img_rows, head_dim), jnp.bfloat16),
                pltpu.VMEM((img_count, img_rows, head_dim), jnp.bfloat16),
                pltpu.VMEM((img_count, img_rows, head_dim), jnp.float32),
                pltpu.VMEM((img_count, img_rows, head_dim), jnp.float32),
            ],
        ),
        compiler_params=pltpu.CompilerParams(vmem_limit_bytes=32 * 1024 * 1024),
        name="attend",
    )(assignment, tiles, owners, *pieces, *pieces, normed, masked, gain)


def after_kernel(query, score_grad, keys, gain, target):
    text_len, columns = query.shape[1:]
    head_dim = gain.shape[1]
    inv_root = 1.0 / math.sqrt(head_dim)
    for j in range(columns // head_dim):
        head = pl.ds(j * head_dim, head_dim)
        source = query[0, :, head].astype(jnp.float32)
        part = dot(score_grad[0, 0, pl.ds(j * text_len, text_len), :], keys[0, 0], 1, 0)
        grad = rms_back(source, rms_scale(source), gain[...], part * inv_root)
        target[0, :, head] = grad.astype(jnp.bfloat16)


def after(queries, score_grad, keys, gain):
    seq_count, text_len, columns = queries.shape
    groups, stacked, img_rows = score_grad.shape[1:]
    head_dim = gain.shape[1]
    source = pl.BlockSpec((1, text_len, columns // groups), lambda b, g: (b, 0, g))
    return pl.pallas_call(
        after_kernel,
        out_shape=jax.ShapeDtypeStruct(queries.shape, jnp.bfloat16),
        grid=(seq_count, groups),
        in_specs=[
            source,
            pl.BlockSpec((1, 1, stacked, img_rows), lambda b, g: (b, g, 0, 0)),
            pl.BlockSpec((1, 1, img_rows, head_dim), lambda b, g: (b, g, 0, 0)),
            pl.BlockSpec((1, head_dim), lambda *_: (0, 0)),
        ],
        out_specs=source,
        name="after",
    )(queries, score_grad, keys, gain)


def terms_kernel(splits, rows, weight, *outs):
    parts, img_count, own_rows, cols = rows.shape
    term = dot(rows[...].reshape(-1, cols), weight[...], 1, 1).astype(jnp.bfloat16)
    term = term.reshape(parts, img_count, own_rows, -1)
    for (part, low, high), out in zip(splits, outs):
        out[...] = term[part, low:high]


def terms(rows, weight, splits, chunks):
    parts, img_count, own_rows, cols = rows.shape
    vis_width = weight.shape[0]
    width = vis_width // chunks
    counts = [high - low for _, low, high in splits]
    return pl.pallas_call(
        functools.partial(terms_kernel, splits),
        out_shape=[
            jax.ShapeDtypeStruct((count, own_rows, vis_width), jnp.bfloat16) for count in counts
        ],
        grid=(chunks,),
        in_specs=[
            pl.BlockSpec(rows.shape, lambda c: (0, 0, 0, 0)),
            pl.BlockSpec((width, cols), lambda c: (c, 0)),
        ],
        out_specs=[
            pl.BlockSpec((count, own_rows, width), lambda c: (0, 0, c)) for count in counts
        ],
        compiler_params=pltpu.CompilerParams(vmem_limit_bytes=32 * 1024 * 1024),
        name="terms",
    )(rows, weight)


def weights_kernel(place, near, far, rows, own, mate, total):
    low, width = near.shape[0], own.shape[1]
    total[...] = dot(near[...], rows[:low], 0, 0) + dot(far[...], rows[low:], 0, 0)
    core = place[0]
    own[0] = total[pl.ds(pl.multiple_of(core * width, width), width)].astype(own.dtype)
    mate[0] = total[pl.ds(pl.multiple_of((1 - core) * width, width), width)].astype(mate.dtype)


def weights(near, far, rows, place, pairs):
    vis_width, cols = near.shape[1], rows.shape[1]
    width = vis_width // pairs
    shape = jax.ShapeDtypeStruct((pairs, width // 2, cols), jnp.bfloat16)
    target = pl.BlockSpec((1, width // 2, cols), lambda p, *_: (p, 0, 0))
    return pl.pallas_call(
        weights_kernel,
        out_shape=(shape, shape),
        grid_spec=pltpu.PrefetchScalarGridSpec(
            num_scalar_prefetch=1,
            grid=(pairs,),
            in_specs=[
                pl.BlockSpec((near.shape[0], width), lambda p, *_: (0, p)),
                pl.BlockSpec((far.shape[0], width), lambda p, *_: (0, p)),
                pl.BlockSpec(rows.shape, lambda *_: (0, 0)),
            ],
            out_specs=(target, target),
            scratch_shapes=[pltpu.VMEM((width, cols), jnp.float32)],
        ),
        compiler_params=pltpu.CompilerParams(vmem_limit_bytes=32 * 1024 * 1024),
        name="weights",
    )(place, near, far, rows)


def merge_kernel(place, held, given, out):
    out[...] = (held[...].astype(jnp.float32) + given[...].astype(jnp.float32)).astype(out.dtype)


def merge(held, given, place):
    pairs, own_width, cols = held.shape
    return [
        pl.pallas_call(
            merge_kernel,
            out_shape=jax.ShapeDtypeStruct((1, own_width, cols), kind),
            grid_spec=pltpu.PrefetchScalarGridSpec(
                num_scalar_prefetch=1,
                grid=(1,),
                in_specs=[
                    pl.BlockSpec(
                        (1, own_width, cols),
                        lambda i, place, r=r: (jnp.bitwise_xor(place[1], r), 0, 0),
                    )
                ]
                * 2,
                out_specs=pl.BlockSpec((1, own_width, cols), lambda *_: (0, 0, 0)),
            ),
            compiler_params=pltpu.CompilerParams(vmem_limit_bytes=32 * 1024 * 1024),
            name="merge",
        )(place, held, given)[0]
        for r, kind in enumerate([jnp.float32] + [jnp.bfloat16] * (pairs - 1))
    ]


def per_device(
    dp_size,
    mp_size,
    queries,
    out_grad,
    images,
    key_weight,
    value_weight,
    query_gain,
    key_gain,
    assignment,
    tile_counts,
    lengths,
):
    img_count, own_rows, vis_width = images.shape
    head_dim = query_gain.shape[0]
    own_width, key_cols = key_weight.shape
    key_heads = key_cols // head_dim
    cols = 2 * key_cols
    pairs = dp_size // 2
    place = lax.axis_index("dp")
    pair, core = place // 2, place % 2
    line = lax.axis_index("mp")
    first = img_count // 2

    def ring(value, step):
        return lax.ppermute(value, "mp", [(i, (i + step) % mp_size) for i in range(mp_size)])

    def swap(value, mask):
        return lax.ppermute(value, "dp", [(i, i ^ mask) for i in range(dp_size)])

    from_left, from_right = ring(images, 1), ring(images, -1)
    query_gain, key_gain = query_gain[None, :], key_gain[None, :]
    normed, masked = before(queries, out_grad, query_gain, lengths, key_heads)

    own_weight = jnp.concatenate((key_weight, value_weight), axis=1)
    leaving = (from_left[:first], from_right[first:])
    if pairs != 4:
        weight = lax.all_gather(own_weight, "dp", axis=0, tiled=True)
        opposite = (ring(leaving[0], 1), ring(leaving[1], -1))
    else:
        side, up, across = (swap(own_weight, 2 * r) for r in range(1, pairs))
        twice = jnp.stack((own_weight, side))
        weight = jnp.zeros((2 * pairs, own_width, cols), jnp.bfloat16)
        leaving, twice, up, across, normed, masked, weight = lax.optimization_barrier(
            (leaving, twice, up, across, normed, masked, weight)
        )
        opposite = (ring(leaving[0], 1), ring(leaving[1], -1))
        for r, pieces in ((0, twice), (2, up[None]), (3, across[None])):
            mates = swap(pieces, 1)
            for k in range(pieces.shape[0]):
                for source, half in ((pieces, core), (mates, 1 - core)):
                    weight = lax.dynamic_update_slice_in_dim(
                        weight, source[k : k + 1], 2 * (pair ^ (r + k)) + half, axis=0
                    )
        weight = weight.reshape(vis_width, cols)

    near = jnp.stack((images, from_left, from_right)).reshape(-1, vis_width)
    near_total = dot(near, weight, 1, 0)
    near_total, opposite = lax.optimization_barrier((near_total, opposite))
    near_total = near_total.reshape(3, img_count, own_rows, cols)
    far = jnp.concatenate(opposite).reshape(-1, vis_width)
    far_total = dot(far, weight, 1, 0).reshape(1, img_count, own_rows, cols)
    owners = (line + jnp.array((0, -1, 1, 2), jnp.int32)) % mp_size
    rows, score_grad, seq_keys = attend(
        [near_total, far_total], normed, masked, key_gain, assignment, tile_counts, owners
    )
    halves = ((0, 0, first), (0, first, img_count))
    leaving_right, leaving_left = terms(rows[3:], weight, halves, 4)
    wholes = tuple((part, 0, img_count) for part in range(3))
    own, to_left, to_right = terms(rows[:3], weight, wholes, 4)

    all_rows = rows.reshape(-1, cols)
    if pairs != 4:
        weight_part = dot(jnp.concatenate((near, far)), all_rows, 0, 0)
        weight_grad = lax.psum_scatter(weight_part, "dp", scatter_dimension=0, tiled=True)
    else:
        where = jnp.stack((core, pair))
        all_rows, leaving_right, leaving_left = lax.optimization_barrier(
            (all_rows, leaving_right, leaving_left)
        )
        kept, given = weights(near, far, all_rows, where, pairs)
        sent = merge(kept, swap(given, 1), where)
        score_grad, sent = lax.optimization_barrier((score_grad, sent))
        weight_grad = sent[0]
        for r in range(1, pairs):
            weight_grad = weight_grad + swap(sent[r], 2 * r).astype(jnp.float32)
    query_grad = after(queries, score_grad, seq_keys, query_gain)

    right_half, left_half = lax.optimization_barrier(
        (ring(leaving_right, 1), ring(leaving_left, -1))
    )

    def added(held, half):
        return (held.astype(jnp.float32) + half.astype(jnp.float32)).astype(jnp.bfloat16)

    to_right = jnp.concatenate((added(to_right[:first], right_half), to_right[first:]))
    to_left = jnp.concatenate((to_left[:first], added(to_left[first:], left_half)))
    to_right, to_left = lax.optimization_barrier((to_right, to_left))
    from_left, from_right = ring(to_right, 1), ring(to_left, -1)
    from_left, from_right, weight_grad, query_grad = lax.optimization_barrier(
        (from_left, from_right, weight_grad, query_grad)
    )
    image_grad = (
        own.astype(jnp.float32) + from_left.astype(jnp.float32) + from_right.astype(jnp.float32)
    ).astype(jnp.bfloat16)
    return (query_grad, image_grad, weight_grad[:, :key_cols], weight_grad[:, key_cols:])


def solution(mesh):
    placed = (
        P("dp", None, "mp"),
        P("dp", None, "mp"),
        P("dp", "mp", None),
        P("dp", "mp"),
        P("dp", "mp"),
        P(),
        P(),
        P("dp"),
        P("dp"),
        P("dp"),
    )

    def body(*args):
        return per_device(mesh.shape["dp"], mesh.shape["mp"], *args)

    return jax.shard_map(
        body,
        mesh=mesh,
        in_specs=placed,
        out_specs=(P("dp", None, "mp"), P("dp", "mp", None), P("dp", "mp"), P("dp", "mp")),
        check_vma=False,
    )
```

```python
import functools
import math

import jax
import jax.numpy as jnp
from jax import lax
from jax.experimental import pallas as pl
from jax.experimental.pallas import tpu as pltpu
from jax.sharding import PartitionSpec as P

TILE_ROWS = 32


EPSILON = 1e-05


def rms_scale(source):
    return lax.rsqrt(jnp.mean(source * source, axis=-1, keepdims=True) + EPSILON)


def rms_back(source, factor, gain_vector, upstream):
    weighted = gain_vector * upstream
    return factor * weighted - source * (factor * factor * factor) * jnp.mean(
        source * weighted, axis=-1, keepdims=True
    )


def dot(left, right, left_dim, right_dim):
    return lax.dot_general(
        left,
        right,
        (((left_dim,), (right_dim,)), ((), ())),
        preferred_element_type=jnp.float32,
    )


def before_kernel(lengths, query, grad, gain, normed, masked):
    text_len, columns = query.shape[1:]
    head_dim = gain.shape[1]
    live = lax.broadcasted_iota(jnp.int32, (text_len, head_dim), 0) < lengths[pl.program_id(0)]
    for j in range(columns // head_dim):
        head = pl.ds(j * head_dim, head_dim)
        rows = pl.ds(j * text_len, text_len)
        source = query[0, :, head].astype(jnp.float32)
        normed[0, 0, rows, :] = (source * rms_scale(source) * gain[...]).astype(jnp.bfloat16)
        upstream = grad[0, :, head]
        masked[0, 0, rows, :] = jnp.where(live, upstream, jnp.zeros_like(upstream))


def before(queries, out_grad, gain, lengths, groups):
    seq_count, text_len, columns = queries.shape
    head_dim = gain.shape[1]
    span = columns // groups
    stacked = span // head_dim * text_len
    source = pl.BlockSpec((1, text_len, span), lambda b, g, *_: (b, 0, g))
    target = pl.BlockSpec((1, 1, stacked, head_dim), lambda b, g, *_: (b, g, 0, 0))
    shape = jax.ShapeDtypeStruct((seq_count, groups, stacked, head_dim), jnp.bfloat16)
    return pl.pallas_call(
        before_kernel,
        out_shape=(shape, shape),
        grid_spec=pltpu.PrefetchScalarGridSpec(
            num_scalar_prefetch=1,
            grid=(seq_count, groups),
            in_specs=[source, source, pl.BlockSpec((1, head_dim), lambda *_: (0, 0))],
            out_specs=(target, target),
        ),
        name="before",
    )(lengths, queries, out_grad, gain)


def attend_kernel(count, assignment, tiles, owners, *refs):
    key_parts, value_parts = refs[:count], refs[count : 2 * count]
    normed, masked, gain = refs[2 * count : 2 * count + 3]
    rows_out, score_out, picked = refs[2 * count + 3 : 2 * count + 6]
    key_pre, key_normed, values, key_sum, value_sum = refs[2 * count + 6 :]
    img_count, own_rows, head_dim = key_parts[0].shape[1:]
    parts = rows_out.shape[0]
    img_rows = parts * own_rows
    group, step = pl.program_id(0), pl.program_id(1)
    inv_root = 1.0 / math.sqrt(head_dim)

    @pl.when(step == 0)
    def _():
        for i in range(img_count):
            keys, upper = [
                jnp.concatenate(
                    [source[:, i].reshape(-1, head_dim) for source in sources], axis=0
                )
                for sources in (key_parts, value_parts)
            ]
            key_pre[i] = keys
            key_normed[i] = (keys * rms_scale(keys) * gain[...]).astype(jnp.bfloat16)
            values[i] = upper.astype(jnp.bfloat16)
        key_sum[...] = jnp.zeros_like(key_sum)
        value_sum[...] = jnp.zeros_like(value_sum)

    image = assignment[step]
    keys = key_normed[image]
    picked[0, 0] = keys
    column = lax.broadcasted_iota(jnp.int32, (1, img_rows), 1)
    place = jnp.zeros_like(column)
    for k in range(parts):
        inside = (column >= k * own_rows) & (column < (k + 1) * own_rows)
        place = jnp.where(inside, column + (owners[k] - k) * own_rows, place)
    live = (place < tiles[image] * TILE_ROWS).astype(jnp.float32)
    queries = normed[0, 0]
    upstream = masked[0, 0]
    raised = jnp.exp(dot(queries, keys, 1, 1) * inv_root) * live
    prob = raised * (1.0 / jnp.sum(raised, axis=-1, keepdims=True))
    prob_grad = dot(upstream, values[image], 1, 1)
    inner = jnp.sum(prob * prob_grad, axis=-1, keepdims=True)
    score_grad = (prob * (prob_grad - inner)).astype(jnp.bfloat16)
    score_out[0, 0] = score_grad
    value_sum[image] += dot(prob.astype(jnp.bfloat16), upstream, 0, 0)
    key_sum[image] += dot(score_grad, queries, 0, 0) * inv_root

    @pl.when(step == pl.num_programs(1) - 1)
    def _():
        shape = (parts, own_rows, head_dim)
        key_cols = pl.ds(pl.multiple_of(group * head_dim, head_dim), head_dim)
        value_cols = pl.ds(
            pl.multiple_of((pl.num_programs(0) + group) * head_dim, head_dim), head_dim
        )
        for i in range(img_count):
            source = key_pre[i]
            key_rows = rms_back(source, rms_scale(source), gain[...], key_sum[i])
            rows_out[:, i, :, key_cols] = key_rows.astype(jnp.bfloat16).reshape(shape)
            rows_out[:, i, :, value_cols] = value_sum[i].astype(jnp.bfloat16).reshape(shape)


def attend(pieces, normed, masked, gain, assignment, tiles, owners):
    seq_count, groups, stacked, head_dim = normed.shape
    img_count, own_rows, columns = pieces[0].shape[1:]
    parts = sum(piece.shape[0] for piece in pieces)
    img_rows = parts * own_rows
    shapes = [(piece.shape[0], img_count, own_rows, head_dim) for piece in pieces]
    keys = [pl.BlockSpec(shape, lambda g, b, *_: (0, 0, 0, g)) for shape in shapes]
    values = [pl.BlockSpec(shape, lambda g, b, *_: (0, 0, 0, groups + g)) for shape in shapes]
    stack = pl.BlockSpec((1, 1, stacked, head_dim), lambda g, b, *_: (b, g, 0, 0))
    rows = (parts, img_count, own_rows, columns)
    return pl.pallas_call(
        functools.partial(attend_kernel, len(pieces)),
        out_shape=(
            jax.ShapeDtypeStruct(rows, jnp.bfloat16),
            jax.ShapeDtypeStruct((seq_count, groups, stacked, img_rows), jnp.bfloat16),
            jax.ShapeDtypeStruct((seq_count, groups, img_rows, head_dim), jnp.bfloat16),
        ),
        grid_spec=pltpu.PrefetchScalarGridSpec(
            num_scalar_prefetch=3,
            grid=(groups, seq_count),
            in_specs=keys
            + values
            + [stack, stack, pl.BlockSpec((1, head_dim), lambda *_: (0, 0))],
            out_specs=(
                pl.BlockSpec(rows, lambda *_: (0, 0, 0, 0)),
                pl.BlockSpec((1, 1, stacked, img_rows), lambda g, b, *_: (b, g, 0, 0)),
                pl.BlockSpec((1, 1, img_rows, head_dim), lambda g, b, *_: (b, g, 0, 0)),
            ),
            scratch_shapes=[
                pltpu.VMEM((img_count, img_rows, head_dim), jnp.float32),
                pltpu.VMEM((img_count, img_rows, head_dim), jnp.bfloat16),
                pltpu.VMEM((img_count, img_rows, head_dim), jnp.bfloat16),
                pltpu.VMEM((img_count, img_rows, head_dim), jnp.float32),
                pltpu.VMEM((img_count, img_rows, head_dim), jnp.float32),
            ],
        ),
        compiler_params=pltpu.CompilerParams(vmem_limit_bytes=32 * 1024 * 1024),
        name="attend",
    )(assignment, tiles, owners, *pieces, *pieces, normed, masked, gain)


def after_kernel(query, score_grad, keys, gain, target):
    text_len, columns = query.shape[1:]
    head_dim = gain.shape[1]
    inv_root = 1.0 / math.sqrt(head_dim)
    for j in range(columns // head_dim):
        head = pl.ds(j * head_dim, head_dim)
        source = query[0, :, head].astype(jnp.float32)
        part = dot(score_grad[0, 0, pl.ds(j * text_len, text_len), :], keys[0, 0], 1, 0)
        grad = rms_back(source, rms_scale(source), gain[...], part * inv_root)
        target[0, :, head] = grad.astype(jnp.bfloat16)


def after(queries, score_grad, keys, gain):
    seq_count, text_len, columns = queries.shape
    groups, stacked, img_rows = score_grad.shape[1:]
    head_dim = gain.shape[1]
    source = pl.BlockSpec((1, text_len, columns // groups), lambda b, g: (b, 0, g))
    return pl.pallas_call(
        after_kernel,
        out_shape=jax.ShapeDtypeStruct(queries.shape, jnp.bfloat16),
        grid=(seq_count, groups),
        in_specs=[
            source,
            pl.BlockSpec((1, 1, stacked, img_rows), lambda b, g: (b, g, 0, 0)),
            pl.BlockSpec((1, 1, img_rows, head_dim), lambda b, g: (b, g, 0, 0)),
            pl.BlockSpec((1, head_dim), lambda *_: (0, 0)),
        ],
        out_specs=source,
        name="after",
    )(queries, score_grad, keys, gain)


def beside_kernel(left, right, out):
    cut = left.shape[1]
    out[:, :cut] = left[...]
    out[:, cut:] = right[...]


def beside(left, right):
    rows, columns = left.shape
    return pl.pallas_call(
        beside_kernel,
        out_shape=jax.ShapeDtypeStruct((rows, 2 * columns), left.dtype),
        name="beside",
    )(left, right)


def terms_kernel(splits, rows, weight, *outs):
    parts, img_count, own_rows, cols = rows.shape
    term = dot(rows[...].reshape(-1, cols), weight[...], 1, 1).astype(jnp.bfloat16)
    term = term.reshape(parts, img_count, own_rows, -1)
    for (part, low, high), out in zip(splits, outs):
        out[...] = term[part, low:high]


def terms(rows, weight, splits, chunks):
    parts, img_count, own_rows, cols = rows.shape
    vis_width = weight.shape[0]
    width = vis_width // chunks
    counts = [high - low for _, low, high in splits]
    return pl.pallas_call(
        functools.partial(terms_kernel, splits),
        out_shape=[
            jax.ShapeDtypeStruct((count, own_rows, vis_width), jnp.bfloat16) for count in counts
        ],
        grid=(chunks,),
        in_specs=[
            pl.BlockSpec(rows.shape, lambda c: (0, 0, 0, 0)),
            pl.BlockSpec((width, cols), lambda c: (c, 0)),
        ],
        out_specs=[
            pl.BlockSpec((count, own_rows, width), lambda c: (0, 0, c)) for count in counts
        ],
        compiler_params=pltpu.CompilerParams(vmem_limit_bytes=32 * 1024 * 1024),
        name="terms",
    )(rows, weight)


def merge_kernel(place, held, given, out):
    out[0] = (held[0, 0].astype(jnp.float32) + given[0].astype(jnp.float32)).astype(out.dtype)


def merge(held, given, place):
    pairs, _, own_width, cols = held.shape
    return [
        pl.pallas_call(
            merge_kernel,
            out_shape=jax.ShapeDtypeStruct((1, own_width, cols), kind),
            grid_spec=pltpu.PrefetchScalarGridSpec(
                num_scalar_prefetch=1,
                grid=(1,),
                in_specs=[
                    pl.BlockSpec(
                        (1, 1, own_width, cols),
                        lambda i, place, r=r: (jnp.bitwise_xor(place[1], r), place[0], 0, 0),
                    ),
                    pl.BlockSpec(
                        (1, own_width, cols),
                        lambda i, place, r=r: (jnp.bitwise_xor(place[1], r), 0, 0),
                    ),
                ],
                out_specs=pl.BlockSpec((1, own_width, cols), lambda *_: (0, 0, 0)),
            ),
            compiler_params=pltpu.CompilerParams(vmem_limit_bytes=32 * 1024 * 1024),
            name="merge",
        )(place, held, given)[0]
        for r, kind in enumerate([jnp.float32] + [jnp.bfloat16] * (pairs - 1))
    ]


def per_device(
    dp_size,
    mp_size,
    queries,
    out_grad,
    images,
    key_weight,
    value_weight,
    query_gain,
    key_gain,
    assignment,
    tile_counts,
    lengths,
):
    img_count, own_rows, vis_width = images.shape
    head_dim = query_gain.shape[0]
    own_width, key_cols = key_weight.shape
    key_heads = key_cols // head_dim
    cols = 2 * key_cols
    pairs = dp_size // 2
    place = lax.axis_index("dp")
    pair, core = place // 2, place % 2
    line = lax.axis_index("mp")
    first = img_count // 2

    def ring(value, step):
        return lax.ppermute(value, "mp", [(i, (i + step) % mp_size) for i in range(mp_size)])

    def swap(value, mask):
        return lax.ppermute(value, "dp", [(i, i ^ mask) for i in range(dp_size)])

    from_left, from_right = ring(images, 1), ring(images, -1)
    query_gain, key_gain = query_gain[None, :], key_gain[None, :]
    normed, masked = before(queries, out_grad, query_gain, lengths, key_heads)

    own_weight = beside(key_weight, value_weight)
    leaving = (from_left[:first], from_right[first:])
    if pairs != 4:
        weight = lax.all_gather(own_weight, "dp", axis=0, tiled=True)
        opposite = (ring(leaving[0], 1), ring(leaving[1], -1))
    else:
        side, up, across = (swap(own_weight, 2 * r) for r in range(1, pairs))
        twice = jnp.stack((own_weight, side))
        weight = jnp.zeros((2 * pairs, own_width, cols), jnp.bfloat16)
        leaving, twice, up, across, normed, masked, weight = lax.optimization_barrier(
            (leaving, twice, up, across, normed, masked, weight)
        )
        opposite = (ring(leaving[0], 1), ring(leaving[1], -1))
        for r, pieces in ((0, twice), (2, up[None]), (3, across[None])):
            mates = swap(pieces, 1)
            for k in range(pieces.shape[0]):
                for source, half in ((pieces, core), (mates, 1 - core)):
                    weight = lax.dynamic_update_slice_in_dim(
                        weight, source[k : k + 1], 2 * (pair ^ (r + k)) + half, axis=0
                    )
        weight = weight.reshape(vis_width, cols)

    near = jnp.stack((images, from_left, from_right)).reshape(-1, vis_width)
    near_total = dot(near, weight, 1, 0)
    near_total, opposite = lax.optimization_barrier((near_total, opposite))
    near_total = near_total.reshape(3, img_count, own_rows, cols)
    far = jnp.concatenate(opposite).reshape(-1, vis_width)
    far_total = dot(far, weight, 1, 0).reshape(1, img_count, own_rows, cols)
    owners = (line + jnp.array((0, -1, 1, 2), jnp.int32)) % mp_size
    rows, score_grad, seq_keys = attend(
        [near_total, far_total], normed, masked, key_gain, assignment, tile_counts, owners
    )
    halves = ((0, 0, first), (0, first, img_count))
    leaving_right, leaving_left = terms(rows[3:], weight, halves, 4)
    wholes = tuple((part, 0, img_count) for part in range(3))
    own, to_left, to_right = terms(rows[:3], weight, wholes, 4)

    right_half, left_half = lax.optimization_barrier(
        (ring(leaving_right, 1), ring(leaving_left, -1))
    )

    def added(held, half):
        return (held.astype(jnp.float32) + half.astype(jnp.float32)).astype(jnp.bfloat16)

    to_right = jnp.concatenate((added(to_right[:first], right_half), to_right[first:]))
    to_left = jnp.concatenate((to_left[:first], added(to_left[first:], left_half)))
    to_right, to_left = lax.optimization_barrier((to_right, to_left))
    from_left, from_right = ring(to_right, 1), ring(to_left, -1)
    image_grad = (
        own.astype(jnp.float32) + from_left.astype(jnp.float32) + from_right.astype(jnp.float32)
    ).astype(jnp.bfloat16)

    weight_part = dot(jnp.concatenate((near, far)), rows.reshape(-1, cols), 0, 0)
    if pairs != 4:
        weight_grad = lax.psum_scatter(weight_part, "dp", scatter_dimension=0, tiled=True)
    else:
        weight_part = weight_part.astype(jnp.bfloat16).reshape(pairs, 2, own_width, cols)
        given = swap(lax.dynamic_index_in_dim(weight_part, 1 - core, 1, keepdims=False), 1)
        given, to_right, to_left = lax.optimization_barrier((given, to_right, to_left))
        weight_grad, *sent = merge(weight_part, given, jnp.stack((core, pair)))
        score_grad, sent = lax.optimization_barrier((score_grad, sent))
        sent = [swap(piece, 2 * r) for r, piece in enumerate(sent, 1)]
        image_grad, sent = lax.optimization_barrier((image_grad, sent))
        for piece in sent:
            weight_grad = weight_grad + piece.astype(jnp.float32)
    query_grad = after(queries, score_grad, seq_keys, query_gain)
    return (query_grad, image_grad, weight_grad[:, :key_cols], weight_grad[:, key_cols:])


def solution(mesh):
    placed = (
        P("dp", None, "mp"),
        P("dp", None, "mp"),
        P("dp", "mp", None),
        P("dp", "mp"),
        P("dp", "mp"),
        P(),
        P(),
        P("dp"),
        P("dp"),
        P("dp"),
    )

    def body(*args):
        return per_device(mesh.shape["dp"], mesh.shape["mp"], *args)

    return jax.shard_map(
        body,
        mesh=mesh,
        in_specs=placed,
        out_specs=(P("dp", None, "mp"), P("dp", "mp", None), P("dp", "mp"), P("dp", "mp")),
        check_vma=False,
    )
```

```python
import functools
import math

import jax
import jax.numpy as jnp
from jax import lax
from jax.experimental import pallas as pl
from jax.experimental.pallas import tpu as pltpu
from jax.sharding import PartitionSpec as P

TILE_ROWS = 32


EPSILON = 1e-05


def rms_scale(source):
    return lax.rsqrt(jnp.mean(source * source, axis=-1, keepdims=True) + EPSILON)


def rms_back(source, factor, gain_vector, upstream):
    weighted = gain_vector * upstream
    return factor * weighted - source * (factor * factor * factor) * jnp.mean(
        source * weighted, axis=-1, keepdims=True
    )


def dot(left, right, left_dim, right_dim):
    return lax.dot_general(
        left,
        right,
        (((left_dim,), (right_dim,)), ((), ())),
        preferred_element_type=jnp.float32,
    )


def before_kernel(lengths, query, grad, gain, normed, masked):
    text_len, columns = query.shape[1:]
    head_dim = gain.shape[1]
    live = lax.broadcasted_iota(jnp.int32, (text_len, head_dim), 0) < lengths[pl.program_id(0)]
    for j in range(columns // head_dim):
        head = pl.ds(j * head_dim, head_dim)
        rows = pl.ds(j * text_len, text_len)
        source = query[0, :, head].astype(jnp.float32)
        normed[0, 0, rows, :] = (source * rms_scale(source) * gain[...]).astype(jnp.bfloat16)
        upstream = grad[0, :, head]
        masked[0, 0, rows, :] = jnp.where(live, upstream, jnp.zeros_like(upstream))


def before(queries, out_grad, gain, lengths, groups):
    seq_count, text_len, columns = queries.shape
    head_dim = gain.shape[1]
    span = columns // groups
    stacked = span // head_dim * text_len
    source = pl.BlockSpec((1, text_len, span), lambda b, g, *_: (b, 0, g))
    target = pl.BlockSpec((1, 1, stacked, head_dim), lambda b, g, *_: (b, g, 0, 0))
    shape = jax.ShapeDtypeStruct((seq_count, groups, stacked, head_dim), jnp.bfloat16)
    return pl.pallas_call(
        before_kernel,
        out_shape=(shape, shape),
        grid_spec=pltpu.PrefetchScalarGridSpec(
            num_scalar_prefetch=1,
            grid=(seq_count, groups),
            in_specs=[source, source, pl.BlockSpec((1, head_dim), lambda *_: (0, 0))],
            out_specs=(target, target),
        ),
        name="before",
    )(lengths, queries, out_grad, gain)


def attend_kernel(count, assignment, tiles, owners, *refs):
    key_parts, value_parts = refs[:count], refs[count : 2 * count]
    normed, masked, gain = refs[2 * count : 2 * count + 3]
    rows_out, score_out, picked = refs[2 * count + 3 : 2 * count + 6]
    key_pre, key_normed, values, key_sum, value_sum = refs[2 * count + 6 :]
    img_count, own_rows, head_dim = key_parts[0].shape[1:]
    parts = rows_out.shape[0]
    img_rows = parts * own_rows
    group, step = pl.program_id(0), pl.program_id(1)
    inv_root = 1.0 / math.sqrt(head_dim)

    @pl.when(step == 0)
    def _():
        for i in range(img_count):
            keys, upper = [
                jnp.concatenate(
                    [source[:, i].reshape(-1, head_dim) for source in sources], axis=0
                )
                for sources in (key_parts, value_parts)
            ]
            key_pre[i] = keys
            key_normed[i] = (keys * rms_scale(keys) * gain[...]).astype(jnp.bfloat16)
            values[i] = upper.astype(jnp.bfloat16)
        key_sum[...] = jnp.zeros_like(key_sum)
        value_sum[...] = jnp.zeros_like(value_sum)

    image = assignment[step]
    keys = key_normed[image]
    picked[0, 0] = keys
    column = lax.broadcasted_iota(jnp.int32, (1, img_rows), 1)
    place = jnp.zeros_like(column)
    for k in range(parts):
        inside = (column >= k * own_rows) & (column < (k + 1) * own_rows)
        place = jnp.where(inside, column + (owners[k] - k) * own_rows, place)
    live = (place < tiles[image] * TILE_ROWS).astype(jnp.float32)
    queries = normed[0, 0]
    upstream = masked[0, 0]
    raised = jnp.exp(dot(queries, keys, 1, 1) * inv_root) * live
    prob = raised * (1.0 / jnp.sum(raised, axis=-1, keepdims=True))
    prob_grad = dot(upstream, values[image], 1, 1)
    inner = jnp.sum(prob * prob_grad, axis=-1, keepdims=True)
    score_grad = (prob * (prob_grad - inner)).astype(jnp.bfloat16)
    score_out[0, 0] = score_grad
    value_sum[image] += dot(prob.astype(jnp.bfloat16), upstream, 0, 0)
    key_sum[image] += dot(score_grad, queries, 0, 0) * inv_root

    @pl.when(step == pl.num_programs(1) - 1)
    def _():
        shape = (parts, own_rows, head_dim)
        key_cols = pl.ds(pl.multiple_of(group * head_dim, head_dim), head_dim)
        value_cols = pl.ds(
            pl.multiple_of((pl.num_programs(0) + group) * head_dim, head_dim), head_dim
        )
        for i in range(img_count):
            source = key_pre[i]
            key_rows = rms_back(source, rms_scale(source), gain[...], key_sum[i])
            rows_out[:, i, :, key_cols] = key_rows.astype(jnp.bfloat16).reshape(shape)
            rows_out[:, i, :, value_cols] = value_sum[i].astype(jnp.bfloat16).reshape(shape)


def attend(pieces, normed, masked, gain, assignment, tiles, owners):
    seq_count, groups, stacked, head_dim = normed.shape
    img_count, own_rows, columns = pieces[0].shape[1:]
    parts = sum(piece.shape[0] for piece in pieces)
    img_rows = parts * own_rows
    shapes = [(piece.shape[0], img_count, own_rows, head_dim) for piece in pieces]
    keys = [pl.BlockSpec(shape, lambda g, b, *_: (0, 0, 0, g)) for shape in shapes]
    values = [pl.BlockSpec(shape, lambda g, b, *_: (0, 0, 0, groups + g)) for shape in shapes]
    stack = pl.BlockSpec((1, 1, stacked, head_dim), lambda g, b, *_: (b, g, 0, 0))
    rows = (parts, img_count, own_rows, columns)
    return pl.pallas_call(
        functools.partial(attend_kernel, len(pieces)),
        out_shape=(
            jax.ShapeDtypeStruct(rows, jnp.bfloat16),
            jax.ShapeDtypeStruct((seq_count, groups, stacked, img_rows), jnp.bfloat16),
            jax.ShapeDtypeStruct((seq_count, groups, img_rows, head_dim), jnp.bfloat16),
        ),
        grid_spec=pltpu.PrefetchScalarGridSpec(
            num_scalar_prefetch=3,
            grid=(groups, seq_count),
            in_specs=keys
            + values
            + [stack, stack, pl.BlockSpec((1, head_dim), lambda *_: (0, 0))],
            out_specs=(
                pl.BlockSpec(rows, lambda *_: (0, 0, 0, 0)),
                pl.BlockSpec((1, 1, stacked, img_rows), lambda g, b, *_: (b, g, 0, 0)),
                pl.BlockSpec((1, 1, img_rows, head_dim), lambda g, b, *_: (b, g, 0, 0)),
            ),
            scratch_shapes=[
                pltpu.VMEM((img_count, img_rows, head_dim), jnp.float32),
                pltpu.VMEM((img_count, img_rows, head_dim), jnp.bfloat16),
                pltpu.VMEM((img_count, img_rows, head_dim), jnp.bfloat16),
                pltpu.VMEM((img_count, img_rows, head_dim), jnp.float32),
                pltpu.VMEM((img_count, img_rows, head_dim), jnp.float32),
            ],
        ),
        compiler_params=pltpu.CompilerParams(vmem_limit_bytes=32 * 1024 * 1024),
        name="attend",
    )(assignment, tiles, owners, *pieces, *pieces, normed, masked, gain)


def after_kernel(query, score_grad, keys, gain, target):
    text_len, columns = query.shape[1:]
    head_dim = gain.shape[1]
    inv_root = 1.0 / math.sqrt(head_dim)
    for j in range(columns // head_dim):
        head = pl.ds(j * head_dim, head_dim)
        source = query[0, :, head].astype(jnp.float32)
        part = dot(score_grad[0, 0, pl.ds(j * text_len, text_len), :], keys[0, 0], 1, 0)
        grad = rms_back(source, rms_scale(source), gain[...], part * inv_root)
        target[0, :, head] = grad.astype(jnp.bfloat16)


def after(queries, score_grad, keys, gain):
    seq_count, text_len, columns = queries.shape
    groups, stacked, img_rows = score_grad.shape[1:]
    head_dim = gain.shape[1]
    source = pl.BlockSpec((1, text_len, columns // groups), lambda b, g: (b, 0, g))
    return pl.pallas_call(
        after_kernel,
        out_shape=jax.ShapeDtypeStruct(queries.shape, jnp.bfloat16),
        grid=(seq_count, groups),
        in_specs=[
            source,
            pl.BlockSpec((1, 1, stacked, img_rows), lambda b, g: (b, g, 0, 0)),
            pl.BlockSpec((1, 1, img_rows, head_dim), lambda b, g: (b, g, 0, 0)),
            pl.BlockSpec((1, head_dim), lambda *_: (0, 0)),
        ],
        out_specs=source,
        name="after",
    )(queries, score_grad, keys, gain)


def beside_kernel(left, right, out):
    cut = left.shape[1]
    out[:, :cut] = left[...]
    out[:, cut:] = right[...]


def beside(left, right):
    rows, columns = left.shape
    return pl.pallas_call(
        beside_kernel,
        out_shape=jax.ShapeDtypeStruct((rows, 2 * columns), left.dtype),
        name="beside",
    )(left, right)


def terms_kernel(splits, rows, weight, *outs):
    parts, img_count, own_rows, cols = rows.shape
    term = dot(rows[...].reshape(-1, cols), weight[...], 1, 1).astype(jnp.bfloat16)
    term = term.reshape(parts, img_count, own_rows, -1)
    for (part, low, high), out in zip(splits, outs):
        out[...] = term[part, low:high]


def terms(rows, weight, splits, chunks):
    parts, img_count, own_rows, cols = rows.shape
    vis_width = weight.shape[0]
    width = vis_width // chunks
    counts = [high - low for _, low, high in splits]
    return pl.pallas_call(
        functools.partial(terms_kernel, splits),
        out_shape=[
            jax.ShapeDtypeStruct((count, own_rows, vis_width), jnp.bfloat16) for count in counts
        ],
        grid=(chunks,),
        in_specs=[
            pl.BlockSpec(rows.shape, lambda c: (0, 0, 0, 0)),
            pl.BlockSpec((width, cols), lambda c: (c, 0)),
        ],
        out_specs=[
            pl.BlockSpec((count, own_rows, width), lambda c: (0, 0, c)) for count in counts
        ],
        compiler_params=pltpu.CompilerParams(vmem_limit_bytes=32 * 1024 * 1024),
        name="terms",
    )(rows, weight)


def pair_sum(held, given):
    return held[0, 0].astype(jnp.float32) + given[0].astype(jnp.float32)


def merge_kernel(place, *refs):
    count = len(refs) // 3
    for held, given, out in zip(refs[:count], refs[count : 2 * count], refs[2 * count :]):
        out[...] = pair_sum(held, given).astype(out.dtype)


def finish_kernel(place, held, given, *refs):
    *sent, key_out, value_out = refs
    total = pair_sum(held, given)
    for piece in sent:
        total = total + piece[...].astype(jnp.float32)
    cut = key_out.shape[1]
    key_out[...] = total[:, :cut]
    value_out[...] = total[:, cut:]


def held_specs(own_width, cols, steps, r):
    rows = own_width // steps
    return (
        pl.BlockSpec(
            (1, 1, rows, cols),
            lambda i, place: (jnp.bitwise_xor(place[1], r), place[0], i, 0),
        ),
        pl.BlockSpec(
            (1, rows, cols), lambda i, place: (jnp.bitwise_xor(place[1], r), i, 0)
        ),
    )


def merge(held, given, place):
    pairs, _, own_width, cols = held.shape
    specs = [held_specs(own_width, cols, 2, r) for r in range(1, pairs)]
    return pl.pallas_call(
        merge_kernel,
        out_shape=[jax.ShapeDtypeStruct((own_width, cols), jnp.bfloat16)] * len(specs),
        grid_spec=pltpu.PrefetchScalarGridSpec(
            num_scalar_prefetch=1,
            grid=(2,),
            in_specs=[spec[0] for spec in specs] + [spec[1] for spec in specs],
            out_specs=[pl.BlockSpec((own_width // 2, cols), lambda i, _: (i, 0))] * len(specs),
        ),
        compiler_params=pltpu.CompilerParams(vmem_limit_bytes=32 * 1024 * 1024),
        name="merge",
    )(place, *[held] * len(specs), *[given] * len(specs))


def finish(held, given, sent, place):
    _, _, own_width, cols = held.shape
    rows = own_width // 2
    half = jax.ShapeDtypeStruct((own_width, cols // 2), jnp.float32)
    return pl.pallas_call(
        finish_kernel,
        out_shape=(half, half),
        grid_spec=pltpu.PrefetchScalarGridSpec(
            num_scalar_prefetch=1,
            grid=(2,),
            in_specs=[*held_specs(own_width, cols, 2, 0)]
            + [pl.BlockSpec((rows, cols), lambda i, _: (i, 0))] * len(sent),
            out_specs=[pl.BlockSpec((rows, cols // 2), lambda i, _: (i, 0))] * 2,
        ),
        compiler_params=pltpu.CompilerParams(vmem_limit_bytes=32 * 1024 * 1024),
        name="finish",
    )(place, held, given, *sent)


def per_device(
    dp_size,
    mp_size,
    queries,
    out_grad,
    images,
    key_weight,
    value_weight,
    query_gain,
    key_gain,
    assignment,
    tile_counts,
    lengths,
):
    img_count, own_rows, vis_width = images.shape
    head_dim = query_gain.shape[0]
    own_width, key_cols = key_weight.shape
    key_heads = key_cols // head_dim
    cols = 2 * key_cols
    pairs = dp_size // 2
    place = lax.axis_index("dp")
    pair, core = place // 2, place % 2
    line = lax.axis_index("mp")
    first = img_count // 2

    def ring(value, step):
        return lax.ppermute(value, "mp", [(i, (i + step) % mp_size) for i in range(mp_size)])

    def swap(value, mask):
        return lax.ppermute(value, "dp", [(i, i ^ mask) for i in range(dp_size)])

    from_left, from_right = ring(images, 1), ring(images, -1)
    query_gain, key_gain = query_gain[None, :], key_gain[None, :]
    normed, masked = before(queries, out_grad, query_gain, lengths, key_heads)

    own_weight = beside(key_weight, value_weight)
    leaving = (from_left[:first], from_right[first:])
    if pairs != 4:
        weight = lax.all_gather(own_weight, "dp", axis=0, tiled=True)
        opposite = (ring(leaving[0], 1), ring(leaving[1], -1))
    else:
        side, up, across = (swap(own_weight, 2 * r) for r in range(1, pairs))
        twice = jnp.stack((own_weight, side))
        weight = jnp.zeros((2 * pairs, own_width, cols), jnp.bfloat16)
        leaving, twice, up, across, normed, masked, weight = lax.optimization_barrier(
            (leaving, twice, up, across, normed, masked, weight)
        )
        opposite = (ring(leaving[0], 1), ring(leaving[1], -1))
        for r, pieces in ((0, twice), (2, up[None]), (3, across[None])):
            mates = swap(pieces, 1)
            for k in range(pieces.shape[0]):
                for source, half in ((pieces, core), (mates, 1 - core)):
                    weight = lax.dynamic_update_slice_in_dim(
                        weight, source[k : k + 1], 2 * (pair ^ (r + k)) + half, axis=0
                    )
        weight = weight.reshape(vis_width, cols)

    near = jnp.stack((images, from_left, from_right)).reshape(-1, vis_width)
    near_total = dot(near, weight, 1, 0)
    near_total, opposite = lax.optimization_barrier((near_total, opposite))
    near_total = near_total.reshape(3, img_count, own_rows, cols)
    far = jnp.concatenate(opposite).reshape(-1, vis_width)
    far_total = dot(far, weight, 1, 0).reshape(1, img_count, own_rows, cols)
    owners = (line + jnp.array((0, -1, 1, 2), jnp.int32)) % mp_size
    rows, score_grad, seq_keys = attend(
        [near_total, far_total], normed, masked, key_gain, assignment, tile_counts, owners
    )
    halves = ((0, 0, first), (0, first, img_count))
    leaving_right, leaving_left = terms(rows[3:], weight, halves, 4)
    wholes = tuple((part, 0, img_count) for part in range(3))
    own, to_left, to_right = terms(rows[:3], weight, wholes, 4)

    right_half, left_half = ring(leaving_right, 1), ring(leaving_left, -1)

    if pairs != 4:
        all_images = jnp.concatenate((near, far))
        weight_part = dot(all_images, rows.reshape(-1, cols), 0, 0)
        weight_grad = lax.psum_scatter(weight_part, "dp", scatter_dimension=0, tiled=True)
    else:
        held_rows, leaving_right, leaving_left = lax.optimization_barrier(
            (rows, leaving_right, leaving_left)
        )
        all_images = jnp.concatenate((near, far))
        weight_part = dot(all_images, held_rows.reshape(-1, cols), 0, 0)
        weight_part = weight_part.astype(jnp.bfloat16).reshape(pairs, 2, own_width, cols)
        given = swap(lax.dynamic_index_in_dim(weight_part, 1 - core, 1, keepdims=False), 1)
        where = jnp.stack((core, pair))
        sent = merge(weight_part, given, where)
        right_half, left_half, sent = lax.optimization_barrier((right_half, left_half, sent))

    def added(held, half):
        return (held.astype(jnp.float32) + half.astype(jnp.float32)).astype(jnp.bfloat16)

    to_right = jnp.concatenate((added(to_right[:first], right_half), to_right[first:]))
    to_left = jnp.concatenate((to_left[:first], added(to_left[first:], left_half)))
    to_right, to_left, score_grad = lax.optimization_barrier((to_right, to_left, score_grad))
    from_left, from_right = ring(to_right, 1), ring(to_left, -1)
    query_grad = after(queries, score_grad, seq_keys, query_gain)
    from_left, from_right, query_grad = lax.optimization_barrier(
        (from_left, from_right, query_grad)
    )
    image_grad = (
        own.astype(jnp.float32) + from_left.astype(jnp.float32) + from_right.astype(jnp.float32)
    ).astype(jnp.bfloat16)
    if pairs == 4:
        sent = [swap(piece, 2 * r) for r, piece in enumerate(sent, 1)]
        image_grad, sent = lax.optimization_barrier((image_grad, sent))
        return (query_grad, image_grad, *finish(weight_part, given, sent, where))
    return (query_grad, image_grad, weight_grad[:, :key_cols], weight_grad[:, key_cols:])


def solution(mesh):
    placed = (
        P("dp", None, "mp"),
        P("dp", None, "mp"),
        P("dp", "mp", None),
        P("dp", "mp"),
        P("dp", "mp"),
        P(),
        P(),
        P("dp"),
        P("dp"),
        P("dp"),
    )

    def body(*args):
        return per_device(mesh.shape["dp"], mesh.shape["mp"], *args)

    return jax.shard_map(
        body,
        mesh=mesh,
        in_specs=placed,
        out_specs=(P("dp", None, "mp"), P("dp", "mp", None), P("dp", "mp"), P("dp", "mp")),
        check_vma=False,
    )
```

```python
import functools
import math

import jax
import jax.numpy as jnp
from jax import lax
from jax.experimental import pallas as pl
from jax.experimental.pallas import tpu as pltpu
from jax.sharding import PartitionSpec as P

TILE_ROWS = 32


EPSILON = 1e-05


def rms_scale(source):
    return lax.rsqrt(jnp.mean(source * source, axis=-1, keepdims=True) + EPSILON)


def rms_back(source, factor, gain_vector, upstream):
    weighted = gain_vector * upstream
    return factor * weighted - source * (factor * factor * factor) * jnp.mean(
        source * weighted, axis=-1, keepdims=True
    )


def dot(left, right, left_dim, right_dim):
    return lax.dot_general(
        left,
        right,
        (((left_dim,), (right_dim,)), ((), ())),
        preferred_element_type=jnp.float32,
    )


def before_kernel(lengths, query, grad, gain, normed, masked):
    text_len, columns = query.shape[1:]
    head_dim = gain.shape[1]
    live = lax.broadcasted_iota(jnp.int32, (text_len, head_dim), 0) < lengths[pl.program_id(0)]
    for j in range(columns // head_dim):
        head = pl.ds(j * head_dim, head_dim)
        rows = pl.ds(j * text_len, text_len)
        source = query[0, :, head].astype(jnp.float32)
        normed[0, 0, rows, :] = (source * rms_scale(source) * gain[...]).astype(jnp.bfloat16)
        upstream = grad[0, :, head]
        masked[0, 0, rows, :] = jnp.where(live, upstream, jnp.zeros_like(upstream))


def before(queries, out_grad, gain, lengths, groups):
    seq_count, text_len, columns = queries.shape
    head_dim = gain.shape[1]
    span = columns // groups
    stacked = span // head_dim * text_len
    source = pl.BlockSpec((1, text_len, span), lambda b, g, *_: (b, 0, g))
    target = pl.BlockSpec((1, 1, stacked, head_dim), lambda b, g, *_: (b, g, 0, 0))
    shape = jax.ShapeDtypeStruct((seq_count, groups, stacked, head_dim), jnp.bfloat16)
    return pl.pallas_call(
        before_kernel,
        out_shape=(shape, shape),
        grid_spec=pltpu.PrefetchScalarGridSpec(
            num_scalar_prefetch=1,
            grid=(seq_count, groups),
            in_specs=[source, source, pl.BlockSpec((1, head_dim), lambda *_: (0, 0))],
            out_specs=(target, target),
        ),
        name="before",
    )(lengths, queries, out_grad, gain)


def attend_kernel(count, assignment, tiles, owners, *refs):
    key_parts, value_parts = refs[:count], refs[count : 2 * count]
    normed, masked, gain = refs[2 * count : 2 * count + 3]
    rows_out, score_out, picked = refs[2 * count + 3 : 2 * count + 6]
    key_pre, key_normed, values, key_sum, value_sum = refs[2 * count + 6 :]
    img_count, own_rows, head_dim = key_parts[0].shape[1:]
    parts = rows_out.shape[0]
    img_rows = parts * own_rows
    group, step = pl.program_id(0), pl.program_id(1)
    inv_root = 1.0 / math.sqrt(head_dim)

    @pl.when(step == 0)
    def _():
        for i in range(img_count):
            keys, upper = [
                jnp.concatenate(
                    [source[:, i].reshape(-1, head_dim) for source in sources], axis=0
                )
                for sources in (key_parts, value_parts)
            ]
            key_pre[i] = keys
            key_normed[i] = (keys * rms_scale(keys) * gain[...]).astype(jnp.bfloat16)
            values[i] = upper.astype(jnp.bfloat16)
        key_sum[...] = jnp.zeros_like(key_sum)
        value_sum[...] = jnp.zeros_like(value_sum)

    image = assignment[step]
    keys = key_normed[image]
    picked[0, 0] = keys
    column = lax.broadcasted_iota(jnp.int32, (1, img_rows), 1)
    place = jnp.zeros_like(column)
    for k in range(parts):
        inside = (column >= k * own_rows) & (column < (k + 1) * own_rows)
        place = jnp.where(inside, column + (owners[k] - k) * own_rows, place)
    live = (place < tiles[image] * TILE_ROWS).astype(jnp.float32)
    queries = normed[0, 0]
    upstream = masked[0, 0]
    raised = jnp.exp(dot(queries, keys, 1, 1) * inv_root) * live
    prob = raised * (1.0 / jnp.sum(raised, axis=-1, keepdims=True))
    prob_grad = dot(upstream, values[image], 1, 1)
    inner = jnp.sum(prob * prob_grad, axis=-1, keepdims=True)
    score_grad = (prob * (prob_grad - inner)).astype(jnp.bfloat16)
    score_out[0, 0] = score_grad
    value_sum[image] += dot(prob.astype(jnp.bfloat16), upstream, 0, 0)
    key_sum[image] += dot(score_grad, queries, 0, 0) * inv_root

    @pl.when(step == pl.num_programs(1) - 1)
    def _():
        shape = (parts, own_rows, head_dim)
        key_cols = pl.ds(pl.multiple_of(group * head_dim, head_dim), head_dim)
        value_cols = pl.ds(
            pl.multiple_of((pl.num_programs(0) + group) * head_dim, head_dim), head_dim
        )
        for i in range(img_count):
            source = key_pre[i]
            key_rows = rms_back(source, rms_scale(source), gain[...], key_sum[i])
            rows_out[:, i, :, key_cols] = key_rows.astype(jnp.bfloat16).reshape(shape)
            rows_out[:, i, :, value_cols] = value_sum[i].astype(jnp.bfloat16).reshape(shape)


def attend(pieces, normed, masked, gain, assignment, tiles, owners):
    seq_count, groups, stacked, head_dim = normed.shape
    img_count, own_rows, columns = pieces[0].shape[1:]
    parts = sum(piece.shape[0] for piece in pieces)
    img_rows = parts * own_rows
    shapes = [(piece.shape[0], img_count, own_rows, head_dim) for piece in pieces]
    keys = [pl.BlockSpec(shape, lambda g, b, *_: (0, 0, 0, g)) for shape in shapes]
    values = [pl.BlockSpec(shape, lambda g, b, *_: (0, 0, 0, groups + g)) for shape in shapes]
    stack = pl.BlockSpec((1, 1, stacked, head_dim), lambda g, b, *_: (b, g, 0, 0))
    rows = (parts, img_count, own_rows, columns)
    return pl.pallas_call(
        functools.partial(attend_kernel, len(pieces)),
        out_shape=(
            jax.ShapeDtypeStruct(rows, jnp.bfloat16),
            jax.ShapeDtypeStruct((seq_count, groups, stacked, img_rows), jnp.bfloat16),
            jax.ShapeDtypeStruct((seq_count, groups, img_rows, head_dim), jnp.bfloat16),
        ),
        grid_spec=pltpu.PrefetchScalarGridSpec(
            num_scalar_prefetch=3,
            grid=(groups, seq_count),
            in_specs=keys
            + values
            + [stack, stack, pl.BlockSpec((1, head_dim), lambda *_: (0, 0))],
            out_specs=(
                pl.BlockSpec(rows, lambda *_: (0, 0, 0, 0)),
                pl.BlockSpec((1, 1, stacked, img_rows), lambda g, b, *_: (b, g, 0, 0)),
                pl.BlockSpec((1, 1, img_rows, head_dim), lambda g, b, *_: (b, g, 0, 0)),
            ),
            scratch_shapes=[
                pltpu.VMEM((img_count, img_rows, head_dim), jnp.float32),
                pltpu.VMEM((img_count, img_rows, head_dim), jnp.bfloat16),
                pltpu.VMEM((img_count, img_rows, head_dim), jnp.bfloat16),
                pltpu.VMEM((img_count, img_rows, head_dim), jnp.float32),
                pltpu.VMEM((img_count, img_rows, head_dim), jnp.float32),
            ],
        ),
        compiler_params=pltpu.CompilerParams(vmem_limit_bytes=32 * 1024 * 1024),
        name="attend",
    )(assignment, tiles, owners, *pieces, *pieces, normed, masked, gain)


def after_kernel(query, score_grad, keys, gain, target):
    text_len, columns = query.shape[1:]
    head_dim = gain.shape[1]
    inv_root = 1.0 / math.sqrt(head_dim)
    for j in range(columns // head_dim):
        head = pl.ds(j * head_dim, head_dim)
        source = query[0, :, head].astype(jnp.float32)
        part = dot(score_grad[0, 0, pl.ds(j * text_len, text_len), :], keys[0, 0], 1, 0)
        grad = rms_back(source, rms_scale(source), gain[...], part * inv_root)
        target[0, :, head] = grad.astype(jnp.bfloat16)


def after(queries, score_grad, keys, gain):
    seq_count, text_len, columns = queries.shape
    groups, stacked, img_rows = score_grad.shape[1:]
    head_dim = gain.shape[1]
    source = pl.BlockSpec((1, text_len, columns // groups), lambda b, g: (b, 0, g))
    return pl.pallas_call(
        after_kernel,
        out_shape=jax.ShapeDtypeStruct(queries.shape, jnp.bfloat16),
        grid=(seq_count, groups),
        in_specs=[
            source,
            pl.BlockSpec((1, 1, stacked, img_rows), lambda b, g: (b, g, 0, 0)),
            pl.BlockSpec((1, 1, img_rows, head_dim), lambda b, g: (b, g, 0, 0)),
            pl.BlockSpec((1, head_dim), lambda *_: (0, 0)),
        ],
        out_specs=source,
        name="after",
    )(queries, score_grad, keys, gain)


def beside_kernel(left, right, out):
    cut = left.shape[1]
    out[:, :cut] = left[...]
    out[:, cut:] = right[...]


def beside(left, right):
    rows, columns = left.shape
    return pl.pallas_call(
        beside_kernel,
        out_shape=jax.ShapeDtypeStruct((rows, 2 * columns), left.dtype),
        name="beside",
    )(left, right)


def terms_kernel(splits, rows, weight, *outs):
    parts, img_count, own_rows, cols = rows.shape
    term = dot(rows[...].reshape(-1, cols), weight[...], 1, 1).astype(jnp.bfloat16)
    term = term.reshape(parts, img_count, own_rows, -1)
    for (part, low, high), out in zip(splits, outs):
        out[...] = term[part, low:high]


def terms(rows, weight, splits, chunks):
    parts, img_count, own_rows, cols = rows.shape
    vis_width = weight.shape[0]
    width = vis_width // chunks
    counts = [high - low for _, low, high in splits]
    return pl.pallas_call(
        functools.partial(terms_kernel, splits),
        out_shape=[
            jax.ShapeDtypeStruct((count, own_rows, vis_width), jnp.bfloat16) for count in counts
        ],
        grid=(chunks,),
        in_specs=[
            pl.BlockSpec(rows.shape, lambda c: (0, 0, 0, 0)),
            pl.BlockSpec((width, cols), lambda c: (c, 0)),
        ],
        out_specs=[
            pl.BlockSpec((count, own_rows, width), lambda c: (0, 0, c)) for count in counts
        ],
        compiler_params=pltpu.CompilerParams(vmem_limit_bytes=32 * 1024 * 1024),
        name="terms",
    )(rows, weight)


def merge_kernel(place, *refs):
    count = len(refs) // 3
    for held, given, out in zip(refs[:count], refs[count : 2 * count], refs[2 * count :]):
        total = held[0, 0].astype(jnp.float32) + given[0].astype(jnp.float32)
        out[...] = total.astype(out.dtype)


def finish_kernel(own, *refs):
    *sent, key_out, value_out = refs
    total = own[...]
    for piece in sent:
        total = total + piece[...].astype(jnp.float32)
    cut = key_out.shape[1]
    key_out[...] = total[:, :cut]
    value_out[...] = total[:, cut:]


def held_specs(own_width, cols, steps, r):
    rows = own_width // steps
    return (
        pl.BlockSpec(
            (1, 1, rows, cols),
            lambda i, place: (jnp.bitwise_xor(place[1], r), place[0], i, 0),
        ),
        pl.BlockSpec(
            (1, rows, cols), lambda i, place: (jnp.bitwise_xor(place[1], r), i, 0)
        ),
    )


def merge(held, given, place):
    pairs, _, own_width, cols = held.shape
    specs = [held_specs(own_width, cols, 2, r) for r in range(pairs)]
    kinds = [jnp.float32] + [jnp.bfloat16] * (pairs - 1)
    return pl.pallas_call(
        merge_kernel,
        out_shape=[jax.ShapeDtypeStruct((own_width, cols), kind) for kind in kinds],
        grid_spec=pltpu.PrefetchScalarGridSpec(
            num_scalar_prefetch=1,
            grid=(2,),
            in_specs=[spec[0] for spec in specs] + [spec[1] for spec in specs],
            out_specs=[pl.BlockSpec((own_width // 2, cols), lambda i, _: (i, 0))] * len(specs),
        ),
        compiler_params=pltpu.CompilerParams(vmem_limit_bytes=32 * 1024 * 1024),
        name="merge",
    )(place, *[held] * len(specs), *[given] * len(specs))


def finish(own, sent):
    own_width, cols = own.shape
    rows = own_width // 2
    half = jax.ShapeDtypeStruct((own_width, cols // 2), jnp.float32)
    return pl.pallas_call(
        finish_kernel,
        out_shape=(half, half),
        grid=(2,),
        in_specs=[pl.BlockSpec((rows, cols), lambda i: (i, 0))] * (1 + len(sent)),
        out_specs=[pl.BlockSpec((rows, cols // 2), lambda i: (i, 0))] * 2,
        compiler_params=pltpu.CompilerParams(vmem_limit_bytes=32 * 1024 * 1024),
        name="finish",
    )(own, *sent)


def per_device(
    dp_size,
    mp_size,
    queries,
    out_grad,
    images,
    key_weight,
    value_weight,
    query_gain,
    key_gain,
    assignment,
    tile_counts,
    lengths,
):
    img_count, own_rows, vis_width = images.shape
    head_dim = query_gain.shape[0]
    own_width, key_cols = key_weight.shape
    key_heads = key_cols // head_dim
    cols = 2 * key_cols
    pairs = dp_size // 2
    place = lax.axis_index("dp")
    pair, core = place // 2, place % 2
    line = lax.axis_index("mp")
    first = img_count // 2

    def ring(value, step):
        return lax.ppermute(value, "mp", [(i, (i + step) % mp_size) for i in range(mp_size)])

    def swap(value, mask):
        return lax.ppermute(value, "dp", [(i, i ^ mask) for i in range(dp_size)])

    from_left, from_right = ring(images, 1), ring(images, -1)
    query_gain, key_gain = query_gain[None, :], key_gain[None, :]
    normed, masked = before(queries, out_grad, query_gain, lengths, key_heads)

    own_weight = beside(key_weight, value_weight)
    leaving = (from_left[:first], from_right[first:])
    if pairs != 4:
        weight = lax.all_gather(own_weight, "dp", axis=0, tiled=True)
        opposite = (ring(leaving[0], 1), ring(leaving[1], -1))
    else:
        side, up, across = (swap(own_weight, 2 * r) for r in range(1, pairs))
        twice = jnp.stack((own_weight, side))
        weight = jnp.zeros((2 * pairs, own_width, cols), jnp.bfloat16)
        leaving, twice, up, across, normed, masked, weight = lax.optimization_barrier(
            (leaving, twice, up, across, normed, masked, weight)
        )
        opposite = (ring(leaving[0], 1), ring(leaving[1], -1))
        for r, pieces in ((0, twice), (2, up[None]), (3, across[None])):
            mates = swap(pieces, 1)
            for k in range(pieces.shape[0]):
                for source, half in ((pieces, core), (mates, 1 - core)):
                    weight = lax.dynamic_update_slice_in_dim(
                        weight, source[k : k + 1], 2 * (pair ^ (r + k)) + half, axis=0
                    )
        weight = weight.reshape(vis_width, cols)

    near = jnp.stack((images, from_left, from_right)).reshape(-1, vis_width)
    near_total = dot(near, weight, 1, 0)
    near_total, opposite = lax.optimization_barrier((near_total, opposite))
    near_total = near_total.reshape(3, img_count, own_rows, cols)
    far = jnp.concatenate(opposite).reshape(-1, vis_width)
    far_total = dot(far, weight, 1, 0).reshape(1, img_count, own_rows, cols)
    owners = (line + jnp.array((0, -1, 1, 2), jnp.int32)) % mp_size
    rows, score_grad, seq_keys = attend(
        [near_total, far_total], normed, masked, key_gain, assignment, tile_counts, owners
    )
    halves = ((0, 0, first), (0, first, img_count))
    leaving_right, leaving_left = terms(rows[3:], weight, halves, 4)
    wholes = tuple((part, 0, img_count) for part in range(3))
    own, to_left, to_right = terms(rows[:3], weight, wholes, 4)

    right_half, left_half = lax.optimization_barrier(
        (ring(leaving_right, 1), ring(leaving_left, -1))
    )

    def added(held, half):
        return (held.astype(jnp.float32) + half.astype(jnp.float32)).astype(jnp.bfloat16)

    to_right = jnp.concatenate((added(to_right[:first], right_half), to_right[first:]))
    to_left = jnp.concatenate((to_left[:first], added(to_left[first:], left_half)))
    to_right, to_left = lax.optimization_barrier((to_right, to_left))
    from_left, from_right = ring(to_right, 1), ring(to_left, -1)

    if pairs != 4:
        all_images = jnp.concatenate((near, far))
        weight_part = dot(all_images, rows.reshape(-1, cols), 0, 0)
        weight_grad = lax.psum_scatter(weight_part, "dp", scatter_dimension=0, tiled=True)
    else:
        all_images = jnp.concatenate((near, far))
        weight_part = dot(all_images, rows.reshape(-1, cols), 0, 0)
        weight_part = weight_part.astype(jnp.bfloat16).reshape(pairs, 2, own_width, cols)
        given = swap(lax.dynamic_index_in_dim(weight_part, 1 - core, 1, keepdims=False), 1)
        given, to_right, to_left, score_grad = lax.optimization_barrier(
            (given, to_right, to_left, score_grad)
        )
        own_sum, *sent = merge(weight_part, given, jnp.stack((core, pair)))
        sent = [swap(piece, 2 * r) for r, piece in enumerate(sent, 1)]
    query_grad = after(queries, score_grad, seq_keys, query_gain)
    from_left, from_right, query_grad = lax.optimization_barrier(
        (from_left, from_right, query_grad)
    )
    image_grad = (
        own.astype(jnp.float32) + from_left.astype(jnp.float32) + from_right.astype(jnp.float32)
    ).astype(jnp.bfloat16)
    if pairs == 4:
        image_grad, sent = lax.optimization_barrier((image_grad, sent))
        return (query_grad, image_grad, *finish(own_sum, sent))
    return (query_grad, image_grad, weight_grad[:, :key_cols], weight_grad[:, key_cols:])


def solution(mesh):
    placed = (
        P("dp", None, "mp"),
        P("dp", None, "mp"),
        P("dp", "mp", None),
        P("dp", "mp"),
        P("dp", "mp"),
        P(),
        P(),
        P("dp"),
        P("dp"),
        P("dp"),
    )

    def body(*args):
        return per_device(mesh.shape["dp"], mesh.shape["mp"], *args)

    return jax.shard_map(
        body,
        mesh=mesh,
        in_specs=placed,
        out_specs=(P("dp", None, "mp"), P("dp", "mp", None), P("dp", "mp"), P("dp", "mp")),
        check_vma=False,
    )
```

```python
import functools
import math

import jax
import jax.numpy as jnp
from jax import lax
from jax.experimental import pallas as pl
from jax.experimental.pallas import tpu as pltpu
from jax.sharding import PartitionSpec as P

TILE_ROWS = 32


EPSILON = 1e-05


def rms_scale(source):
    return lax.rsqrt(jnp.mean(source * source, axis=-1, keepdims=True) + EPSILON)


def rms_back(source, factor, gain_vector, upstream):
    weighted = gain_vector * upstream
    return factor * weighted - source * (factor * factor * factor) * jnp.mean(
        source * weighted, axis=-1, keepdims=True
    )


def dot(left, right, left_dim, right_dim):
    return lax.dot_general(
        left,
        right,
        (((left_dim,), (right_dim,)), ((), ())),
        preferred_element_type=jnp.float32,
    )


def before_kernel(lengths, query, grad, gain, normed, masked):
    text_len, columns = query.shape[1:]
    head_dim = gain.shape[1]
    live = lax.broadcasted_iota(jnp.int32, (text_len, head_dim), 0) < lengths[pl.program_id(0)]
    for j in range(columns // head_dim):
        head = pl.ds(j * head_dim, head_dim)
        rows = pl.ds(j * text_len, text_len)
        source = query[0, :, head].astype(jnp.float32)
        normed[0, 0, rows, :] = (source * rms_scale(source) * gain[...]).astype(jnp.bfloat16)
        upstream = grad[0, :, head]
        masked[0, 0, rows, :] = jnp.where(live, upstream, jnp.zeros_like(upstream))


def before(queries, out_grad, gain, lengths, groups):
    seq_count, text_len, columns = queries.shape
    head_dim = gain.shape[1]
    span = columns // groups
    stacked = span // head_dim * text_len
    source = pl.BlockSpec((1, text_len, span), lambda b, g, *_: (b, 0, g))
    target = pl.BlockSpec((1, 1, stacked, head_dim), lambda b, g, *_: (b, g, 0, 0))
    shape = jax.ShapeDtypeStruct((seq_count, groups, stacked, head_dim), jnp.bfloat16)
    return pl.pallas_call(
        before_kernel,
        out_shape=(shape, shape),
        grid_spec=pltpu.PrefetchScalarGridSpec(
            num_scalar_prefetch=1,
            grid=(seq_count, groups),
            in_specs=[source, source, pl.BlockSpec((1, head_dim), lambda *_: (0, 0))],
            out_specs=(target, target),
        ),
        name="before",
    )(lengths, queries, out_grad, gain)


def attend_kernel(count, assignment, tiles, owners, *refs):
    key_parts, value_parts = refs[:count], refs[count : 2 * count]
    normed, masked, gain = refs[2 * count : 2 * count + 3]
    rows_out, score_out, picked = refs[2 * count + 3 : 2 * count + 6]
    key_pre, key_normed, values, key_sum, value_sum = refs[2 * count + 6 :]
    img_count, own_rows, head_dim = key_parts[0].shape[1:]
    parts = rows_out.shape[0]
    img_rows = parts * own_rows
    group, step = pl.program_id(0), pl.program_id(1)
    inv_root = 1.0 / math.sqrt(head_dim)

    @pl.when(step == 0)
    def _():
        for i in range(img_count):
            keys, upper = [
                jnp.concatenate(
                    [source[:, i].reshape(-1, head_dim) for source in sources], axis=0
                )
                for sources in (key_parts, value_parts)
            ]
            key_pre[i] = keys
            key_normed[i] = (keys * rms_scale(keys) * gain[...]).astype(jnp.bfloat16)
            values[i] = upper.astype(jnp.bfloat16)
        key_sum[...] = jnp.zeros_like(key_sum)
        value_sum[...] = jnp.zeros_like(value_sum)

    image = assignment[step]
    keys = key_normed[image]
    picked[0, 0] = keys
    column = lax.broadcasted_iota(jnp.int32, (1, img_rows), 1)
    place = jnp.zeros_like(column)
    for k in range(parts):
        inside = (column >= k * own_rows) & (column < (k + 1) * own_rows)
        place = jnp.where(inside, column + (owners[k] - k) * own_rows, place)
    live = (place < tiles[image] * TILE_ROWS).astype(jnp.float32)
    queries = normed[0, 0]
    upstream = masked[0, 0]
    raised = jnp.exp(dot(queries, keys, 1, 1) * inv_root) * live
    prob = raised * (1.0 / jnp.sum(raised, axis=-1, keepdims=True))
    prob_grad = dot(upstream, values[image], 1, 1)
    inner = jnp.sum(prob * prob_grad, axis=-1, keepdims=True)
    score_grad = (prob * (prob_grad - inner)).astype(jnp.bfloat16)
    score_out[0, 0] = score_grad
    value_sum[image] += dot(prob.astype(jnp.bfloat16), upstream, 0, 0)
    key_sum[image] += dot(score_grad, queries, 0, 0) * inv_root

    @pl.when(step == pl.num_programs(1) - 1)
    def _():
        shape = (parts, own_rows, head_dim)
        key_cols = pl.ds(pl.multiple_of(group * head_dim, head_dim), head_dim)
        value_cols = pl.ds(
            pl.multiple_of((pl.num_programs(0) + group) * head_dim, head_dim), head_dim
        )
        for i in range(img_count):
            source = key_pre[i]
            key_rows = rms_back(source, rms_scale(source), gain[...], key_sum[i])
            rows_out[:, i, :, key_cols] = key_rows.astype(jnp.bfloat16).reshape(shape)
            rows_out[:, i, :, value_cols] = value_sum[i].astype(jnp.bfloat16).reshape(shape)


def attend(pieces, normed, masked, gain, assignment, tiles, owners):
    seq_count, groups, stacked, head_dim = normed.shape
    img_count, own_rows, columns = pieces[0].shape[1:]
    parts = sum(piece.shape[0] for piece in pieces)
    img_rows = parts * own_rows
    shapes = [(piece.shape[0], img_count, own_rows, head_dim) for piece in pieces]
    keys = [pl.BlockSpec(shape, lambda g, b, *_: (0, 0, 0, g)) for shape in shapes]
    values = [pl.BlockSpec(shape, lambda g, b, *_: (0, 0, 0, groups + g)) for shape in shapes]
    stack = pl.BlockSpec((1, 1, stacked, head_dim), lambda g, b, *_: (b, g, 0, 0))
    rows = (parts, img_count, own_rows, columns)
    return pl.pallas_call(
        functools.partial(attend_kernel, len(pieces)),
        out_shape=(
            jax.ShapeDtypeStruct(rows, jnp.bfloat16),
            jax.ShapeDtypeStruct((seq_count, groups, stacked, img_rows), jnp.bfloat16),
            jax.ShapeDtypeStruct((seq_count, groups, img_rows, head_dim), jnp.bfloat16),
        ),
        grid_spec=pltpu.PrefetchScalarGridSpec(
            num_scalar_prefetch=3,
            grid=(groups, seq_count),
            in_specs=keys
            + values
            + [stack, stack, pl.BlockSpec((1, head_dim), lambda *_: (0, 0))],
            out_specs=(
                pl.BlockSpec(rows, lambda *_: (0, 0, 0, 0)),
                pl.BlockSpec((1, 1, stacked, img_rows), lambda g, b, *_: (b, g, 0, 0)),
                pl.BlockSpec((1, 1, img_rows, head_dim), lambda g, b, *_: (b, g, 0, 0)),
            ),
            scratch_shapes=[
                pltpu.VMEM((img_count, img_rows, head_dim), jnp.float32),
                pltpu.VMEM((img_count, img_rows, head_dim), jnp.bfloat16),
                pltpu.VMEM((img_count, img_rows, head_dim), jnp.bfloat16),
                pltpu.VMEM((img_count, img_rows, head_dim), jnp.float32),
                pltpu.VMEM((img_count, img_rows, head_dim), jnp.float32),
            ],
        ),
        compiler_params=pltpu.CompilerParams(vmem_limit_bytes=16 * 1024 * 1024),
        name="attend",
    )(assignment, tiles, owners, *pieces, *pieces, normed, masked, gain)


def after_kernel(query, score_grad, keys, gain, target):
    text_len, columns = query.shape[1:]
    head_dim = gain.shape[1]
    inv_root = 1.0 / math.sqrt(head_dim)
    for j in range(columns // head_dim):
        head = pl.ds(j * head_dim, head_dim)
        source = query[0, :, head].astype(jnp.float32)
        part = dot(score_grad[0, 0, pl.ds(j * text_len, text_len), :], keys[0, 0], 1, 0)
        grad = rms_back(source, rms_scale(source), gain[...], part * inv_root)
        target[0, :, head] = grad.astype(jnp.bfloat16)


def after(queries, score_grad, keys, gain):
    seq_count, text_len, columns = queries.shape
    groups, stacked, img_rows = score_grad.shape[1:]
    head_dim = gain.shape[1]
    source = pl.BlockSpec((1, text_len, columns // groups), lambda b, g: (b, 0, g))
    return pl.pallas_call(
        after_kernel,
        out_shape=jax.ShapeDtypeStruct(queries.shape, jnp.bfloat16),
        grid=(seq_count, groups),
        in_specs=[
            source,
            pl.BlockSpec((1, 1, stacked, img_rows), lambda b, g: (b, g, 0, 0)),
            pl.BlockSpec((1, 1, img_rows, head_dim), lambda b, g: (b, g, 0, 0)),
            pl.BlockSpec((1, head_dim), lambda *_: (0, 0)),
        ],
        out_specs=source,
        name="after",
    )(queries, score_grad, keys, gain)


def beside_kernel(left, right, out):
    cut = left.shape[1]
    out[:, :cut] = left[...]
    out[:, cut:] = right[...]


def beside(left, right):
    rows, columns = left.shape
    return pl.pallas_call(
        beside_kernel,
        out_shape=jax.ShapeDtypeStruct((rows, 2 * columns), left.dtype),
        name="beside",
    )(left, right)


def terms_kernel(splits, rows, weight, *outs):
    parts, img_count, own_rows, cols = rows.shape
    term = dot(rows[...].reshape(-1, cols), weight[...], 1, 1).astype(jnp.bfloat16)
    term = term.reshape(parts, img_count, own_rows, -1)
    for (part, low, high), out in zip(splits, outs):
        out[...] = term[part, low:high]


def terms(rows, weight, splits, chunks):
    parts, img_count, own_rows, cols = rows.shape
    vis_width = weight.shape[0]
    width = vis_width // chunks
    counts = [high - low for _, low, high in splits]
    return pl.pallas_call(
        functools.partial(terms_kernel, splits),
        out_shape=[
            jax.ShapeDtypeStruct((count, own_rows, vis_width), jnp.bfloat16) for count in counts
        ],
        grid=(chunks,),
        in_specs=[
            pl.BlockSpec(rows.shape, lambda c: (0, 0, 0, 0)),
            pl.BlockSpec((width, cols), lambda c: (c, 0)),
        ],
        out_specs=[
            pl.BlockSpec((count, own_rows, width), lambda c: (0, 0, c)) for count in counts
        ],
        compiler_params=pltpu.CompilerParams(vmem_limit_bytes=16 * 1024 * 1024),
        name="terms",
    )(rows, weight)


def merge_kernel(place, *refs):
    count = len(refs) // 3
    for held, given, out in zip(refs[:count], refs[count : 2 * count], refs[2 * count :]):
        total = held[0, 0].astype(jnp.float32) + given[0].astype(jnp.float32)
        out[...] = total.astype(out.dtype)


def finish_kernel(own, *refs):
    *sent, key_out, value_out = refs
    total = own[...]
    for piece in sent:
        total = total + piece[...].astype(jnp.float32)
    cut = key_out.shape[1]
    key_out[...] = total[:, :cut]
    value_out[...] = total[:, cut:]


def held_specs(own_width, cols, steps, r):
    rows = own_width // steps
    return (
        pl.BlockSpec(
            (1, 1, rows, cols),
            lambda i, place: (jnp.bitwise_xor(place[1], r), place[0], i, 0),
        ),
        pl.BlockSpec(
            (1, rows, cols), lambda i, place: (jnp.bitwise_xor(place[1], r), i, 0)
        ),
    )


def merge(held, given, place):
    pairs, _, own_width, cols = held.shape
    specs = [held_specs(own_width, cols, 2, r) for r in range(pairs)]
    kinds = [jnp.float32] + [jnp.bfloat16] * (pairs - 1)
    return pl.pallas_call(
        merge_kernel,
        out_shape=[jax.ShapeDtypeStruct((own_width, cols), kind) for kind in kinds],
        grid_spec=pltpu.PrefetchScalarGridSpec(
            num_scalar_prefetch=1,
            grid=(2,),
            in_specs=[spec[0] for spec in specs] + [spec[1] for spec in specs],
            out_specs=[pl.BlockSpec((own_width // 2, cols), lambda i, _: (i, 0))] * len(specs),
        ),
        compiler_params=pltpu.CompilerParams(vmem_limit_bytes=16 * 1024 * 1024),
        name="merge",
    )(place, *[held] * len(specs), *[given] * len(specs))


def finish(own, sent):
    own_width, cols = own.shape
    rows = own_width // 2
    half = jax.ShapeDtypeStruct((own_width, cols // 2), jnp.float32)
    return pl.pallas_call(
        finish_kernel,
        out_shape=(half, half),
        grid=(2,),
        in_specs=[pl.BlockSpec((rows, cols), lambda i: (i, 0))] * (1 + len(sent)),
        out_specs=[pl.BlockSpec((rows, cols // 2), lambda i: (i, 0))] * 2,
        compiler_params=pltpu.CompilerParams(vmem_limit_bytes=16 * 1024 * 1024),
        name="finish",
    )(own, *sent)


def per_device(
    dp_size,
    mp_size,
    queries,
    out_grad,
    images,
    key_weight,
    value_weight,
    query_gain,
    key_gain,
    assignment,
    tile_counts,
    lengths,
):
    img_count, own_rows, vis_width = images.shape
    head_dim = query_gain.shape[0]
    own_width, key_cols = key_weight.shape
    key_heads = key_cols // head_dim
    cols = 2 * key_cols
    pairs = dp_size // 2
    place = lax.axis_index("dp")
    pair, core = place // 2, place % 2
    line = lax.axis_index("mp")
    first = img_count // 2

    def ring(value, step):
        return lax.ppermute(value, "mp", [(i, (i + step) % mp_size) for i in range(mp_size)])

    def swap(value, mask):
        return lax.ppermute(value, "dp", [(i, i ^ mask) for i in range(dp_size)])

    from_left, from_right = ring(images, 1), ring(images, -1)
    query_gain, key_gain = query_gain[None, :], key_gain[None, :]
    normed, masked = before(queries, out_grad, query_gain, lengths, key_heads)

    own_weight = beside(key_weight, value_weight)
    leaving = (from_left[:first], from_right[first:])
    if pairs != 4:
        weight = lax.all_gather(own_weight, "dp", axis=0, tiled=True)
        opposite = (ring(leaving[0], 1), ring(leaving[1], -1))
    else:
        side, up, across = (swap(own_weight, 2 * r) for r in range(1, pairs))
        weight = jnp.zeros((2 * pairs, own_width, cols), jnp.bfloat16)
        leaving, side, up, across, normed, masked = lax.optimization_barrier(
            (leaving, side, up, across, normed, masked)
        )
        opposite = (ring(leaving[0], 1), ring(leaving[1], -1))
        mates = [swap(piece, 1) for piece in (side, up, across)]
        own_weight, mates = lax.optimization_barrier((own_weight, mates))
        mates = [swap(own_weight, 1), *mates]
        for r, pieces in enumerate(zip((own_weight, side, up, across), mates)):
            for source, half in zip(pieces, (core, 1 - core)):
                weight = lax.dynamic_update_slice_in_dim(
                    weight, source[None], 2 * (pair ^ r) + half, axis=0
                )
        weight = weight.reshape(vis_width, cols)

    near = jnp.stack((images, from_left, from_right)).reshape(-1, vis_width)
    near_total = dot(near, weight, 1, 0)
    near_total, opposite = lax.optimization_barrier((near_total, opposite))
    near_total = near_total.reshape(3, img_count, own_rows, cols)
    far = jnp.concatenate(opposite).reshape(-1, vis_width)
    far_total = dot(far, weight, 1, 0).reshape(1, img_count, own_rows, cols)
    owners = (line + jnp.array((0, -1, 1, 2), jnp.int32)) % mp_size
    rows, score_grad, seq_keys = attend(
        [near_total, far_total], normed, masked, key_gain, assignment, tile_counts, owners
    )
    halves = ((0, 0, first), (0, first, img_count))
    leaving_right, leaving_left = terms(rows[3:], weight, halves, 4)
    wholes = tuple((part, 0, img_count) for part in range(3))
    own, to_left, to_right = terms(rows[:3], weight, wholes, 4)

    right_half, left_half = lax.optimization_barrier(
        (ring(leaving_right, 1), ring(leaving_left, -1))
    )

    def added(held, half):
        return (held.astype(jnp.float32) + half.astype(jnp.float32)).astype(jnp.bfloat16)

    to_right = jnp.concatenate((added(to_right[:first], right_half), to_right[first:]))
    to_left = jnp.concatenate((to_left[:first], added(to_left[first:], left_half)))
    to_right, to_left = lax.optimization_barrier((to_right, to_left))
    from_left, from_right = ring(to_right, 1), ring(to_left, -1)

    if pairs != 4:
        all_images = jnp.concatenate((near, far))
        weight_part = dot(all_images, rows.reshape(-1, cols), 0, 0)
        weight_grad = lax.psum_scatter(weight_part, "dp", scatter_dimension=0, tiled=True)
    else:
        all_images = jnp.concatenate((near, far))
        weight_part = dot(all_images, rows.reshape(-1, cols), 0, 0)
        weight_part = weight_part.astype(jnp.bfloat16).reshape(pairs, 2, own_width, cols)
        given = swap(lax.dynamic_index_in_dim(weight_part, 1 - core, 1, keepdims=False), 1)
        given, to_right, to_left, score_grad = lax.optimization_barrier(
            (given, to_right, to_left, score_grad)
        )
        own_sum, *sent = merge(weight_part, given, jnp.stack((core, pair)))
        sent = [swap(piece, 2 * r) for r, piece in enumerate(sent, 1)]
    query_grad = after(queries, score_grad, seq_keys, query_gain)
    from_left, from_right, query_grad = lax.optimization_barrier(
        (from_left, from_right, query_grad)
    )
    image_grad = (
        own.astype(jnp.float32) + from_left.astype(jnp.float32) + from_right.astype(jnp.float32)
    ).astype(jnp.bfloat16)
    if pairs == 4:
        image_grad, sent = lax.optimization_barrier((image_grad, sent))
        return (query_grad, image_grad, *finish(own_sum, sent))
    return (query_grad, image_grad, weight_grad[:, :key_cols], weight_grad[:, key_cols:])


def solution(mesh):
    placed = (
        P("dp", None, "mp"),
        P("dp", None, "mp"),
        P("dp", "mp", None),
        P("dp", "mp"),
        P("dp", "mp"),
        P(),
        P(),
        P("dp"),
        P("dp"),
        P("dp"),
    )

    def body(*args):
        return per_device(mesh.shape["dp"], mesh.shape["mp"], *args)

    return jax.shard_map(
        body,
        mesh=mesh,
        in_specs=placed,
        out_specs=(P("dp", None, "mp"), P("dp", "mp", None), P("dp", "mp"), P("dp", "mp")),
        check_vma=False,
    )
```

```python
import functools
import math

import jax
import jax.numpy as jnp
from jax import lax
from jax.experimental import pallas as pl
from jax.experimental.pallas import tpu as pltpu
from jax.sharding import PartitionSpec as P

TILE_ROWS = 32


EPSILON = 1e-05


def rms_scale(source):
    return lax.rsqrt(jnp.mean(source * source, axis=-1, keepdims=True) + EPSILON)


def rms_back(source, factor, gain_vector, upstream):
    weighted = gain_vector * upstream
    return factor * weighted - source * (factor * factor * factor) * jnp.mean(
        source * weighted, axis=-1, keepdims=True
    )


def dot(left, right, left_dim, right_dim):
    return lax.dot_general(
        left,
        right,
        (((left_dim,), (right_dim,)), ((), ())),
        preferred_element_type=jnp.float32,
    )


def before_kernel(lengths, query, grad, gain, normed, masked):
    text_len, columns = query.shape[1:]
    head_dim = gain.shape[1]
    live = lax.broadcasted_iota(jnp.int32, (text_len, head_dim), 0) < lengths[pl.program_id(0)]
    for j in range(columns // head_dim):
        head = pl.ds(j * head_dim, head_dim)
        rows = pl.ds(j * text_len, text_len)
        source = query[0, :, head].astype(jnp.float32)
        normed[0, 0, rows, :] = (source * rms_scale(source) * gain[...]).astype(jnp.bfloat16)
        upstream = grad[0, :, head]
        masked[0, 0, rows, :] = jnp.where(live, upstream, jnp.zeros_like(upstream))


def before(queries, out_grad, gain, lengths, groups):
    seq_count, text_len, columns = queries.shape
    head_dim = gain.shape[1]
    span = columns // groups
    stacked = span // head_dim * text_len
    source = pl.BlockSpec((1, text_len, span), lambda b, g, *_: (b, 0, g))
    target = pl.BlockSpec((1, 1, stacked, head_dim), lambda b, g, *_: (b, g, 0, 0))
    shape = jax.ShapeDtypeStruct((seq_count, groups, stacked, head_dim), jnp.bfloat16)
    return pl.pallas_call(
        before_kernel,
        out_shape=(shape, shape),
        grid_spec=pltpu.PrefetchScalarGridSpec(
            num_scalar_prefetch=1,
            grid=(seq_count, groups),
            in_specs=[source, source, pl.BlockSpec((1, head_dim), lambda *_: (0, 0))],
            out_specs=(target, target),
        ),
        name="before",
    )(lengths, queries, out_grad, gain)


def attend_kernel(count, assignment, tiles, owners, *refs):
    key_parts, value_parts = refs[:count], refs[count : 2 * count]
    normed, masked, gain = refs[2 * count : 2 * count + 3]
    rows_out, score_out, picked = refs[2 * count + 3 : 2 * count + 6]
    key_pre, key_normed, values, key_sum, value_sum = refs[2 * count + 6 :]
    img_count, own_rows, head_dim = key_parts[0].shape[1:]
    parts = rows_out.shape[0]
    img_rows = parts * own_rows
    group, step = pl.program_id(0), pl.program_id(1)
    inv_root = 1.0 / math.sqrt(head_dim)

    @pl.when(step == 0)
    def _():
        for i in range(img_count):
            keys, upper = [
                jnp.concatenate(
                    [source[:, i].reshape(-1, head_dim) for source in sources], axis=0
                )
                for sources in (key_parts, value_parts)
            ]
            key_pre[i] = keys
            key_normed[i] = (keys * rms_scale(keys) * gain[...]).astype(jnp.bfloat16)
            values[i] = upper.astype(jnp.bfloat16)
        key_sum[...] = jnp.zeros_like(key_sum)
        value_sum[...] = jnp.zeros_like(value_sum)

    image = assignment[step]
    keys = key_normed[image]
    picked[0, 0] = keys
    column = lax.broadcasted_iota(jnp.int32, (1, img_rows), 1)
    place = jnp.zeros_like(column)
    for k in range(parts):
        inside = (column >= k * own_rows) & (column < (k + 1) * own_rows)
        place = jnp.where(inside, column + (owners[k] - k) * own_rows, place)
    live = (place < tiles[image] * TILE_ROWS).astype(jnp.float32)
    queries = normed[0, 0]
    upstream = masked[0, 0]
    raised = jnp.exp(dot(queries, keys, 1, 1) * inv_root) * live
    prob = raised * (1.0 / jnp.sum(raised, axis=-1, keepdims=True))
    prob_grad = dot(upstream, values[image], 1, 1)
    inner = jnp.sum(prob * prob_grad, axis=-1, keepdims=True)
    score_grad = (prob * (prob_grad - inner)).astype(jnp.bfloat16)
    score_out[0, 0] = score_grad
    value_sum[image] += dot(prob.astype(jnp.bfloat16), upstream, 0, 0)
    key_sum[image] += dot(score_grad, queries, 0, 0) * inv_root

    @pl.when(step == pl.num_programs(1) - 1)
    def _():
        shape = (parts, own_rows, head_dim)
        key_cols = pl.ds(pl.multiple_of(group * head_dim, head_dim), head_dim)
        value_cols = pl.ds(
            pl.multiple_of((pl.num_programs(0) + group) * head_dim, head_dim), head_dim
        )
        for i in range(img_count):
            source = key_pre[i]
            key_rows = rms_back(source, rms_scale(source), gain[...], key_sum[i])
            rows_out[:, i, :, key_cols] = key_rows.astype(jnp.bfloat16).reshape(shape)
            rows_out[:, i, :, value_cols] = value_sum[i].astype(jnp.bfloat16).reshape(shape)


def attend(pieces, normed, masked, gain, assignment, tiles, owners):
    seq_count, groups, stacked, head_dim = normed.shape
    img_count, own_rows, columns = pieces[0].shape[1:]
    parts = sum(piece.shape[0] for piece in pieces)
    img_rows = parts * own_rows
    shapes = [(piece.shape[0], img_count, own_rows, head_dim) for piece in pieces]
    keys = [pl.BlockSpec(shape, lambda g, b, *_: (0, 0, 0, g)) for shape in shapes]
    values = [pl.BlockSpec(shape, lambda g, b, *_: (0, 0, 0, groups + g)) for shape in shapes]
    stack = pl.BlockSpec((1, 1, stacked, head_dim), lambda g, b, *_: (b, g, 0, 0))
    rows = (parts, img_count, own_rows, columns)
    return pl.pallas_call(
        functools.partial(attend_kernel, len(pieces)),
        out_shape=(
            jax.ShapeDtypeStruct(rows, jnp.bfloat16),
            jax.ShapeDtypeStruct((seq_count, groups, stacked, img_rows), jnp.bfloat16),
            jax.ShapeDtypeStruct((seq_count, groups, img_rows, head_dim), jnp.bfloat16),
        ),
        grid_spec=pltpu.PrefetchScalarGridSpec(
            num_scalar_prefetch=3,
            grid=(groups, seq_count),
            in_specs=keys
            + values
            + [stack, stack, pl.BlockSpec((1, head_dim), lambda *_: (0, 0))],
            out_specs=(
                pl.BlockSpec(rows, lambda *_: (0, 0, 0, 0)),
                pl.BlockSpec((1, 1, stacked, img_rows), lambda g, b, *_: (b, g, 0, 0)),
                pl.BlockSpec((1, 1, img_rows, head_dim), lambda g, b, *_: (b, g, 0, 0)),
            ),
            scratch_shapes=[
                pltpu.VMEM((img_count, img_rows, head_dim), jnp.float32),
                pltpu.VMEM((img_count, img_rows, head_dim), jnp.bfloat16),
                pltpu.VMEM((img_count, img_rows, head_dim), jnp.bfloat16),
                pltpu.VMEM((img_count, img_rows, head_dim), jnp.float32),
                pltpu.VMEM((img_count, img_rows, head_dim), jnp.float32),
            ],
        ),
        compiler_params=pltpu.CompilerParams(vmem_limit_bytes=16 * 1024 * 1024),
        name="attend",
    )(assignment, tiles, owners, *pieces, *pieces, normed, masked, gain)


def after_kernel(query, score_grad, keys, gain, target):
    text_len, columns = query.shape[1:]
    head_dim = gain.shape[1]
    inv_root = 1.0 / math.sqrt(head_dim)
    for j in range(columns // head_dim):
        head = pl.ds(j * head_dim, head_dim)
        source = query[0, :, head].astype(jnp.float32)
        part = dot(score_grad[0, 0, pl.ds(j * text_len, text_len), :], keys[0, 0], 1, 0)
        grad = rms_back(source, rms_scale(source), gain[...], part * inv_root)
        target[0, :, head] = grad.astype(jnp.bfloat16)


def after(queries, score_grad, keys, gain):
    seq_count, text_len, columns = queries.shape
    groups, stacked, img_rows = score_grad.shape[1:]
    head_dim = gain.shape[1]
    source = pl.BlockSpec((1, text_len, columns // groups), lambda b, g: (b, 0, g))
    return pl.pallas_call(
        after_kernel,
        out_shape=jax.ShapeDtypeStruct(queries.shape, jnp.bfloat16),
        grid=(seq_count, groups),
        in_specs=[
            source,
            pl.BlockSpec((1, 1, stacked, img_rows), lambda b, g: (b, g, 0, 0)),
            pl.BlockSpec((1, 1, img_rows, head_dim), lambda b, g: (b, g, 0, 0)),
            pl.BlockSpec((1, head_dim), lambda *_: (0, 0)),
        ],
        out_specs=source,
        name="after",
    )(queries, score_grad, keys, gain)


def beside_kernel(left, right, out):
    cut = left.shape[1]
    out[:, :cut] = left[...]
    out[:, cut:] = right[...]


def beside(left, right):
    rows, columns = left.shape
    return pl.pallas_call(
        beside_kernel,
        out_shape=jax.ShapeDtypeStruct((rows, 2 * columns), left.dtype),
        grid=(2,),
        in_specs=[pl.BlockSpec((rows // 2, columns), lambda i: (i, 0))] * 2,
        out_specs=pl.BlockSpec((rows // 2, 2 * columns), lambda i: (i, 0)),
        name="beside",
    )(left, right)


def terms_kernel(splits, rows, weight, *outs):
    parts, img_count, own_rows, cols = rows.shape
    term = dot(rows[...].reshape(-1, cols), weight[...], 1, 1).astype(jnp.bfloat16)
    term = term.reshape(parts, img_count, own_rows, -1)
    for (part, low, high), out in zip(splits, outs):
        out[...] = term[part, low:high]


def terms(rows, weight, splits, chunks):
    parts, img_count, own_rows, cols = rows.shape
    vis_width = weight.shape[0]
    width = vis_width // chunks
    counts = [high - low for _, low, high in splits]
    return pl.pallas_call(
        functools.partial(terms_kernel, splits),
        out_shape=[
            jax.ShapeDtypeStruct((count, own_rows, vis_width), jnp.bfloat16) for count in counts
        ],
        grid=(chunks,),
        in_specs=[
            pl.BlockSpec(rows.shape, lambda c: (0, 0, 0, 0)),
            pl.BlockSpec((width, cols), lambda c: (c, 0)),
        ],
        out_specs=[
            pl.BlockSpec((count, own_rows, width), lambda c: (0, 0, c)) for count in counts
        ],
        compiler_params=pltpu.CompilerParams(vmem_limit_bytes=16 * 1024 * 1024),
        name="terms",
    )(rows, weight)


def total_kernel(own, left, right, out):
    total = own[...].astype(jnp.float32) + left[...].astype(jnp.float32)
    out[...] = (total + right[...].astype(jnp.float32)).astype(out.dtype)


def total_of(own, left, right):
    images, own_rows, vis_width = own.shape
    spec = pl.BlockSpec((images, own_rows, vis_width // 4), lambda i: (0, 0, i))
    return pl.pallas_call(
        total_kernel,
        out_shape=jax.ShapeDtypeStruct(own.shape, own.dtype),
        grid=(4,),
        in_specs=[spec] * 3,
        out_specs=spec,
        cost_estimate=pl.CostEstimate(
            flops=2 * own.size, transcendentals=0, bytes_accessed=8 * own.size
        ),
        name="total",
    )(own, left, right)


def merge_kernel(place, *refs):
    count = len(refs) // 3
    for held, given, out in zip(refs[:count], refs[count : 2 * count], refs[2 * count :]):
        total = held[0, 0].astype(jnp.float32) + given[0].astype(jnp.float32)
        out[...] = total.astype(out.dtype)


def finish_kernel(own, *refs):
    *sent, key_out, value_out = refs
    total = own[...]
    for piece in sent:
        total = total + piece[...].astype(jnp.float32)
    cut = key_out.shape[1]
    key_out[...] = total[:, :cut]
    value_out[...] = total[:, cut:]


def held_specs(own_width, cols, steps, r):
    rows = own_width // steps
    return (
        pl.BlockSpec(
            (1, 1, rows, cols),
            lambda i, place: (jnp.bitwise_xor(place[1], r), place[0], i, 0),
        ),
        pl.BlockSpec(
            (1, rows, cols), lambda i, place: (jnp.bitwise_xor(place[1], r), i, 0)
        ),
    )


def merge(held, given, place):
    pairs, _, own_width, cols = held.shape
    specs = [held_specs(own_width, cols, 2, r) for r in range(pairs)]
    kinds = [jnp.float32] + [jnp.bfloat16] * (pairs - 1)
    return pl.pallas_call(
        merge_kernel,
        out_shape=[jax.ShapeDtypeStruct((own_width, cols), kind) for kind in kinds],
        grid_spec=pltpu.PrefetchScalarGridSpec(
            num_scalar_prefetch=1,
            grid=(2,),
            in_specs=[spec[0] for spec in specs] + [spec[1] for spec in specs],
            out_specs=[pl.BlockSpec((own_width // 2, cols), lambda i, _: (i, 0))] * len(specs),
        ),
        compiler_params=pltpu.CompilerParams(vmem_limit_bytes=16 * 1024 * 1024),
        name="merge",
    )(place, *[held] * len(specs), *[given] * len(specs))


def finish(own, sent):
    own_width, cols = own.shape
    rows = own_width // 2
    half = jax.ShapeDtypeStruct((own_width, cols // 2), jnp.float32)
    return pl.pallas_call(
        finish_kernel,
        out_shape=(half, half),
        grid=(2,),
        in_specs=[pl.BlockSpec((rows, cols), lambda i: (i, 0))] * (1 + len(sent)),
        out_specs=[pl.BlockSpec((rows, cols // 2), lambda i: (i, 0))] * 2,
        compiler_params=pltpu.CompilerParams(vmem_limit_bytes=16 * 1024 * 1024),
        name="finish",
    )(own, *sent)


def per_device(
    dp_size,
    mp_size,
    queries,
    out_grad,
    images,
    key_weight,
    value_weight,
    query_gain,
    key_gain,
    assignment,
    tile_counts,
    lengths,
):
    img_count, own_rows, vis_width = images.shape
    head_dim = query_gain.shape[0]
    own_width, key_cols = key_weight.shape
    key_heads = key_cols // head_dim
    cols = 2 * key_cols
    pairs = dp_size // 2
    place = lax.axis_index("dp")
    pair, core = place // 2, place % 2
    line = lax.axis_index("mp")
    first = img_count // 2

    def ring(value, step):
        return lax.ppermute(value, "mp", [(i, (i + step) % mp_size) for i in range(mp_size)])

    def swap(value, mask):
        return lax.ppermute(value, "dp", [(i, i ^ mask) for i in range(dp_size)])

    from_left, from_right = ring(images, 1), ring(images, -1)
    query_gain, key_gain = query_gain[None, :], key_gain[None, :]
    normed, masked = before(queries, out_grad, query_gain, lengths, key_heads)

    if pairs != 4:
        own_weight = jnp.concatenate((key_weight, value_weight), axis=1)
    else:
        own_weight = beside(key_weight, value_weight)
    leaving = (from_left[:first], from_right[first:])
    if pairs != 4:
        weight = lax.all_gather(own_weight, "dp", axis=0, tiled=True)
        opposite = (ring(leaving[0], 1), ring(leaving[1], -1))
    else:
        side, up, across = (swap(own_weight, 2 * r) for r in range(1, pairs))
        weight = jnp.zeros((2 * pairs, own_width, cols), jnp.bfloat16)
        leaving, side, up, across, normed, masked = lax.optimization_barrier(
            (leaving, side, up, across, normed, masked)
        )
        opposite = (ring(leaving[0], 1), ring(leaving[1], -1))
        mates = [swap(piece, 1) for piece in (side, up, across)]
        own_weight, mates = lax.optimization_barrier((own_weight, mates))
        mates = [swap(own_weight, 1), *mates]
        for r, pieces in enumerate(zip((own_weight, side, up, across), mates)):
            for source, half in zip(pieces, (core, 1 - core)):
                weight = lax.dynamic_update_slice_in_dim(
                    weight, source[None], 2 * (pair ^ r) + half, axis=0
                )
        weight = weight.reshape(vis_width, cols)

    near = jnp.stack((images, from_left, from_right)).reshape(-1, vis_width)
    near_total = dot(near, weight, 1, 0)
    near_total, opposite = lax.optimization_barrier((near_total, opposite))
    near_total = near_total.reshape(3, img_count, own_rows, cols)
    far = jnp.concatenate(opposite).reshape(-1, vis_width)
    far_total = dot(far, weight, 1, 0).reshape(1, img_count, own_rows, cols)
    owners = (line + jnp.array((0, -1, 1, 2), jnp.int32)) % mp_size
    rows, score_grad, seq_keys = attend(
        [near_total, far_total], normed, masked, key_gain, assignment, tile_counts, owners
    )
    halves = ((0, 0, first), (0, first, img_count))
    leaving_right, leaving_left = terms(rows[3:], weight, halves, 4)
    wholes = tuple((part, 0, img_count) for part in range(3))
    own, to_left, to_right = terms(rows[:3], weight, wholes, 4)

    right_half, left_half = lax.optimization_barrier(
        (ring(leaving_right, 1), ring(leaving_left, -1))
    )

    def added(held, half):
        return (held.astype(jnp.float32) + half.astype(jnp.float32)).astype(jnp.bfloat16)

    to_right = jnp.concatenate((added(to_right[:first], right_half), to_right[first:]))
    to_left = jnp.concatenate((to_left[:first], added(to_left[first:], left_half)))
    to_right, to_left = lax.optimization_barrier((to_right, to_left))
    from_left, from_right = ring(to_right, 1), ring(to_left, -1)

    if pairs != 4:
        all_images = jnp.concatenate((near, far))
        weight_part = dot(all_images, rows.reshape(-1, cols), 0, 0)
        weight_grad = lax.psum_scatter(weight_part, "dp", scatter_dimension=0, tiled=True)
    else:
        all_images = jnp.concatenate((near, far))
        weight_part = dot(all_images, rows.reshape(-1, cols), 0, 0)
        weight_part = weight_part.astype(jnp.bfloat16).reshape(pairs, 2, own_width, cols)
        given = swap(lax.dynamic_index_in_dim(weight_part, 1 - core, 1, keepdims=False), 1)
        given, to_right, to_left, score_grad = lax.optimization_barrier(
            (given, to_right, to_left, score_grad)
        )
        own_sum, *sent = merge(weight_part, given, jnp.stack((core, pair)))
        sent = [swap(piece, 2 * r) for r, piece in enumerate(sent, 1)]
    query_grad = after(queries, score_grad, seq_keys, query_gain)
    from_left, from_right, query_grad = lax.optimization_barrier(
        (from_left, from_right, query_grad)
    )
    image_grad = total_of(own, from_left, from_right)
    if pairs == 4:
        image_grad, sent = lax.optimization_barrier((image_grad, sent))
        return (query_grad, image_grad, *finish(own_sum, sent))
    return (query_grad, image_grad, weight_grad[:, :key_cols], weight_grad[:, key_cols:])


def solution(mesh):
    placed = (
        P("dp", None, "mp"),
        P("dp", None, "mp"),
        P("dp", "mp", None),
        P("dp", "mp"),
        P("dp", "mp"),
        P(),
        P(),
        P("dp"),
        P("dp"),
        P("dp"),
    )

    def body(*args):
        return per_device(mesh.shape["dp"], mesh.shape["mp"], *args)

    return jax.shard_map(
        body,
        mesh=mesh,
        in_specs=placed,
        out_specs=(P("dp", None, "mp"), P("dp", "mp", None), P("dp", "mp"), P("dp", "mp")),
        check_vma=False,
    )
```

```python
import functools
import math

import jax
import jax.numpy as jnp
from jax import lax
from jax.experimental import pallas as pl
from jax.experimental.pallas import tpu as pltpu
from jax.sharding import PartitionSpec as P

TILE_ROWS = 32


EPSILON = 1e-05


def rms_scale(source):
    return lax.rsqrt(jnp.mean(source * source, axis=-1, keepdims=True) + EPSILON)


def rms_back(source, factor, gain_vector, upstream):
    weighted = gain_vector * upstream
    return factor * weighted - source * (factor * factor * factor) * jnp.mean(
        source * weighted, axis=-1, keepdims=True
    )


def dot(left, right, left_dim, right_dim):
    return lax.dot_general(
        left,
        right,
        (((left_dim,), (right_dim,)), ((), ())),
        preferred_element_type=jnp.float32,
    )


def before_kernel(lengths, query, grad, gain, normed, masked):
    text_len, columns = query.shape[1:]
    head_dim = gain.shape[1]
    live = lax.broadcasted_iota(jnp.int32, (text_len, head_dim), 0) < lengths[pl.program_id(0)]
    for j in range(columns // head_dim):
        head = pl.ds(j * head_dim, head_dim)
        rows = pl.ds(j * text_len, text_len)
        source = query[0, :, head].astype(jnp.float32)
        normed[0, 0, rows, :] = (source * rms_scale(source) * gain[...]).astype(jnp.bfloat16)
        upstream = grad[0, :, head]
        masked[0, 0, rows, :] = jnp.where(live, upstream, jnp.zeros_like(upstream))


def before(queries, out_grad, gain, lengths, groups):
    seq_count, text_len, columns = queries.shape
    head_dim = gain.shape[1]
    span = columns // groups
    stacked = span // head_dim * text_len
    source = pl.BlockSpec((1, text_len, span), lambda b, g, *_: (b, 0, g))
    target = pl.BlockSpec((1, 1, stacked, head_dim), lambda b, g, *_: (b, g, 0, 0))
    shape = jax.ShapeDtypeStruct((seq_count, groups, stacked, head_dim), jnp.bfloat16)
    return pl.pallas_call(
        before_kernel,
        out_shape=(shape, shape),
        grid_spec=pltpu.PrefetchScalarGridSpec(
            num_scalar_prefetch=1,
            grid=(seq_count, groups),
            in_specs=[source, source, pl.BlockSpec((1, head_dim), lambda *_: (0, 0))],
            out_specs=(target, target),
        ),
        name="before",
    )(lengths, queries, out_grad, gain)


def attend_kernel(count, assignment, tiles, owners, *refs):
    key_parts, value_parts = refs[:count], refs[count : 2 * count]
    normed, masked, gain = refs[2 * count : 2 * count + 3]
    rows_out, score_out, picked = refs[2 * count + 3 : 2 * count + 6]
    key_pre, key_normed, values, key_sum, value_sum = refs[2 * count + 6 :]
    img_count, own_rows, head_dim = key_parts[0].shape[1:]
    parts = rows_out.shape[0]
    img_rows = parts * own_rows
    group, step = pl.program_id(0), pl.program_id(1)
    inv_root = 1.0 / math.sqrt(head_dim)

    @pl.when(step == 0)
    def _():
        for i in range(img_count):
            keys, upper = [
                jnp.concatenate(
                    [source[:, i].reshape(-1, head_dim) for source in sources], axis=0
                )
                for sources in (key_parts, value_parts)
            ]
            key_pre[i] = keys
            key_normed[i] = (keys * rms_scale(keys) * gain[...]).astype(jnp.bfloat16)
            values[i] = upper.astype(jnp.bfloat16)
        key_sum[...] = jnp.zeros_like(key_sum)
        value_sum[...] = jnp.zeros_like(value_sum)

    image = assignment[step]
    keys = key_normed[image]
    picked[0, 0] = keys
    column = lax.broadcasted_iota(jnp.int32, (1, img_rows), 1)
    place = jnp.zeros_like(column)
    for k in range(parts):
        inside = (column >= k * own_rows) & (column < (k + 1) * own_rows)
        place = jnp.where(inside, column + (owners[k] - k) * own_rows, place)
    live = (place < tiles[image] * TILE_ROWS).astype(jnp.float32)
    queries = normed[0, 0]
    upstream = masked[0, 0]
    raised = jnp.exp(dot(queries, keys, 1, 1) * inv_root) * live
    prob = raised * (1.0 / jnp.sum(raised, axis=-1, keepdims=True))
    prob_grad = dot(upstream, values[image], 1, 1)
    inner = jnp.sum(prob * prob_grad, axis=-1, keepdims=True)
    score_grad = (prob * (prob_grad - inner)).astype(jnp.bfloat16)
    score_out[0, 0] = score_grad
    value_sum[image] += dot(prob.astype(jnp.bfloat16), upstream, 0, 0)
    key_sum[image] += dot(score_grad, queries, 0, 0) * inv_root

    @pl.when(step == pl.num_programs(1) - 1)
    def _():
        shape = (parts, own_rows, head_dim)
        key_cols = pl.ds(pl.multiple_of(group * head_dim, head_dim), head_dim)
        value_cols = pl.ds(
            pl.multiple_of((pl.num_programs(0) + group) * head_dim, head_dim), head_dim
        )
        for i in range(img_count):
            source = key_pre[i]
            key_rows = rms_back(source, rms_scale(source), gain[...], key_sum[i])
            rows_out[:, i, :, key_cols] = key_rows.astype(jnp.bfloat16).reshape(shape)
            rows_out[:, i, :, value_cols] = value_sum[i].astype(jnp.bfloat16).reshape(shape)


def attend(pieces, normed, masked, gain, assignment, tiles, owners):
    seq_count, groups, stacked, head_dim = normed.shape
    img_count, own_rows, columns = pieces[0].shape[1:]
    parts = sum(piece.shape[0] for piece in pieces)
    img_rows = parts * own_rows
    shapes = [(piece.shape[0], img_count, own_rows, head_dim) for piece in pieces]
    keys = [pl.BlockSpec(shape, lambda g, b, *_: (0, 0, 0, g)) for shape in shapes]
    values = [pl.BlockSpec(shape, lambda g, b, *_: (0, 0, 0, groups + g)) for shape in shapes]
    stack = pl.BlockSpec((1, 1, stacked, head_dim), lambda g, b, *_: (b, g, 0, 0))
    rows = (parts, img_count, own_rows, columns)
    return pl.pallas_call(
        functools.partial(attend_kernel, len(pieces)),
        out_shape=(
            jax.ShapeDtypeStruct(rows, jnp.bfloat16),
            jax.ShapeDtypeStruct((seq_count, groups, stacked, img_rows), jnp.bfloat16),
            jax.ShapeDtypeStruct((seq_count, groups, img_rows, head_dim), jnp.bfloat16),
        ),
        grid_spec=pltpu.PrefetchScalarGridSpec(
            num_scalar_prefetch=3,
            grid=(groups, seq_count),
            in_specs=keys
            + values
            + [stack, stack, pl.BlockSpec((1, head_dim), lambda *_: (0, 0))],
            out_specs=(
                pl.BlockSpec(rows, lambda *_: (0, 0, 0, 0)),
                pl.BlockSpec((1, 1, stacked, img_rows), lambda g, b, *_: (b, g, 0, 0)),
                pl.BlockSpec((1, 1, img_rows, head_dim), lambda g, b, *_: (b, g, 0, 0)),
            ),
            scratch_shapes=[
                pltpu.VMEM((img_count, img_rows, head_dim), jnp.float32),
                pltpu.VMEM((img_count, img_rows, head_dim), jnp.bfloat16),
                pltpu.VMEM((img_count, img_rows, head_dim), jnp.bfloat16),
                pltpu.VMEM((img_count, img_rows, head_dim), jnp.float32),
                pltpu.VMEM((img_count, img_rows, head_dim), jnp.float32),
            ],
        ),
        compiler_params=pltpu.CompilerParams(vmem_limit_bytes=32 * 1024 * 1024),
        name="attend",
    )(assignment, tiles, owners, *pieces, *pieces, normed, masked, gain)


def after_kernel(query, score_grad, keys, gain, target):
    text_len, columns = query.shape[1:]
    head_dim = gain.shape[1]
    inv_root = 1.0 / math.sqrt(head_dim)
    for j in range(columns // head_dim):
        head = pl.ds(j * head_dim, head_dim)
        source = query[0, :, head].astype(jnp.float32)
        part = dot(score_grad[0, 0, pl.ds(j * text_len, text_len), :], keys[0, 0], 1, 0)
        grad = rms_back(source, rms_scale(source), gain[...], part * inv_root)
        target[0, :, head] = grad.astype(jnp.bfloat16)


def after(queries, score_grad, keys, gain):
    seq_count, text_len, columns = queries.shape
    groups, stacked, img_rows = score_grad.shape[1:]
    head_dim = gain.shape[1]
    source = pl.BlockSpec((1, text_len, columns // groups), lambda b, g: (b, 0, g))
    return pl.pallas_call(
        after_kernel,
        out_shape=jax.ShapeDtypeStruct(queries.shape, jnp.bfloat16),
        grid=(seq_count, groups),
        in_specs=[
            source,
            pl.BlockSpec((1, 1, stacked, img_rows), lambda b, g: (b, g, 0, 0)),
            pl.BlockSpec((1, 1, img_rows, head_dim), lambda b, g: (b, g, 0, 0)),
            pl.BlockSpec((1, head_dim), lambda *_: (0, 0)),
        ],
        out_specs=source,
        name="after",
    )(queries, score_grad, keys, gain)


def beside_kernel(left, right, out):
    cut = left.shape[1]
    out[:, :cut] = left[...]
    out[:, cut:] = right[...]


def beside(left, right):
    rows, columns = left.shape
    return pl.pallas_call(
        beside_kernel,
        out_shape=jax.ShapeDtypeStruct((rows, 2 * columns), left.dtype),
        name="beside",
    )(left, right)


def terms_kernel(splits, rows, weight, *outs):
    parts, img_count, own_rows, cols = rows.shape
    term = dot(rows[...].reshape(-1, cols), weight[...], 1, 1).astype(jnp.bfloat16)
    term = term.reshape(parts, img_count, own_rows, -1)
    for (part, low, high), out in zip(splits, outs):
        out[...] = term[part, low:high]


def terms(rows, weight, splits, chunks):
    parts, img_count, own_rows, cols = rows.shape
    vis_width = weight.shape[0]
    width = vis_width // chunks
    counts = [high - low for _, low, high in splits]
    return pl.pallas_call(
        functools.partial(terms_kernel, splits),
        out_shape=[
            jax.ShapeDtypeStruct((count, own_rows, vis_width), jnp.bfloat16) for count in counts
        ],
        grid=(chunks,),
        in_specs=[
            pl.BlockSpec(rows.shape, lambda c: (0, 0, 0, 0)),
            pl.BlockSpec((width, cols), lambda c: (c, 0)),
        ],
        out_specs=[
            pl.BlockSpec((count, own_rows, width), lambda c: (0, 0, c)) for count in counts
        ],
        compiler_params=pltpu.CompilerParams(vmem_limit_bytes=32 * 1024 * 1024),
        name="terms",
    )(rows, weight)


def merge_kernel(place, *refs):
    count = len(refs) // 3
    for held, given, out in zip(refs[:count], refs[count : 2 * count], refs[2 * count :]):
        total = held[0, 0].astype(jnp.float32) + given[0].astype(jnp.float32)
        out[...] = total.astype(out.dtype)


def finish_kernel(own, *refs):
    *sent, key_out, value_out = refs
    total = own[...]
    for piece in sent:
        total = total + piece[...].astype(jnp.float32)
    cut = key_out.shape[1]
    key_out[...] = total[:, :cut]
    value_out[...] = total[:, cut:]


def held_specs(own_width, cols, steps, r):
    rows = own_width // steps
    return (
        pl.BlockSpec(
            (1, 1, rows, cols),
            lambda i, place: (jnp.bitwise_xor(place[1], r), place[0], i, 0),
        ),
        pl.BlockSpec(
            (1, rows, cols), lambda i, place: (jnp.bitwise_xor(place[1], r), i, 0)
        ),
    )


def merge(held, given, place, others, kind):
    own_width, cols = held.shape[2:]
    specs = [held_specs(own_width, cols, 2, r) for r in others]
    kinds = [kind] * len(specs)
    return pl.pallas_call(
        merge_kernel,
        out_shape=[jax.ShapeDtypeStruct((own_width, cols), kind) for kind in kinds],
        grid_spec=pltpu.PrefetchScalarGridSpec(
            num_scalar_prefetch=1,
            grid=(2,),
            in_specs=[spec[0] for spec in specs] + [spec[1] for spec in specs],
            out_specs=[pl.BlockSpec((own_width // 2, cols), lambda i, _: (i, 0))] * len(specs),
        ),
        compiler_params=pltpu.CompilerParams(vmem_limit_bytes=32 * 1024 * 1024),
        name="merge",
    )(place, *[held] * len(specs), *[given] * len(specs))


def finish(own, sent):
    own_width, cols = own.shape
    rows = own_width // 2
    half = jax.ShapeDtypeStruct((own_width, cols // 2), jnp.float32)
    return pl.pallas_call(
        finish_kernel,
        out_shape=(half, half),
        grid=(2,),
        in_specs=[pl.BlockSpec((rows, cols), lambda i: (i, 0))] * (1 + len(sent)),
        out_specs=[pl.BlockSpec((rows, cols // 2), lambda i: (i, 0))] * 2,
        compiler_params=pltpu.CompilerParams(vmem_limit_bytes=32 * 1024 * 1024),
        name="finish",
    )(own, *sent)


def per_device(
    dp_size,
    mp_size,
    queries,
    out_grad,
    images,
    key_weight,
    value_weight,
    query_gain,
    key_gain,
    assignment,
    tile_counts,
    lengths,
):
    img_count, own_rows, vis_width = images.shape
    head_dim = query_gain.shape[0]
    own_width, key_cols = key_weight.shape
    key_heads = key_cols // head_dim
    cols = 2 * key_cols
    pairs = dp_size // 2
    place = lax.axis_index("dp")
    pair, core = place // 2, place % 2
    line = lax.axis_index("mp")
    first = img_count // 2

    def ring(value, step):
        return lax.ppermute(value, "mp", [(i, (i + step) % mp_size) for i in range(mp_size)])

    def swap(value, mask):
        return lax.ppermute(value, "dp", [(i, i ^ mask) for i in range(dp_size)])

    from_left, from_right = ring(images, 1), ring(images, -1)
    query_gain, key_gain = query_gain[None, :], key_gain[None, :]
    normed, masked = before(queries, out_grad, query_gain, lengths, key_heads)

    own_weight = beside(key_weight, value_weight)
    leaving = (from_left[:first], from_right[first:])
    if pairs != 4:
        weight = lax.all_gather(own_weight, "dp", axis=0, tiled=True)
        opposite = (ring(leaving[0], 1), ring(leaving[1], -1))
    else:
        side, up, across = (swap(own_weight, 2 * r) for r in range(1, pairs))
        twice = jnp.stack((own_weight, side))
        weight = jnp.zeros((2 * pairs, own_width, cols), jnp.bfloat16)
        leaving, twice, up, across, normed, masked, weight = lax.optimization_barrier(
            (leaving, twice, up, across, normed, masked, weight)
        )
        opposite = (ring(leaving[0], 1), ring(leaving[1], -1))
        for r, pieces in ((0, twice), (2, up[None]), (3, across[None])):
            mates = swap(pieces, 1)
            for k in range(pieces.shape[0]):
                for source, half in ((pieces, core), (mates, 1 - core)):
                    weight = lax.dynamic_update_slice_in_dim(
                        weight, source[k : k + 1], 2 * (pair ^ (r + k)) + half, axis=0
                    )
        weight = weight.reshape(vis_width, cols)

    near = jnp.stack((images, from_left, from_right)).reshape(-1, vis_width)
    near_total = dot(near, weight, 1, 0)
    near_total, opposite = lax.optimization_barrier((near_total, opposite))
    near_total = near_total.reshape(3, img_count, own_rows, cols)
    far = jnp.concatenate(opposite).reshape(-1, vis_width)
    far_total = dot(far, weight, 1, 0).reshape(1, img_count, own_rows, cols)
    owners = (line + jnp.array((0, -1, 1, 2), jnp.int32)) % mp_size
    rows, score_grad, seq_keys = attend(
        [near_total, far_total], normed, masked, key_gain, assignment, tile_counts, owners
    )
    halves = ((0, 0, first), (0, first, img_count))
    leaving_right, leaving_left = terms(rows[3:], weight, halves, 2)
    wholes = tuple((part, 0, img_count) for part in range(3))
    own, to_left, to_right = terms(rows[:3], weight, wholes, 4)

    right_half, left_half = lax.optimization_barrier(
        (ring(leaving_right, 1), ring(leaving_left, -1))
    )

    def added(held, half):
        return (held.astype(jnp.float32) + half.astype(jnp.float32)).astype(jnp.bfloat16)

    to_right = jnp.concatenate((added(to_right[:first], right_half), to_right[first:]))
    to_left = jnp.concatenate((to_left[:first], added(to_left[first:], left_half)))
    to_right, to_left = lax.optimization_barrier((to_right, to_left))
    from_left, from_right = ring(to_right, 1), ring(to_left, -1)

    if pairs != 4:
        all_images = jnp.concatenate((near, far))
        weight_part = dot(all_images, rows.reshape(-1, cols), 0, 0)
        weight_grad = lax.psum_scatter(weight_part, "dp", scatter_dimension=0, tiled=True)
    else:
        all_images = jnp.concatenate((near, far))
        weight_part = dot(all_images, rows.reshape(-1, cols), 0, 0)
        weight_part = weight_part.astype(jnp.bfloat16).reshape(pairs, 2, own_width, cols)
        given = swap(lax.dynamic_index_in_dim(weight_part, 1 - core, 1, keepdims=False), 1)
        given, to_right, to_left, score_grad = lax.optimization_barrier(
            (given, to_right, to_left, score_grad)
        )
        where = jnp.stack((core, pair))
        sent = merge(weight_part, given, where, range(1, pairs), jnp.bfloat16)
        given, score_grad, sent = lax.optimization_barrier((given, score_grad, sent))
        (own_sum,) = merge(weight_part, given, where, (0,), jnp.float32)
        sent = [swap(piece, 2 * r) for r, piece in enumerate(sent, 1)]
    query_grad = after(queries, score_grad, seq_keys, query_gain)
    from_left, from_right, query_grad = lax.optimization_barrier(
        (from_left, from_right, query_grad)
    )
    image_grad = (
        own.astype(jnp.float32) + from_left.astype(jnp.float32) + from_right.astype(jnp.float32)
    ).astype(jnp.bfloat16)
    if pairs == 4:
        image_grad, sent = lax.optimization_barrier((image_grad, sent))
        return (query_grad, image_grad, *finish(own_sum, sent))
    return (query_grad, image_grad, weight_grad[:, :key_cols], weight_grad[:, key_cols:])


def solution(mesh):
    placed = (
        P("dp", None, "mp"),
        P("dp", None, "mp"),
        P("dp", "mp", None),
        P("dp", "mp"),
        P("dp", "mp"),
        P(),
        P(),
        P("dp"),
        P("dp"),
        P("dp"),
    )

    def body(*args):
        return per_device(mesh.shape["dp"], mesh.shape["mp"], *args)

    return jax.shard_map(
        body,
        mesh=mesh,
        in_specs=placed,
        out_specs=(P("dp", None, "mp"), P("dp", "mp", None), P("dp", "mp"), P("dp", "mp")),
        check_vma=False,
    )
```
